32 devices in a mesh: tm: 4 (over z), lat: 2 (over x), lon: 4 (over y, core).
Axes of the slice: x: 2, y: 2, z: 4, core: 2. Of those that a mesh axis runs over, the one named last changes fastest.
Arguments:
- tokens: bfloat16 [16, 8, 32, 768], P('tm', 'lat', 'lon'), may hold values from -40 to 40
- key_count: int32 [4, 2, 8], P('tm', 'lat', 'lon'), may hold values from 1 to 64
- norm_gain: float32 [768], replicated, may hold values from 0.1 to 1.9
- qkv_weight: bfloat16 [3, 768, 384], replicated, may hold values from -0.21875 to 0.21875
- out_weight: bfloat16 [384, 768], replicated, may hold values from -0.3125 to 0.3125
- logit_scale: float32 [6], replicated, may hold values from 1 to 3
- grad_out: bfloat16 [16, 8, 32, 768], P('tm', 'lat', 'lon'), may hold values from -12 to 12
Outputs:
- grad_tokens: bfloat16 [16, 8, 32, 768], P('tm', 'lat', 'lon')
The draws below stay inside these ranges and needn't reach their ends.
All inputs are finite; a program needn't handle non-finite values.
Results may differ from the reference program's by a relative error of at most 0.012.
The reference program's roundings to bfloat16 on the way count: a program that leaves them out, or rounds other values in their place, can miss the bound.
Values may be sent and summed in bfloat16 or wider, within the bound.
No kernel may reach another device: no remote copies, remote signals or barrier semaphores. Data moves between devices by JAX's collectives and lax.ppermute only.
A program may use at most 128 MiB of HBM per device.

```python
import math
import jax
import jax.numpy as jnp
from jax import lax

D = 768
HEADS = 6
HEAD_DIM = 64
BLOCK = 4
NT = 16
NH = 8
NW = 32


def draw_tokens(key, part):
    key_mine = jax.random.fold_in(key, 11)
    key_base = jax.random.fold_in(key_mine, 0)
    grid_shape = (NT, NH, NW, D)
    normal = jax.random.truncated_normal(key_base, -6.0, 6.0, grid_shape, jnp.float32)
    return normal.astype(jnp.bfloat16)


def draw_grad_out(key, part):
    key_mine = jax.random.fold_in(key, 23)
    key_base = jax.random.fold_in(key_mine, 0)
    grid_shape = (NT, NH, NW, D)
    normal = jax.random.truncated_normal(key_base, -6.0, 6.0, grid_shape, jnp.float32)
    return normal.astype(jnp.bfloat16)


def plant(array, stream_key, low, top_value):
    spot = [jax.random.randint(jax.random.fold_in(stream_key, axis), (), 0, length) for axis, length in enumerate(array.shape)]
    main_axis = array.shape.index(max(array.shape))
    neighbour = spot[:main_axis] + [(spot[main_axis] + 1) % array.shape[main_axis]] + spot[main_axis + 1:]
    return array.at[tuple(spot)].set(low).at[tuple(neighbour)].set(top_value)


def normal_values(rng, shape, width, reach, held_as=jnp.bfloat16):
    values = jax.random.normal(rng, shape, jnp.float32) * width
    return jnp.minimum(jnp.maximum(values, -reach), reach).astype(held_as)


def setup_inputs(seed: int = 0) -> dict:
    streams_of = jax.random.split(jax.random.key(seed), 8)
    tokens = draw_tokens(jax.random.fold_in(streams_of[7], 71), 0)
    key_count = plant(jax.random.randint(streams_of[1], (NT // BLOCK, NH // BLOCK, NW // BLOCK), 1, BLOCK**3 + 1), jax.random.fold_in(streams_of[1], 1), 1, BLOCK**3).astype(jnp.int32)
    norm_gain = jnp.clip(1.0 + 0.18 * jax.random.normal(streams_of[2], (D,), jnp.float32), 0.1, 1.9)
    qkv_weight = normal_values(streams_of[3], (3, D, HEADS * HEAD_DIM), D ** -0.5, 0.21875)
    out_weight = normal_values(streams_of[4], (HEADS * HEAD_DIM, D), (HEADS * HEAD_DIM) ** -0.5, 0.3125)
    logit_scale = jnp.clip(jnp.exp(jax.random.uniform(streams_of[5], (HEADS,), jnp.float32, math.log(1.0), math.log(3.0))), 1.0, 3.0)
    grad_out = draw_grad_out(jax.random.fold_in(streams_of[7], 71), 0)
    return dict(tokens=tokens, key_count=key_count, norm_gain=norm_gain, qkv_weight=qkv_weight, out_weight=out_weight, logit_scale=logit_scale, grad_out=grad_out)


EPS = 1e-06

def unit_rows(values):
    inverse = lax.rsqrt(lax.optimization_barrier(jnp.mean(values * values, -1, keepdims=True)) + EPS)
    return (values * inverse, inverse)

def unit_rows_back(values, inverse, grad_in):
    inner_mean = lax.optimization_barrier(jnp.mean(values * grad_in, -1, keepdims=True))
    return inverse * grad_in - inverse * inverse * inverse * values * inner_mean

def to_blocks(layout):
    shape_in = layout.shape
    trailing = shape_in[3:]
    split_up = layout.reshape((shape_in[0] // BLOCK, BLOCK, shape_in[1] // BLOCK, BLOCK, shape_in[2] // BLOCK, BLOCK) + trailing)
    axes_order = (0, 2, 4, 1, 3, 5) + tuple(range(6, 6 + len(trailing)))
    return split_up.transpose(axes_order).reshape((shape_in[0] // BLOCK, shape_in[1] // BLOCK, shape_in[2] // BLOCK, BLOCK * BLOCK * BLOCK) + trailing)

def from_blocks(blocked):
    shape_in = blocked.shape
    trailing = shape_in[4:]
    split_up = blocked.reshape(shape_in[:3] + (BLOCK, BLOCK, BLOCK) + trailing)
    axes_order = (0, 3, 1, 4, 2, 5) + tuple(range(6, 6 + len(trailing)))
    return split_up.transpose(axes_order).reshape((shape_in[0] * BLOCK, shape_in[1] * BLOCK, shape_in[2] * BLOCK) + trailing)

def gather_neighbours(blocked):
    inner_dims = (blocked.shape[0] - 2, blocked.shape[1] - 2, blocked.shape[2] - 2)
    pieces = []
    for frame_off in range(3):
        for row_off in range(3):
            for col_off in range(3):
                pieces.append(blocked[frame_off:frame_off + inner_dims[0], row_off:row_off + inner_dims[1], col_off:col_off + inner_dims[2]])
    stacked = jnp.stack(pieces, 3)
    return stacked.reshape((inner_dims[0] * inner_dims[1] * inner_dims[2], 27 * stacked.shape[4]) + stacked.shape[5:])

def spread_neighbours(nearby, inner_dims):
    trailing = nearby.shape[2:]
    block_cells = BLOCK * BLOCK * BLOCK
    blocked = nearby.reshape(inner_dims + (27, block_cells) + trailing)
    padded = jnp.zeros((inner_dims[0] + 2, inner_dims[1] + 2, inner_dims[2] + 2, block_cells) + trailing, nearby.dtype)
    offset_id = 0
    for frame_off in range(3):
        for row_off in range(3):
            for col_off in range(3):
                padded = padded.at[frame_off:frame_off + inner_dims[0], row_off:row_off + inner_dims[1], col_off:col_off + inner_dims[2]].add(blocked[:, :, :, offset_id])
                offset_id = offset_id + 1
    return padded

def query_side(query_blocks, keys_near, values_near, live_near, grad_blocks, scale_rows):
    scores = jnp.einsum('nqhe,nkhe->nhqk', query_blocks.astype(jnp.float32), keys_near.astype(jnp.float32)) * scale_rows[:, None, None]
    masked = jnp.exp(scores) * live_near[:, None, None, :]
    totals = lax.optimization_barrier(jnp.sum(masked, -1))
    prob_full = masked / totals[..., None]
    prob_half = prob_full.astype(jnp.bfloat16)
    attended = jnp.einsum('nhqk,nkhe->nqhe', prob_half.astype(jnp.float32), values_near.astype(jnp.float32))
    inner_grad = lax.optimization_barrier(jnp.sum(grad_blocks.astype(jnp.float32) * attended, -1))
    grad_prob = jnp.einsum('nqhe,nkhe->nhqk', grad_blocks.astype(jnp.float32), values_near.astype(jnp.float32))
    grad_score = (prob_full * (grad_prob - jnp.swapaxes(inner_grad, 1, 2)[..., None]) * scale_rows[:, None, None]).astype(jnp.bfloat16)
    grad_query = jnp.einsum('nhqk,nkhe->nqhe', grad_score.astype(jnp.float32), keys_near.astype(jnp.float32))
    return (prob_half, grad_score, grad_query, totals, inner_grad)

def pad_grid(layout):
    widths = [(BLOCK, BLOCK), (BLOCK, BLOCK), (0, 0)] + [(0, 0)] * (layout.ndim - 3)
    padded = jnp.pad(layout, widths)
    return jnp.concatenate([padded[:, :, -BLOCK:], padded, padded[:, :, :BLOCK]], 2)

def reference(tokens, key_count, norm_gain, qkv_weight, out_weight, logit_scale, grad_out):
    head_width = HEADS * HEAD_DIM
    grid_shape = (NT, NH, NW)
    heads_shape = grid_shape + (HEADS, HEAD_DIM)
    block_cells = BLOCK * BLOCK * BLOCK
    near_count = 27 * block_cells
    slab_grid = (1, NH // BLOCK, NW // BLOCK)
    slab_total = slab_grid[1] * slab_grid[2]
    scale_rows = logit_scale * (1.0 / math.sqrt(HEAD_DIM))
    token_values = tokens.astype(jnp.float32)
    normed_unit, row_inverse = unit_rows(token_values)
    normed = (normed_unit * norm_gain).astype(jnp.bfloat16)
    flat_normed = normed.reshape(NT * NH * NW, D)
    query_raw = jnp.dot(flat_normed, qkv_weight[0], preferred_element_type=jnp.float32).reshape(heads_shape)
    key_raw = jnp.dot(flat_normed, qkv_weight[1], preferred_element_type=jnp.float32).reshape(heads_shape)
    value_raw = jnp.dot(flat_normed, qkv_weight[2], preferred_element_type=jnp.float32)
    query_unit, query_inverse = unit_rows(query_raw)
    key_unit, key_inverse = unit_rows(key_raw)
    queries = query_unit.astype(jnp.bfloat16).reshape(grid_shape + (head_width,))
    keys_all = key_unit.astype(jnp.bfloat16).reshape(grid_shape + (head_width,))
    values_all = value_raw.astype(jnp.bfloat16).reshape(grid_shape + (head_width,))
    grad_attended = jnp.dot(grad_out.reshape(NT * NH * NW, D), out_weight.T, preferred_element_type=jnp.float32).astype(jnp.bfloat16).reshape(grid_shape + (head_width,))
    count_cells = jnp.repeat(jnp.repeat(jnp.repeat(key_count, BLOCK, 0), BLOCK, 1), BLOCK, 2)
    frame_pos = jnp.arange(NT, dtype=jnp.int32) % BLOCK
    row_pos = jnp.arange(NH, dtype=jnp.int32) % BLOCK
    col_pos = jnp.arange(NW, dtype=jnp.int32) % BLOCK
    position = (frame_pos[:, None, None] * BLOCK + row_pos[None, :, None]) * BLOCK + col_pos[None, None, :]
    live_all = (position < count_cells).astype(jnp.float32)
    kv_padded = pad_grid(jnp.stack([keys_all, values_all], 3))
    live_padded = pad_grid(live_all)

    def one_slab(pair_total, slab_id):
        start_row = (slab_id * BLOCK).astype(jnp.int32)
        kv_slab = lax.dynamic_slice_in_dim(kv_padded, start_row, 3 * BLOCK, 0)
        live_slab = lax.dynamic_slice_in_dim(live_padded, start_row, 3 * BLOCK, 0)
        query_slab = lax.dynamic_slice_in_dim(queries, start_row, BLOCK, 0)
        grad_slab = lax.dynamic_slice_in_dim(grad_attended, start_row, BLOCK, 0)
        kv_near = gather_neighbours(to_blocks(kv_slab))
        keys_near = kv_near[:, :, 0].reshape(slab_total, near_count, HEADS, HEAD_DIM)
        values_near = kv_near[:, :, 1].reshape(slab_total, near_count, HEADS, HEAD_DIM)
        live_near = gather_neighbours(to_blocks(live_slab))
        query_blocks = to_blocks(query_slab).reshape(slab_total, block_cells, HEADS, HEAD_DIM)
        grad_blocks = to_blocks(grad_slab).reshape(slab_total, block_cells, HEADS, HEAD_DIM)
        prob_half, grad_score, grad_query, totals, inner_grad = query_side(query_blocks, keys_near, values_near, live_near, grad_blocks, scale_rows)
        key_grad_near = jnp.einsum('nhqk,nqhe->nkhe', grad_score.astype(jnp.float32), query_blocks.astype(jnp.float32))
        value_grad_near = jnp.einsum('nhqk,nqhe->nkhe', prob_half.astype(jnp.float32), grad_blocks.astype(jnp.float32))
        pair_near = jnp.stack([key_grad_near.reshape(slab_total, near_count, head_width), value_grad_near.reshape(slab_total, near_count, head_width)], 2)
        pair_slab = from_blocks(spread_neighbours(pair_near, slab_grid))
        current = lax.dynamic_slice_in_dim(pair_total, start_row, 3 * BLOCK, 0)
        pair_total = lax.dynamic_update_slice_in_dim(pair_total, current + pair_slab, start_row, 0)
        query_grad = from_blocks(grad_query.reshape(slab_grid + (block_cells, head_width)))
        return (pair_total, query_grad)
    pair_init = jnp.zeros((NT + 2 * BLOCK, NH + 2 * BLOCK, NW + 2 * BLOCK, 2, head_width), jnp.float32)
    pair_padded, query_grads = lax.scan(one_slab, pair_init, jnp.arange(NT // BLOCK, dtype=jnp.int32))
    query_grad_all = query_grads.reshape(grid_shape + (head_width,))
    own_part = pair_padded[BLOCK:-BLOCK, BLOCK:-BLOCK]
    pair_grad = own_part[:, :, BLOCK:-BLOCK]
    pair_grad = pair_grad.at[:, :, :BLOCK].add(own_part[:, :, -BLOCK:])
    pair_grad = pair_grad.at[:, :, -BLOCK:].add(own_part[:, :, :BLOCK])
    key_grad = pair_grad[:, :, :, 0]
    value_grad = pair_grad[:, :, :, 1]
    query_grad_raw = unit_rows_back(query_raw, query_inverse, query_grad_all.reshape(heads_shape))
    key_grad_raw = unit_rows_back(key_raw, key_inverse, key_grad.reshape(heads_shape))
    grad_projected = jnp.stack([query_grad_raw.reshape(grid_shape + (head_width,)), key_grad_raw.reshape(grid_shape + (head_width,)), value_grad], 0).astype(jnp.bfloat16)
    flat_grad = grad_projected.reshape(3, NT * NH * NW, head_width)
    grad_normed = jnp.dot(flat_grad[0], qkv_weight[0].T, preferred_element_type=jnp.float32)
    grad_normed = grad_normed + jnp.dot(flat_grad[1], qkv_weight[1].T, preferred_element_type=jnp.float32)
    grad_normed = grad_normed + jnp.dot(flat_grad[2], qkv_weight[2].T, preferred_element_type=jnp.float32)
    grad_normed = grad_normed.reshape(grid_shape + (D,))
    grad_tokens = unit_rows_back(token_values, row_inverse, norm_gain * grad_normed)
    return grad_tokens.astype(jnp.bfloat16)
```

```python
import functools
import math

import jax
import jax.numpy as jnp
from jax import lax
from jax.experimental import pallas as pl
from jax.experimental.pallas import tpu as pltpu
from jax.sharding import PartitionSpec as P

HEADS = 6
HEAD_DIM = 64
BLOCK = 4
CELLS = BLOCK * BLOCK * BLOCK
HALF = HEADS // 2
HALF_WIDTH = HALF * HEAD_DIM
PAIR_WIDTH = 2 * HALF_WIDTH
TILE = 2 * HEAD_DIM
TILES = PAIR_WIDTH // TILE
DEAD_TOKEN = 1024.0
DEAD_KEY = 64.0
DROPPED = -1e30

EPS = 1e-06
F32 = jnp.float32
BF16 = jnp.bfloat16


def pair_swap(array, axis, phase, periodic):
    count = lax.axis_size(axis)
    pairs = []
    for device in range(count):
        partner = device + 1 if device % 2 == phase else device - 1
        if periodic:
            partner = partner % count
        if 0 <= partner < count:
            pairs.append((device, partner))
    return lax.ppermute(array, axis, pairs)


def shift_by(array, axis, step):
    count = lax.axis_size(axis)
    pairs = [(i, i + step) for i in range(count) if 0 <= i + step < count]
    return lax.ppermute(array, axis, pairs)


def dot(a, b):
    return lax.dot_general(a, b, (((1,), (0,)), ((), ())), preferred_element_type=F32)


def dot_last(a, b):
    return lax.dot_general(a, b, (((1,), (1,)), ((), ())), preferred_element_type=F32)


def dot_first(a, b):
    return lax.dot_general(a, b, (((0,), (0,)), ((), ())), preferred_element_type=F32)


def head_means(values):
    rows = lax.broadcasted_iota(jnp.int32, (TILE, TILE), 0) // HEAD_DIM
    cols = lax.broadcasted_iota(jnp.int32, (TILE, TILE), 1) // HEAD_DIM
    ones = (rows == cols).astype(F32).astype(BF16)
    high = values.astype(BF16)
    low = (values - high.astype(F32)).astype(BF16)
    pieces = []
    for start in range(0, values.shape[1], TILE):
        cut = slice(start, start + TILE)
        pieces.append(dot(high[:, cut], ones) + dot(low[:, cut], ones))
    return jnp.concatenate(pieces, 1) * (1.0 / HEAD_DIM)


def block_order(lat_rows, lon_cols, count, parity):
    blocks = lon_cols // BLOCK
    row = lax.broadcasted_iota(jnp.int32, (count, count), 0)
    source = lax.broadcasted_iota(jnp.int32, (count, count), 1)
    slot = row // CELLS
    place = row % CELLS
    frame = place // (BLOCK * BLOCK)
    lat = (place // BLOCK) % BLOCK
    col = place % BLOCK
    block = jnp.where(parity == 1, blocks - 1 - slot, slot)
    wanted = (frame * lat_rows + lat) * lon_cols + block * BLOCK + col
    return (source == wanted).astype(F32).astype(BF16)


def norm_kernel(count_ref, tokens_ref, gain_ref, normed_ref, first_ref, last_ref):
    frames, lat_rows, lon_cols, width = tokens_ref.shape
    cells = frames * lat_rows * lon_cols
    blocks = lon_cols // BLOCK
    parity = lax.rem(lax.axis_index("lon"), 2)
    x = tokens_ref[...].astype(F32).reshape(cells, width)
    inverse = lax.rsqrt(jnp.mean(x * x, -1, keepdims=True) + EPS)
    normed = (x * inverse * gain_ref[...]).astype(BF16)
    normed = dot(block_order(lat_rows, lon_cols, cells, parity), normed)
    normed_ref[...] = normed.astype(BF16)
    place = lax.broadcasted_iota(jnp.int32, (CELLS, 1), 0)
    for slot, out in ((0, first_ref), (blocks - 1, last_ref)):
        block = jnp.where(parity == 1, blocks - 1 - slot, slot)
        live = place < count_ref[0, 0, block]
        rows = normed[slot * CELLS : (slot + 1) * CELLS]
        out[...] = jnp.where(live, rows, DEAD_TOKEN).astype(BF16)


def halves(first, second):
    low = jnp.concatenate([first[:, :HALF_WIDTH], second[:, :HALF_WIDTH]], 1)
    high = jnp.concatenate([first[:, HALF_WIDTH:], second[:, HALF_WIDTH:]], 1)
    return low, high


def project_kernel(
    count_ref, normed_ref, grad_ref, qkv_ref, out_weight_ref,
    kv_own_ref, kv_other_ref, qg_own_ref, qg_other_ref, raw_ref,
):
    frames, lat_rows, lon_cols, width = grad_ref.shape
    cells = frames * lat_rows * lon_cols
    blocks = lon_cols // BLOCK
    parity = lax.rem(lax.axis_index("lon"), 2)
    upper = lax.rem(lax.axis_index("lat"), 2) == 1
    normed = normed_ref[...]
    query = dot(normed, qkv_ref[0])
    key = dot(normed, qkv_ref[1])
    value = dot(normed, qkv_ref[2])
    raw_ref[:, : HEADS * HEAD_DIM] = query
    raw_ref[:, HEADS * HEAD_DIM :] = key
    grad = dot_last(
        grad_ref[...].astype(F32).reshape(cells, width).astype(BF16), out_weight_ref[...]
    ).astype(BF16)
    grad = dot(block_order(lat_rows, lon_cols, cells, parity), grad)
    query = query * lax.rsqrt(head_means(query * query) + EPS)
    key = key * lax.rsqrt(head_means(key * key) + EPS)
    place = lax.broadcasted_iota(jnp.int32, (CELLS, 1), 0)
    live = []
    for slot in range(blocks):
        block = jnp.where(parity == 1, blocks - 1 - slot, slot)
        live.append(place < count_ref[0, 0, block])
    key = jnp.where(jnp.concatenate(live, 0), key, DEAD_KEY)
    low, high = halves(key, value)
    shape = (blocks, CELLS, PAIR_WIDTH)
    kv_own_ref[1 : blocks + 1] = jnp.where(upper, high, low).astype(BF16).reshape(shape)
    kv_other_ref[1 : blocks + 1] = jnp.where(upper, low, high).astype(BF16).reshape(shape)
    low, high = halves(query, grad)
    qg_own_ref[...] = jnp.where(upper, high, low).astype(BF16).reshape(shape)
    qg_other_ref[...] = jnp.where(upper, low, high).astype(BF16).reshape(shape)


def halo_kernel(first_ref, last_ref, qkv_ref, own_in, other_in, kv_own_ref, kv_other_ref):
    slots = own_in.shape[0]
    upper = lax.rem(lax.axis_index("lat"), 2) == 1
    normed = jnp.concatenate([first_ref[...], last_ref[...]], 0)
    key = dot(normed, qkv_ref[1])
    value = dot(normed, qkv_ref[2])
    key = key * lax.rsqrt(head_means(key * key) + EPS)
    dead = normed[:, 0:1].astype(F32) > 0.5 * DEAD_TOKEN
    key = jnp.where(dead, DEAD_KEY, key)
    low, high = halves(key, value)
    own = jnp.where(upper, high, low).astype(BF16)
    other = jnp.where(upper, low, high).astype(BF16)
    for made, source, out in ((own, own_in, kv_own_ref), (other, other_in, kv_other_ref)):
        out[0] = made[:CELLS]
        out[1 : slots - 1] = source[1 : slots - 1]
        out[slots - 1] = made[CELLS:]


def attend_kernel(rows, scale_ref, qg_own_ref, qg_other_ref, *refs):
    kv_refs, refs = refs[: 3 * rows], refs[3 * rows :]
    (own_ref, near_ref, far_ref, dq_own_ref, dq_other_ref,
     mid, left, right, backward, weights, e_buf, p_buf, d_buf, dkv_mid, dkv_left, dkv_right) = refs
    groups = 3 * rows
    tm = lax.axis_index("tm")
    tm_odd = lax.rem(tm, 2) == 1
    frames = lax.axis_size("tm")
    lat = lax.axis_index("lat")
    upper = lax.rem(lat, 2)
    pair = lat // 2
    near_at = jnp.where(tm_odd, tm - 1, tm + 1)
    far_at = jnp.where(tm_odd, tm + 1, tm - 1)
    near_in = ((near_at >= 0) & (near_at < frames)).astype(F32)
    far_in = ((far_at >= 0) & (far_at < frames)).astype(F32)
    queries = 4 * CELLS
    side = 2 * CELLS

    q_rows = jnp.concatenate(
        [qg_own_ref[0], qg_other_ref[0], qg_own_ref[1], qg_other_ref[1]], 0
    ).astype(F32)
    q_cols = q_rows.T
    lane_half = lax.broadcasted_iota(jnp.int32, (queries, TILE), 1) // HEAD_DIM
    row_half = lax.broadcasted_iota(jnp.int32, (TILE, queries), 0) // HEAD_DIM
    for j in range(2 * HALF):
        tile = slice((j // 2) * TILE, (j // 2 + 1) * TILE)
        backward[j] = jnp.where(lane_half == j % 2, q_rows[:, tile], 0.0).astype(BF16)
        weights[j] = jnp.where(row_half == j % 2, q_cols[tile], 0.0).astype(BF16)
    for group, ref in enumerate(kv_refs):
        left[group * CELLS : (group + 1) * CELLS] = ref[0]
        mid[group * side : group * side + CELLS] = ref[1]
        mid[group * side + CELLS : (group + 1) * side] = ref[2]
        right[group * CELLS : (group + 1) * CELLS] = ref[3]

    lane_row = (lax.broadcasted_iota(jnp.int32, (1, queries), 1) // CELLS) % 2

    def group_bias(group):
        frame, row = group // rows, lax.rem(group, rows)
        there = jnp.where(frame == 0, 1.0, jnp.where(frame == 1, near_in, far_in))
        if rows == 2:
            return jnp.full((1, queries), (1.0 - there) * DROPPED)
        pairs = lax.axis_size("lat") // 2
        before = (row == 2).astype(F32) * (pair > 0).astype(F32)
        after = (row == 3).astype(F32) * (pair < pairs - 1).astype(F32)
        inside = (row < 2).astype(F32)
        even = (lane_row == upper).astype(F32)
        return (1.0 - there * (inside + before * even + after * (1.0 - even))) * DROPPED

    scales = [scale_ref[upper * HALF + h] * (1.0 / math.sqrt(HEAD_DIM)) for h in range(HALF)]
    to_exp2 = [s * math.log2(math.e) for s in scales]

    def first_pass(chunk, carry, scores_of, bias_of, count):
        out = []
        start = pl.multiple_of(chunk * count, count)
        bias = bias_of()
        for h in range(HALF):
            total, inner = carry[2 * h], carry[2 * h + 1]
            scores = scores_of(h)
            grad_prob = scores_of(HALF + h)
            masked = jnp.exp2(scores * to_exp2[h] + bias)
            e_buf[h, pl.ds(start, count)] = masked
            p_buf[h, pl.ds(start, count)] = grad_prob
            out.append(total + jnp.sum(masked.reshape(count // 8, 8, queries), 0))
            out.append(inner + jnp.sum((masked * grad_prob).reshape(count // 8, 8, queries), 0))
        return tuple(out)

    def row_bias(keys):
        return jnp.where(keys[:, 0:1].astype(F32) < 0.5 * DEAD_KEY, 0.0, DROPPED)

    def mid_chunk(group, carry):
        keys = mid[pl.ds(pl.multiple_of(group * side, side), side)]

        def scores_of(j):
            tile = slice((j // 2) * TILE, (j // 2 + 1) * TILE)
            return dot(keys[:, tile], weights[j])

        return first_pass(
            group, carry, scores_of, lambda: row_bias(keys) + group_bias(group), side
        )

    def edge_chunk(group, carry):
        at = pl.ds(pl.multiple_of(group * CELLS, CELLS), CELLS)
        keys_left, keys_right = left[at], right[at]

        def scores_of(j):
            tile = slice((j // 2) * TILE, (j // 2 + 1) * TILE)
            return jnp.concatenate(
                [
                    dot(keys_left[:, tile], weights[j, :, :side]),
                    dot(keys_right[:, tile], weights[j, :, side:]),
                ],
                1,
            )

        def bias_of():
            both = jnp.concatenate(
                [
                    jnp.broadcast_to(row_bias(keys_left), (CELLS, side)),
                    jnp.broadcast_to(row_bias(keys_right), (CELLS, side)),
                ],
                1,
            )
            return both + group_bias(group)

        return first_pass(group + 2 * groups, carry, scores_of, bias_of, CELLS)

    carry = tuple(jnp.zeros((8, queries), F32) for _ in range(2 * HALF))
    carry = lax.fori_loop(0, groups, mid_chunk, carry)
    carry = lax.fori_loop(0, groups, edge_chunk, carry)
    inverse, delta = [], []
    for h in range(HALF):
        total = jnp.sum(carry[2 * h], 0, keepdims=True)
        inverse.append(1.0 / total)
        delta.append(jnp.sum(carry[2 * h + 1], 0, keepdims=True) * inverse[h])

    def parts(start, count):
        at = pl.ds(start, count)
        grads, probs = [], []
        for h in range(HALF):
            prob = e_buf[h, at] * inverse[h]
            probs.append(prob.astype(BF16))
            grads.append((prob * (p_buf[h, at] - delta[h]) * scales[h]).astype(BF16))
            d_buf[h, at] = grads[h]
        return grads + probs

    def mid_back(group, carry):
        start = pl.multiple_of(group * side, side)
        pieces = parts(start, side)
        for tile in range(TILES):
            both = jnp.concatenate([pieces[2 * tile], pieces[2 * tile + 1]], 1)
            dkv_mid[pl.ds(start, side), tile * TILE : (tile + 1) * TILE] = dot(
                both, backward[2 * tile : 2 * tile + 2].reshape(2 * queries, TILE)
            )
        return carry

    def edge_back(group, carry):
        start = pl.multiple_of(group * CELLS, CELLS)
        pieces = parts(start + groups * side, CELLS)
        for tile in range(TILES):
            cut = slice(tile * TILE, (tile + 1) * TILE)
            for out, lanes in ((dkv_left, slice(0, side)), (dkv_right, slice(side, queries))):
                both = jnp.concatenate(
                    [pieces[2 * tile][:, lanes], pieces[2 * tile + 1][:, lanes]], 1
                )
                out[pl.ds(start, CELLS), cut] = dot(
                    both, backward[2 * tile : 2 * tile + 2, lanes].reshape(2 * side, TILE)
                )
        return carry

    lax.fori_loop(0, groups, mid_back, 0)
    lax.fori_loop(0, groups, edge_back, 0)

    mid_total = groups * side
    columns = []
    for h in range(HALF):
        tile = slice((h // 2) * TILE, (h // 2 + 1) * TILE)
        own = slice((h % 2) * HEAD_DIM, (h % 2 + 1) * HEAD_DIM)
        from_mid = dot_first(mid[:, tile], d_buf[h, :mid_total])[own]
        from_left = dot_first(left[:, tile], d_buf[h, mid_total:, :side])[own]
        from_right = dot_first(right[:, tile], d_buf[h, mid_total:, side:])[own]
        columns.append(from_mid + jnp.concatenate([from_left, from_right], 1))
    dq = jnp.concatenate(columns, 0).T
    dq_own_ref[...] = jnp.concatenate([dq[:CELLS], dq[2 * CELLS : 3 * CELLS]], 1)
    dq_other_ref[...] = jnp.concatenate([dq[CELLS : 2 * CELLS], dq[3 * CELLS :]], 1)

    for group in range(groups):
        out = (own_ref, near_ref, far_ref)[group // rows]
        row = group % rows
        out[row, 0] = dkv_left[group * CELLS : (group + 1) * CELLS].astype(out.dtype)
        out[row, 1] = dkv_mid[group * side : group * side + CELLS].astype(out.dtype)
        out[row, 2] = dkv_mid[group * side + CELLS : (group + 1) * side].astype(out.dtype)
        out[row, 3] = dkv_right[group * CELLS : (group + 1) * CELLS].astype(out.dtype)


def frame_sum_kernel(own_ref, near_ref, far_ref, inner_ref, first_ref, last_ref):
    total = own_ref[...] + near_ref[...].astype(F32) + far_ref[...].astype(F32)
    slots = own_ref.shape[1]
    first_ref[...] = total[:, 0].astype(BF16)
    last_ref[...] = total[:, slots - 1].astype(BF16)
    inner_ref[...] = total[:, 1 : slots - 1]


def column_sum_kernel(inner_ref, first_ref, last_ref, dq_other_ref, own_ref, other_ref):
    first = inner_ref[:, 0] + first_ref[...].astype(F32)
    last = inner_ref[:, 1] + last_ref[...].astype(F32)
    own_ref[0] = first[0]
    own_ref[1] = last[0]
    other_ref[0] = first[1].astype(BF16)
    other_ref[1] = last[1].astype(BF16)
    other_ref[2] = dq_other_ref[...].astype(BF16)


def finish_kernel(
    dkv_ref, dq_ref, other_ref, raw_ref, tokens_ref, gain_ref, qkv_ref, out_ref
):
    frames, lat_rows, lon_cols, width = tokens_ref.shape
    cells = frames * lat_rows * lon_cols
    parity = lax.rem(lax.axis_index("lon"), 2)
    upper = lax.rem(lax.axis_index("lat"), 2) == 1

    def joined(mine, theirs):
        return jnp.where(
            upper, jnp.concatenate([theirs, mine], 1), jnp.concatenate([mine, theirs], 1)
        )

    def by_slot(packed):
        return jnp.concatenate([packed[:, :HALF_WIDTH], packed[:, HALF_WIDTH:]], 0)

    dkv_mine = dkv_ref[...].reshape(cells, PAIR_WIDTH)
    dkv_theirs = other_ref[:2].astype(F32).reshape(cells, PAIR_WIDTH)
    grads = [
        joined(by_slot(dq_ref[...]), by_slot(other_ref[2].astype(F32))),
        joined(dkv_mine[:, :HALF_WIDTH], dkv_theirs[:, :HALF_WIDTH]),
        joined(dkv_mine[:, HALF_WIDTH:], dkv_theirs[:, HALF_WIDTH:]),
    ]
    head_width = HEADS * HEAD_DIM
    grad_normed = dot_last(grads[2].astype(BF16), qkv_ref[2])
    for c in range(2):
        raw = raw_ref[:, c * head_width : (c + 1) * head_width]
        inverse = lax.rsqrt(head_means(raw * raw) + EPS)
        inner = head_means(raw * grads[c])
        grad_raw = inverse * grads[c] - inverse * inverse * inverse * raw * inner
        grad_normed = grad_normed + dot_last(grad_raw.astype(BF16), qkv_ref[c])
    order = block_order(lat_rows, lon_cols, cells, parity)
    x = tokens_ref[...].astype(F32).reshape(cells, width)
    x = dot(order, x.astype(BF16))
    inverse = lax.rsqrt(jnp.mean(x * x, -1, keepdims=True) + EPS)
    grad = gain_ref[...] * grad_normed
    inner = jnp.mean(x * grad, -1, keepdims=True)
    grad = (inverse * grad - inverse * inverse * inverse * x * inner).astype(BF16)
    grad = dot_first(order, grad)
    out_ref[...] = grad.reshape(tokens_ref.shape).astype(BF16)


SMEM = pl.BlockSpec(memory_space=pltpu.SMEM)
VMEM = pl.BlockSpec(memory_space=pltpu.VMEM)


def kernel_call(body, name, outs, args, smem=0, scratch=(), limit_mib=16, flops=0, moved=0):
    return pl.pallas_call(
        body,
        name=name,
        out_shape=[jax.ShapeDtypeStruct(shape, dtype) for shape, dtype in outs],
        in_specs=[SMEM] * smem + [VMEM] * (len(args) - smem),
        out_specs=[VMEM] * len(outs),
        scratch_shapes=list(scratch),
        compiler_params=pltpu.CompilerParams(vmem_limit_bytes=limit_mib * 1024 * 1024),
        cost_estimate=pl.CostEstimate(flops=flops, bytes_accessed=moved, transcendentals=0),
    )(*args)


def per_device(tokens, key_count, norm_gain, qkv_weight, out_weight, logit_scale, grad_out):
    frames, lat_rows, lon_cols, width = tokens.shape
    assert frames == BLOCK and lat_rows == BLOCK and lon_cols == 2 * BLOCK
    assert lax.axis_size("lat") % 2 == 0 and lax.axis_size("lon") % 2 == 0
    cells = frames * lat_rows * lon_cols
    blocks = lon_cols // BLOCK
    head_width = HEADS * HEAD_DIM
    gain = norm_gain.reshape(1, width)
    kv_shape = ((blocks + 2, CELLS, PAIR_WIDTH), BF16)
    qg_shape = ((blocks, CELLS, PAIR_WIDTH), BF16)

    normed, first, last = kernel_call(
        norm_kernel, "norm",
        [((cells, width), BF16), ((CELLS, width), BF16), ((CELLS, width), BF16)],
        [key_count, tokens, gain], smem=1,
    )
    near_first = pair_swap(first, "lon", 1, True)
    near_last = pair_swap(last, "lon", 0, True)
    kv_own, kv_other, qg_own, qg_other, raw = kernel_call(
        project_kernel, "project",
        [kv_shape, kv_shape, qg_shape, qg_shape, ((cells, 2 * head_width), F32)],
        [key_count, normed, grad_out, qkv_weight, out_weight], smem=1,
        flops=8 * cells * width * head_width, moved=5_000_000,
    )
    kv_own, kv_other = kernel_call(
        halo_kernel, "halo", [kv_shape, kv_shape],
        [near_first, near_last, qkv_weight, kv_own, kv_other],
    )
    kv_rows = [kv_own, pair_swap(kv_other, "lat", 0, False)]
    qg_other = pair_swap(qg_other, "lat", 0, False)
    upper = lax.rem(lax.axis_index("lat"), 2) == 1
    wide = lax.axis_size("lat") > 2
    if wide:
        even = jnp.where(upper, kv_rows[1], kv_rows[0])
        odd = jnp.where(upper, kv_rows[0], kv_rows[1])
        kv_rows += [shift_by(odd, "lat", 2), shift_by(even, "lat", -2)]
    rows = len(kv_rows)
    kv_all = list(kv_rows)
    for phase in range(2):
        kv_all += [pair_swap(kv, "tm", phase, False) for kv in kv_rows]

    groups = 3 * rows
    queries = 4 * CELLS
    part_shape = (rows, blocks + 2, CELLS, PAIR_WIDTH)
    packed = (CELLS, 2 * HALF_WIDTH)
    own, near, far, dq_own, dq_other = kernel_call(
        functools.partial(attend_kernel, rows), "attend",
        [(part_shape, F32), (part_shape, BF16), (part_shape, BF16), (packed, F32), (packed, F32)],
        [logit_scale, qg_own, qg_other, *kv_all], smem=1,
        scratch=[
            pltpu.VMEM((groups * 2 * CELLS, PAIR_WIDTH), BF16),
            pltpu.VMEM((groups * CELLS, PAIR_WIDTH), BF16),
            pltpu.VMEM((groups * CELLS, PAIR_WIDTH), BF16),
            pltpu.VMEM((2 * HALF, queries, TILE), BF16),
            pltpu.VMEM((2 * HALF, TILE, queries), BF16),
            pltpu.VMEM((HALF, groups * 3 * CELLS, queries), F32),
            pltpu.VMEM((HALF, groups * 3 * CELLS, queries), F32),
            pltpu.VMEM((HALF, groups * 3 * CELLS, queries), BF16),
            pltpu.VMEM((groups * 2 * CELLS, PAIR_WIDTH), F32),
            pltpu.VMEM((groups * CELLS, PAIR_WIDTH), F32),
            pltpu.VMEM((groups * CELLS, PAIR_WIDTH), F32),
        ],
        limit_mib=24 * rows // 2,
        flops=24 * groups * 3 * CELLS * queries * HALF * HEAD_DIM, moved=5_000_000,
    )
    if wide:
        summed = []
        for part in (own, near, far):
            to_below = shift_by(part[2].astype(BF16), "lat", -2)
            to_above = shift_by(part[3].astype(BF16), "lat", 2)
            to_odd, to_even = to_below.astype(F32), to_above.astype(F32)
            add_own = jnp.where(upper, to_odd, to_even)
            add_other = jnp.where(upper, to_even, to_odd)
            both = part[:2].astype(F32) + jnp.stack([add_own, add_other], 0)
            summed.append(both.astype(part.dtype))
        own, near, far = summed
    near = pair_swap(near, "tm", 0, False)
    far = pair_swap(far, "tm", 1, False)
    edge = ((2, CELLS, PAIR_WIDTH), BF16)
    inner, first, last = kernel_call(
        frame_sum_kernel, "frame_sum",
        [((2, blocks, CELLS, PAIR_WIDTH), F32), edge, edge], [own, near, far],
    )
    first = pair_swap(first, "lon", 1, True)
    last = pair_swap(last, "lon", 0, True)
    dkv_own, other = kernel_call(
        column_sum_kernel, "column_sum",
        [((blocks, CELLS, PAIR_WIDTH), F32), ((blocks + 1, CELLS, PAIR_WIDTH), BF16)],
        [inner, first, last, dq_other],
    )
    other = pair_swap(other, "lat", 0, False)
    (grad_tokens,) = kernel_call(
        finish_kernel, "finish", [(tokens.shape, BF16)],
        [dkv_own, dq_own, other, raw, tokens, gain, qkv_weight],
        flops=6 * cells * width * head_width, moved=4_000_000,
    )
    return grad_tokens


def solution(mesh):
    in_specs = (
        P("tm", "lat", "lon", None),
        P("tm", "lat", "lon"),
        P(),
        P(),
        P(),
        P(),
        P("tm", "lat", "lon", None),
    )
    out_specs = P("tm", "lat", "lon", None)
    return jax.shard_map(
        per_device, mesh=mesh, in_specs=in_specs, out_specs=out_specs, check_vma=False
    )
```

```python
import functools
import math

import jax
import jax.numpy as jnp
from jax import lax
from jax.experimental import pallas as pl
from jax.experimental.pallas import tpu as pltpu
from jax.sharding import PartitionSpec as P

HEADS = 6
HEAD_DIM = 64
BLOCK = 4
CELLS = BLOCK * BLOCK * BLOCK
HALF = HEADS // 2
HALF_WIDTH = HALF * HEAD_DIM
PAIR_WIDTH = 2 * HALF_WIDTH
TILE = 2 * HEAD_DIM
TILES = PAIR_WIDTH // TILE
DEAD_KEY = 64.0
DROPPED = -1e30
FLOPS_PER_US = 1e9

EPS = 1e-06
F32 = jnp.float32
BF16 = jnp.bfloat16


def partner_of(device, count, phase):
    return device + 1 if device % 2 == phase else device - 1


def pair_swap(array, axis, phase):
    count = lax.axis_size(axis)
    pairs = [(device, partner_of(device, count, phase) % count) for device in range(count)]
    return lax.ppermute(array, axis, pairs)


def frame_swap(array, phase):
    frames, lons = lax.axis_size("tm"), lax.axis_size("lon")
    pairs = []
    for frame in range(frames):
        for lon in range(lons):
            to = (partner_of(frame, frames, phase), lon)
            if not 0 <= to[0] < frames:
                to = (frame, partner_of(lon, lons, 0))
            pairs.append((frame * lons + lon, to[0] * lons + to[1]))
    return lax.ppermute(array, ("tm", "lon"), pairs)


def corner_swap(array):
    lats, lons = lax.axis_size("lat"), lax.axis_size("lon")
    pairs = []
    for lat in range(lats):
        for lon in range(lons):
            to = partner_of(lat, lats, 0) * lons + partner_of(lon, lons, 1) % lons
            pairs.append((lat * lons + lon, to))
    return lax.ppermute(array, ("lat", "lon"), pairs)


def shift_by(array, axis, step):
    count = lax.axis_size(axis)
    pairs = [(i, i + step) for i in range(count) if 0 <= i + step < count]
    return lax.ppermute(array, axis, pairs)


def dot(a, b):
    return lax.dot_general(a, b, (((1,), (0,)), ((), ())), preferred_element_type=F32)


def dot_last(a, b):
    return lax.dot_general(a, b, (((1,), (1,)), ((), ())), preferred_element_type=F32)


def dot_first(a, b):
    return lax.dot_general(a, b, (((0,), (0,)), ((), ())), preferred_element_type=F32)


def head_means(values):
    rows = lax.broadcasted_iota(jnp.int32, (TILE, TILE), 0) // HEAD_DIM
    cols = lax.broadcasted_iota(jnp.int32, (TILE, TILE), 1) // HEAD_DIM
    ones = (rows == cols).astype(F32).astype(BF16)
    high = values.astype(BF16)
    low = (values - high.astype(F32)).astype(BF16)
    pieces = []
    for start in range(0, values.shape[1], TILE):
        cut = slice(start, start + TILE)
        pieces.append(dot(high[:, cut], ones) + dot(low[:, cut], ones))
    return jnp.concatenate(pieces, 1) * (1.0 / HEAD_DIM)


def block_order(lat_rows, lon_cols, count, parity):
    blocks = lon_cols // BLOCK
    row = lax.broadcasted_iota(jnp.int32, (count, count), 0)
    source = lax.broadcasted_iota(jnp.int32, (count, count), 1)
    slot = row // CELLS
    place = row % CELLS
    frame = place // (BLOCK * BLOCK)
    lat = (place // BLOCK) % BLOCK
    col = place % BLOCK
    block = jnp.where(parity == 1, blocks - 1 - slot, slot)
    wanted = (frame * lat_rows + lat) * lon_cols + block * BLOCK + col
    return (source == wanted).astype(F32).astype(BF16)


def halves(first, second):
    low = jnp.concatenate([first[:, :HALF_WIDTH], second[:, :HALF_WIDTH]], 1)
    high = jnp.concatenate([first[:, HALF_WIDTH:], second[:, HALF_WIDTH:]], 1)
    return low, high


def normalised(x, gain_ref):
    inverse = lax.rsqrt(jnp.mean(x * x, -1, keepdims=True) + EPS)
    return (x * inverse * gain_ref[...].reshape(1, x.shape[1])).astype(BF16)


def order_kernel(lat_rows, lon_cols, order_ref):
    parity = lax.rem(lax.axis_index("lon"), 2)
    order_ref[...] = block_order(lat_rows, lon_cols, order_ref.shape[0], parity)


def project_kernel(
    count_ref, order_ref, tokens_ref, gain_ref, grad_ref, qkv_ref, out_weight_ref,
    kv_own_ref, qg_own_ref, kv_other_ref, qg_other_ref, raw_ref, inverse_ref, x_ref,
):
    frames, lat_rows, lon_cols, width = grad_ref.shape
    cells = frames * lat_rows * lon_cols
    blocks = lon_cols // BLOCK
    parity = lax.rem(lax.axis_index("lon"), 2)
    upper = lax.rem(lax.axis_index("lat"), 2) == 1
    order = order_ref[...]
    x = tokens_ref[...].astype(F32).reshape(cells, width)
    x = dot(order, x.astype(BF16))
    x_ref[...] = x.astype(BF16)
    normed = normalised(x, gain_ref)
    query, key, value = (dot(normed, qkv_ref[c]) for c in range(3))
    head_width = HEADS * HEAD_DIM
    raw_ref[:, :head_width] = query
    raw_ref[:, head_width:] = key
    grad = dot_last(
        grad_ref[...].astype(F32).reshape(cells, width).astype(BF16), out_weight_ref[...]
    ).astype(BF16)
    grad = dot(order, grad)
    query_inverse = lax.rsqrt(head_means(query * query) + EPS)
    key_inverse = lax.rsqrt(head_means(key * key) + EPS)
    inverse_ref[:, :head_width] = query_inverse
    inverse_ref[:, head_width:] = key_inverse
    query = query * query_inverse
    key = key * key_inverse
    place = lax.broadcasted_iota(jnp.int32, (CELLS, 1), 0)
    live = []
    for slot in range(blocks):
        block = jnp.where(parity == 1, blocks - 1 - slot, slot)
        live.append(place < count_ref[0, 0, block])
    key = jnp.where(jnp.concatenate(live, 0), key, DEAD_KEY)
    shape = (blocks, CELLS, PAIR_WIDTH)
    low, high = halves(key, value)
    kv_own_ref[...] = jnp.where(upper, high, low).astype(BF16).reshape(shape)
    kv_other_ref[...] = jnp.where(upper, low, high).astype(BF16).reshape(shape)
    low, high = halves(query, grad)
    qg_own_ref[...] = jnp.where(upper, high, low).astype(BF16).reshape(shape)
    qg_other_ref[...] = jnp.where(upper, low, high).astype(BF16).reshape(shape)


def halo_kernel(blocks, count_ref, first_ref, gain_ref, qkv_ref, other_ref, half_ref):
    upper = lax.rem(lax.axis_index("lat"), 2) == 1
    x = first_ref[...].astype(F32)
    normed = normalised(x, gain_ref)
    key = dot(normed, qkv_ref[1])
    value = dot(normed, qkv_ref[2])
    key = key * lax.rsqrt(head_means(key * key) + EPS)
    odd = lax.rem(lax.axis_index("lon"), 2) == 1
    live = count_ref[0, 0, jnp.where(odd, 0, blocks - 1)]
    place = lax.broadcasted_iota(jnp.int32, (CELLS, 1), 0)
    key = jnp.where(place < live, key, DEAD_KEY)
    low, high = halves(key, value)
    half_ref[...] = jnp.where(upper, high, low).astype(BF16)
    other_ref[...] = jnp.where(upper, low, high).astype(BF16)


def join_kernel(half_ref, own_in, kv_own_ref):
    kv_own_ref[0] = half_ref[...]
    kv_own_ref[1:] = own_in[...]


def lane_tile(j):
    return slice((j // 2) * TILE, (j // 2 + 1) * TILE)


class Place:
    def __init__(self, rows):
        self.rows = rows
        tm, frames = lax.axis_index("tm"), lax.axis_size("tm")
        odd = lax.rem(tm, 2) == 1
        near, far = jnp.where(odd, tm - 1, tm + 1), jnp.where(odd, tm + 1, tm - 1)
        self.there = [None] + [((at >= 0) & (at < frames)) for at in (near, far)]
        self.upper = lax.rem(lax.axis_index("lat"), 2)

    def bias(self, frame, row, lanes):
        there = self.there[frame]
        total = 0.0 if there is None else jnp.where(there, 0.0, DROPPED)
        if row < 2:
            return total
        pair, pairs = lax.axis_index("lat") // 2, lax.axis_size("lat") // 2
        if row == 2:
            inside, wanted = pair > 0, self.upper
        else:
            inside, wanted = pair < pairs - 1, 1 - self.upper
        lane_row = (lax.broadcasted_iota(jnp.int32, (1, lanes), 1) // CELLS) % 2
        seen = (lane_row == wanted) & inside
        return total + jnp.where(seen, 0.0, DROPPED)


def head_scales(scale_ref):
    upper = lax.rem(lax.axis_index("lat"), 2)
    return [scale_ref[upper * HALF + h] * (1.0 / math.sqrt(HEAD_DIM)) for h in range(HALF)]


def key_bias(keys):
    return jnp.where(keys[:, 0:1].astype(F32) < 0.5 * DEAD_KEY, 0.0, DROPPED)


def score(keys, bias, weights_ref, lanes, scales, sums):
    count = keys.shape[0]
    exps, probs = [], []
    for h in range(HALF):
        scores = dot(keys[:, lane_tile(h)], weights_ref[h, :, lanes])
        grad_prob = dot(keys[:, lane_tile(HALF + h)], weights_ref[HALF + h, :, lanes])
        masked = jnp.exp2(scores * (scales[h] * math.log2(math.e)) + bias)
        shape = (count // 8, 8, masked.shape[1])
        sums[h] = sums[h] + jnp.sum(masked.reshape(shape), 0)
        sums[HALF + h] = sums[HALF + h] + jnp.sum((masked * grad_prob).reshape(shape), 0)
        exps.append(masked)
        probs.append(grad_prob)
    return exps, probs


ALL = slice(0, 4 * CELLS)
FIRST = slice(0, 2 * CELLS)
LAST = slice(2 * CELLS, 4 * CELLS)


def score_groups(place, frames, kv_refs, weights_ref, scales, sums, e_mid, p_mid, e_left, p_left):
    rows = place.rows
    side = [jnp.zeros((8, 2 * CELLS), F32) for _ in range(2 * HALF)]
    for index, ref in enumerate(kv_refs):
        frame, row = frames[index // rows], index % rows
        keys = ref[1:3].reshape(2 * CELLS, PAIR_WIDTH)
        bias = key_bias(keys) + place.bias(frame, row, 4 * CELLS)
        exps, probs = score(keys, bias, weights_ref, ALL, scales, sums)
        for h in range(HALF):
            e_mid[h, index * 2 * CELLS : (index + 1) * 2 * CELLS] = exps[h]
            p_mid[h, index * 2 * CELLS : (index + 1) * 2 * CELLS] = probs[h]
    for index in range(0, len(kv_refs), 2):
        frame, row = frames[index // rows], index % rows
        pair = [kv_refs[index][0], kv_refs[index + 1][0]]
        bias = jnp.concatenate(
            [
                jnp.broadcast_to(
                    key_bias(keys) + place.bias(frame, row + i, 2 * CELLS), (CELLS, 2 * CELLS)
                )
                for i, keys in enumerate(pair)
            ],
            0,
        )
        keys = jnp.concatenate(pair, 0)
        exps, probs = score(keys, bias, weights_ref, FIRST, scales, side)
        for h in range(HALF):
            e_left[h, index * CELLS : (index + 2) * CELLS] = exps[h]
            p_left[h, index * CELLS : (index + 2) * CELLS] = probs[h]
    return [jnp.concatenate([a[:, FIRST] + b, a[:, LAST]], 1) for a, b in zip(sums, side)]


def own_score_kernel(rows, scale_ref, qg_own_ref, qg_other_ref, *refs):
    kv_refs, refs = refs[:rows], refs[rows:]
    weights, backward, sums_ref, e_mid, p_mid, e_left, p_left = refs
    queries = 4 * CELLS
    q_rows = jnp.concatenate(
        [qg_own_ref[0], qg_other_ref[0], qg_own_ref[1], qg_other_ref[1]], 0
    ).astype(F32)
    q_cols = q_rows.T
    lane_half = lax.broadcasted_iota(jnp.int32, (queries, TILE), 1) // HEAD_DIM
    row_half = lax.broadcasted_iota(jnp.int32, (TILE, queries), 0) // HEAD_DIM
    for j in range(2 * HALF):
        backward[j] = jnp.where(lane_half == j % 2, q_rows[:, lane_tile(j)], 0.0).astype(BF16)
        weights[j] = jnp.where(row_half == j % 2, q_cols[lane_tile(j)], 0.0).astype(BF16)
    sums = [jnp.zeros((8, queries), F32) for _ in range(2 * HALF)]
    sums = score_groups(
        Place(rows), (0,), kv_refs, weights, head_scales(scale_ref), sums,
        e_mid, p_mid, e_left, p_left,
    )
    for j in range(2 * HALF):
        sums_ref[j] = sums[j]


def away_score_kernel(rows, scale_ref, weights, sums_in, *refs):
    kv_refs, refs = refs[: 2 * rows], refs[2 * rows :]
    sums_ref, e_mid, p_mid, e_left, p_left = refs
    sums = [sums_in[j] for j in range(2 * HALF)]
    sums = score_groups(
        Place(rows), (1, 2), kv_refs, weights, head_scales(scale_ref), sums,
        e_mid, p_mid, e_left, p_left,
    )
    for j in range(2 * HALF):
        sums_ref[j] = sums[j]


def grad_parts(exps, probs, inverse, delta, scales):
    grads, halves_of = [], []
    for h in range(HALF):
        prob = exps[h] * inverse[h]
        halves_of.append(prob.astype(BF16))
        grads.append((prob * (probs[h] - delta[h]) * scales[h]).astype(BF16))
    return grads + halves_of


def key_grads(pieces, backward, lanes):
    outs = []
    for tile in range(TILES):
        both = jnp.concatenate([pieces[2 * tile], pieces[2 * tile + 1]], 1)
        rows = jnp.concatenate(
            [backward[2 * tile, lanes], backward[2 * tile + 1, lanes]], 0
        )
        outs.append(dot(both, rows))
    return jnp.concatenate(outs, 1)


def query_grads(keys, grads, h):
    own = slice((h % 2) * HEAD_DIM, (h % 2 + 1) * HEAD_DIM)
    return dot_first(keys[:, lane_tile(h)], grads)[own]


def sibling_kernel(
    rows, scale_ref, weights, backward, sums_in, keys_ref, part_ref, stats_ref, dq_ref
):
    place, scales = Place(rows), head_scales(scale_ref)
    side = [jnp.zeros((8, 2 * CELLS), F32) for _ in range(2 * HALF)]
    made = []
    for index in range(0, 3 * rows, 2):
        frame, row = index // rows, index % rows
        bias = jnp.concatenate(
            [
                jnp.broadcast_to(
                    key_bias(keys_ref[index + i]) + place.bias(frame, row + i, 2 * CELLS),
                    (CELLS, 2 * CELLS),
                )
                for i in range(2)
            ],
            0,
        )
        keys = keys_ref[index : index + 2].reshape(2 * CELLS, PAIR_WIDTH)
        made.append(score(keys, bias, weights, LAST, scales, side))
    inverse, delta = [], []
    for h in range(HALF):
        total, inner = (
            jnp.concatenate([sums_in[j, :, FIRST], sums_in[j, :, LAST] + side[j]], 1)
            for j in (h, HALF + h)
        )
        inverse.append(1.0 / jnp.sum(total, 0, keepdims=True))
        delta.append(jnp.sum(inner, 0, keepdims=True) * inverse[h])
        stats_ref[h : h + 1] = inverse[h]
        stats_ref[HALF + h : HALF + h + 1] = delta[h]
    inverse = [a[:, LAST] for a in inverse]
    delta = [a[:, LAST] for a in delta]
    grads = []
    for index in range(0, 3 * rows, 2):
        pieces = grad_parts(*made[index // 2], inverse, delta, scales)
        grads.append(pieces[:HALF])
        made_part = key_grads(pieces, backward, LAST)
        part_ref[index : index + 2] = made_part.reshape(2, CELLS, PAIR_WIDTH).astype(BF16)
    keys = keys_ref[...].reshape(3 * rows * CELLS, PAIR_WIDTH)
    for h in range(HALF):
        dq_ref[h * HEAD_DIM : (h + 1) * HEAD_DIM] = query_grads(
            keys, jnp.concatenate([g[h] for g in grads], 0), h
        )


def back_groups(scales, stats_ref, backward, e_mid, p_mid, e_left, p_left, d_mid, d_left, put):
    inverse = [stats_ref[h : h + 1] for h in range(HALF)]
    delta = [stats_ref[HALF + h : HALF + h + 1] for h in range(HALF)]
    count = e_left.shape[1] // CELLS
    for index in range(count):
        at = slice(index * 2 * CELLS, (index + 1) * 2 * CELLS)
        exps, probs = [e_mid[h, at] for h in range(HALF)], [p_mid[h, at] for h in range(HALF)]
        pieces = grad_parts(exps, probs, inverse, delta, scales)
        for h in range(HALF):
            d_mid[h, at] = pieces[h]
        part = key_grads(pieces, backward, ALL)
        put(index, 1, part[:CELLS])
        put(index, 2, part[CELLS:])
    inverse = [a[:, FIRST] for a in inverse]
    delta = [a[:, FIRST] for a in delta]
    for index in range(0, count, 2):
        at = slice(index * CELLS, (index + 2) * CELLS)
        exps, probs = [e_left[h, at] for h in range(HALF)], [p_left[h, at] for h in range(HALF)]
        pieces = grad_parts(exps, probs, inverse, delta, scales)
        for h in range(HALF):
            d_left[h, at] = pieces[h]
        part = key_grads(pieces, backward, FIRST)
        put(index, 0, part[:CELLS])
        put(index + 1, 0, part[CELLS:])


def away_back_kernel(
    rows, scale_ref, stats_ref, backward, e_mid, p_mid, e_left, p_left,
    near_ref, far_ref, d_mid, d_left,
):
    def put(index, slot, part):
        (near_ref, far_ref)[index // rows][index % rows, slot] = part

    back_groups(
        head_scales(scale_ref), stats_ref, backward, e_mid, p_mid, e_left, p_left,
        d_mid, d_left, put,
    )


def sibling_sum_kernel(rows, near_in, far_in, sibling_ref, near_ref, far_ref):
    for frame, part, out in ((1, near_in, near_ref), (2, far_in, far_ref)):
        out[:, :2] = part[:, :2].astype(BF16)
        added = sibling_ref[frame * rows : (frame + 1) * rows].astype(F32)
        out[:, 2] = (part[:, 2] + added).astype(BF16)


def own_back_kernel(
    rows, scale_ref, stats_ref, backward, e_mid, p_mid, e_left, p_left,
    away_mid, away_left, dq_sibling, sibling_ref, *refs,
):
    kv_refs, refs = refs[: 3 * rows], refs[3 * rows :]
    own_ref, dq_own_ref, dq_other_ref, d_mid, d_left = refs

    def put(index, slot, part):
        if slot == 2:
            part = part + sibling_ref[index].astype(F32)
        own_ref[index, slot] = part

    back_groups(
        head_scales(scale_ref), stats_ref, backward, e_mid, p_mid, e_left, p_left,
        d_mid, d_left, put,
    )
    mid = jnp.concatenate([ref[1:3].reshape(2 * CELLS, PAIR_WIDTH) for ref in kv_refs], 0)
    left = jnp.concatenate([ref[0] for ref in kv_refs], 0)
    columns = []
    for h in range(HALF):
        made = query_grads(mid, jnp.concatenate([d_mid[h], away_mid[h]], 0), h)
        first = query_grads(left, jnp.concatenate([d_left[h], away_left[h]], 0), h)
        last = dq_sibling[h * HEAD_DIM : (h + 1) * HEAD_DIM]
        columns.append(made + jnp.concatenate([first, last], 1))
    dq = jnp.concatenate(columns, 0).T
    dq_own_ref[...] = jnp.concatenate([dq[:CELLS], dq[2 * CELLS : 3 * CELLS]], 1)
    dq_other_ref[...] = jnp.concatenate([dq[CELLS : 2 * CELLS], dq[3 * CELLS :]], 1)


def frame_sum_kernel(
    own_ref, near_ref, far_ref, dq_other_ref, inner_ref, to_lat_ref, edge_ref, corner_ref
):
    def total(row, slots):
        away = near_ref[row, slots].astype(F32) + far_ref[row, slots].astype(F32)
        return own_ref[row, slots] + away

    inner_ref[...] = total(0, slice(1, 3))
    to_lat_ref[:2] = total(1, slice(1, 3)).astype(BF16)
    to_lat_ref[2] = dq_other_ref[...].astype(BF16)
    edge_ref[...] = total(0, 0).astype(BF16)
    corner_ref[...] = total(1, 0).astype(BF16)


def finish_kernel(
    inner_ref, dq_ref, other_ref, edge_ref, corner_ref,
    raw_ref, inverse_ref, x_ref, order_ref, gain_ref, qkv_ref, out_ref,
):
    frames, lat_rows, lon_cols, width = out_ref.shape
    cells = frames * lat_rows * lon_cols
    parity = lax.rem(lax.axis_index("lon"), 2)
    upper = lax.rem(lax.axis_index("lat"), 2) == 1

    def joined(mine, theirs):
        return jnp.where(
            upper, jnp.concatenate([theirs, mine], 1), jnp.concatenate([mine, theirs], 1)
        )

    def by_slot(packed):
        return jnp.concatenate([packed[:, :HALF_WIDTH], packed[:, HALF_WIDTH:]], 0)

    def with_edge(inner, edge):
        return jnp.concatenate([inner[0] + edge.astype(F32), inner[1]], 0)

    dkv_mine = with_edge(inner_ref[...], edge_ref[...])
    dkv_theirs = with_edge(other_ref[:2].astype(F32), corner_ref[...])
    grads = [
        joined(by_slot(dq_ref[...]), by_slot(other_ref[2].astype(F32))),
        joined(dkv_mine[:, :HALF_WIDTH], dkv_theirs[:, :HALF_WIDTH]),
        joined(dkv_mine[:, HALF_WIDTH:], dkv_theirs[:, HALF_WIDTH:]),
    ]
    head_width = HEADS * HEAD_DIM
    grad_normed = dot_last(grads[2].astype(BF16), qkv_ref[2])
    for c in range(2):
        raw = raw_ref[:, c * head_width : (c + 1) * head_width]
        inverse = inverse_ref[:, c * head_width : (c + 1) * head_width]
        inner = head_means(raw * grads[c])
        grad_raw = inverse * grads[c] - inverse * inverse * inverse * raw * inner
        grad_normed = grad_normed + dot_last(grad_raw.astype(BF16), qkv_ref[c])
    order = order_ref[...]
    x = x_ref[...].astype(F32)
    inverse = lax.rsqrt(jnp.mean(x * x, -1, keepdims=True) + EPS)
    grad = gain_ref[...].reshape(1, width) * grad_normed
    inner = jnp.mean(x * grad, -1, keepdims=True)
    grad = (inverse * grad - inverse * inverse * inverse * x * inner).astype(BF16)
    grad = dot_first(order, grad)
    out_ref[...] = grad.reshape(out_ref.shape).astype(BF16)


SMEM = pl.BlockSpec(memory_space=pltpu.SMEM)
VMEM = pl.BlockSpec(memory_space=pltpu.VMEM)


def kernel_call(
    body, name, outs, args, smem=0, scratch=(), limit_mib=16, micros=1.0
):
    return pl.pallas_call(
        body,
        name=name,
        out_shape=[jax.ShapeDtypeStruct(shape, dtype) for shape, dtype in outs],
        in_specs=[SMEM] * smem + [VMEM] * (len(args) - smem),
        out_specs=[VMEM] * len(outs),
        scratch_shapes=list(scratch),
        compiler_params=pltpu.CompilerParams(vmem_limit_bytes=limit_mib * 1024 * 1024),
        cost_estimate=pl.CostEstimate(
            flops=int(micros * FLOPS_PER_US), bytes_accessed=0, transcendentals=0
        ),
    )(*args)


def per_device(tokens, key_count, norm_gain, qkv_weight, out_weight, logit_scale, grad_out):
    frames, lat_rows, lon_cols, width = tokens.shape
    assert frames == BLOCK and lat_rows == BLOCK and lon_cols == 2 * BLOCK
    assert lax.axis_size("lat") % 2 == 0 and lax.axis_size("lon") % 2 == 0
    cells = frames * lat_rows * lon_cols
    blocks = lon_cols // BLOCK
    head_width = HEADS * HEAD_DIM
    qg_shape = ((blocks, CELLS, PAIR_WIDTH), BF16)
    edge_shape = ((CELLS, PAIR_WIDTH), BF16)
    kv_shape = ((blocks + 1, CELLS, PAIR_WIDTH), BF16)

    start = jnp.where(lax.rem(lax.axis_index("lon"), 2) == 1, lon_cols - BLOCK, 0)
    first = lax.dynamic_slice_in_dim(tokens, start, BLOCK, 2).reshape(CELLS, width)
    first, count = pair_swap(first, "lon", 1), pair_swap(key_count, "lon", 1)
    (order,) = kernel_call(
        functools.partial(order_kernel, lat_rows, lon_cols), "order",
        [((cells, cells), BF16)], [], micros=10.0,
    )
    kv_own, qg_own, kv_other, qg_other, raw, inverse, x = kernel_call(
        project_kernel, "project",
        [qg_shape, qg_shape, qg_shape, qg_shape,
         ((cells, 2 * head_width), F32), ((cells, 2 * head_width), F32), ((cells, width), BF16)],
        [key_count, order, tokens, norm_gain, grad_out, qkv_weight, out_weight],
        smem=1, micros=3.0,
    )
    kv_other, qg_other = pair_swap(kv_other, "lat", 0), pair_swap(qg_other, "lat", 0)
    other_half, half = kernel_call(
        functools.partial(halo_kernel, blocks), "halo", [edge_shape, edge_shape],
        [count, first, norm_gain, qkv_weight], smem=1,
    )
    other_half = pair_swap(other_half, "lat", 0)
    (kv_own,) = kernel_call(join_kernel, "join", [kv_shape], [half, kv_own])
    kv_rows = [kv_own, jnp.concatenate([other_half[None], kv_other], 0)]
    upper = lax.rem(lax.axis_index("lat"), 2) == 1
    wide = lax.axis_size("lat") > 2
    if wide:
        even = jnp.where(upper, kv_rows[1], kv_rows[0])
        odd = jnp.where(upper, kv_rows[0], kv_rows[1])
        kv_rows += [shift_by(odd, "lat", 2), shift_by(even, "lat", -2)]
    rows = len(kv_rows)
    kv_away = []
    for phase in range(2):
        kv_away += [frame_swap(kv, phase) for kv in kv_rows]

    queries = 4 * CELLS
    tables = [((2 * HALF, TILE, queries), BF16), ((2 * HALF, queries, TILE), BF16)]
    sums_shape = ((2 * HALF, 8, queries), F32)

    def kept(groups):
        mid = ((HALF, groups * 2 * CELLS, queries), F32)
        left = ((HALF, groups * CELLS, 2 * CELLS), F32)
        return [mid, mid, left, left]

    def grads_kept(groups):
        return [
            ((HALF, groups * 2 * CELLS, queries), BF16),
            ((HALF, groups * CELLS, 2 * CELLS), BF16),
        ]

    weights, backward, sums, *own_kept = kernel_call(
        functools.partial(own_score_kernel, rows), "own_score",
        tables + [sums_shape] + kept(rows),
        [logit_scale, qg_own, qg_other, *kv_rows], smem=1, micros=1.5,
    )
    siblings = pair_swap(jnp.stack([kv[2] for kv in kv_rows + kv_away], 0), "lon", 0)
    sums, *away_kept = kernel_call(
        functools.partial(away_score_kernel, rows), "away_score",
        [sums_shape] + kept(2 * rows), [logit_scale, weights, sums, *kv_away], smem=1,
        micros=20.0,
    )
    sibling_part, stats, dq_sibling = kernel_call(
        functools.partial(sibling_kernel, rows), "sibling",
        [
            ((3 * rows, CELLS, PAIR_WIDTH), BF16), ((2 * HALF, queries), F32),
            ((HALF_WIDTH, 2 * CELLS), F32),
        ],
        [logit_scale, weights, backward, sums, siblings], smem=1,
    )
    sibling_part = pair_swap(sibling_part, "lon", 0)
    part = (rows, blocks + 1, CELLS, PAIR_WIDTH)
    near, far, *away_grads = kernel_call(
        functools.partial(away_back_kernel, rows), "away_back",
        [(part, F32), (part, F32)] + grads_kept(2 * rows),
        [logit_scale, stats, backward, *away_kept], smem=1, micros=1.5,
    )
    near, far = kernel_call(
        functools.partial(sibling_sum_kernel, rows), "sibling_sum",
        [(part, BF16), (part, BF16)], [near, far, sibling_part],
    )
    near, far = frame_swap(near, 0), frame_swap(far, 1)
    own, dq_own, dq_other = kernel_call(
        functools.partial(own_back_kernel, rows), "own_back",
        [(part, F32), ((CELLS, 2 * HALF_WIDTH), F32), ((CELLS, 2 * HALF_WIDTH), F32)],
        [logit_scale, stats, backward, *own_kept, *away_grads, dq_sibling, sibling_part,
         *kv_rows, *kv_away],
        smem=1, micros=1.5,
        scratch=[pltpu.VMEM(shape, dtype) for shape, dtype in grads_kept(rows)],
    )
    if wide:
        summed = []
        for array in (own, near, far):
            to_odd = shift_by(array[2].astype(BF16), "lat", -2).astype(F32)
            to_even = shift_by(array[3].astype(BF16), "lat", 2).astype(F32)
            added = jnp.stack(
                [jnp.where(upper, to_odd, to_even), jnp.where(upper, to_even, to_odd)], 0
            )
            summed.append((array[:2].astype(F32) + added).astype(array.dtype))
        own, near, far = summed
    inner, to_lat, edge, corner = kernel_call(
        frame_sum_kernel, "frame_sum",
        [((blocks, CELLS, PAIR_WIDTH), F32), ((blocks + 1, CELLS, PAIR_WIDTH), BF16),
         edge_shape, edge_shape],
        [own, near, far, dq_other],
    )
    edge = pair_swap(edge, "lon", 1)
    corner = corner_swap(corner)
    other = pair_swap(to_lat, "lat", 0)
    (grad_tokens,) = kernel_call(
        finish_kernel, "finish", [(tokens.shape, BF16)],
        [inner, dq_own, other, edge, corner, raw, inverse, x, order, norm_gain, qkv_weight],
        micros=2.0,
    )
    return grad_tokens


def solution(mesh):
    in_specs = (
        P("tm", "lat", "lon", None),
        P("tm", "lat", "lon"),
        P(),
        P(),
        P(),
        P(),
        P("tm", "lat", "lon", None),
    )
    out_specs = P("tm", "lat", "lon", None)
    return jax.shard_map(
        per_device, mesh=mesh, in_specs=in_specs, out_specs=out_specs, check_vma=False
    )
```

```python
import functools
import math

import jax
import jax.numpy as jnp
from jax import lax
from jax.experimental import pallas as pl
from jax.experimental.pallas import tpu as pltpu
from jax.sharding import PartitionSpec as P

HEADS = 6
HEAD_DIM = 64
BLOCK = 4
CELLS = BLOCK * BLOCK * BLOCK
HALF = HEADS // 2
HALF_WIDTH = HALF * HEAD_DIM
PAIR_WIDTH = 2 * HALF_WIDTH
TILE = 2 * HEAD_DIM
TILES = PAIR_WIDTH // TILE
DEAD_KEY = 64.0
DROPPED = -1e30
FLOPS_PER_US = 1e9

EPS = 1e-06
F32 = jnp.float32
BF16 = jnp.bfloat16


def partner_of(device, count, phase):
    return device + 1 if device % 2 == phase else device - 1


def pair_swap(array, axis, phase):
    count = lax.axis_size(axis)
    pairs = [(device, partner_of(device, count, phase) % count) for device in range(count)]
    return lax.ppermute(array, axis, pairs)


def frame_swap(array, phase):
    frames, lons = lax.axis_size("tm"), lax.axis_size("lon")
    pairs = []
    for frame in range(frames):
        for lon in range(lons):
            to = (partner_of(frame, frames, phase), lon)
            if not 0 <= to[0] < frames:
                to = (frame, partner_of(lon, lons, 0))
            pairs.append((frame * lons + lon, to[0] * lons + to[1]))
    return lax.ppermute(array, ("tm", "lon"), pairs)


def corner_swap(array):
    lats, lons = lax.axis_size("lat"), lax.axis_size("lon")
    pairs = []
    for lat in range(lats):
        for lon in range(lons):
            to = partner_of(lat, lats, 0) * lons + partner_of(lon, lons, 1) % lons
            pairs.append((lat * lons + lon, to))
    return lax.ppermute(array, ("lat", "lon"), pairs)


def shift_by(array, axis, step):
    count = lax.axis_size(axis)
    pairs = [(i, i + step) for i in range(count) if 0 <= i + step < count]
    return lax.ppermute(array, axis, pairs)


def dot(a, b):
    return lax.dot_general(a, b, (((1,), (0,)), ((), ())), preferred_element_type=F32)


def dot_last(a, b):
    return lax.dot_general(a, b, (((1,), (1,)), ((), ())), preferred_element_type=F32)


def dot_first(a, b):
    return lax.dot_general(a, b, (((0,), (0,)), ((), ())), preferred_element_type=F32)


def head_means(values):
    rows = lax.broadcasted_iota(jnp.int32, (TILE, TILE), 0) // HEAD_DIM
    cols = lax.broadcasted_iota(jnp.int32, (TILE, TILE), 1) // HEAD_DIM
    ones = (rows == cols).astype(F32).astype(BF16)
    high = values.astype(BF16)
    low = (values - high.astype(F32)).astype(BF16)
    pieces = []
    for start in range(0, values.shape[1], TILE):
        cut = slice(start, start + TILE)
        pieces.append(dot(high[:, cut], ones) + dot(low[:, cut], ones))
    return jnp.concatenate(pieces, 1) * (1.0 / HEAD_DIM)


def block_order(lat_rows, lon_cols, count, parity):
    blocks = lon_cols // BLOCK
    row = lax.broadcasted_iota(jnp.int32, (count, count), 0)
    source = lax.broadcasted_iota(jnp.int32, (count, count), 1)
    slot = row // CELLS
    place = row % CELLS
    frame = place // (BLOCK * BLOCK)
    lat = (place // BLOCK) % BLOCK
    col = place % BLOCK
    block = jnp.where(parity == 1, blocks - 1 - slot, slot)
    wanted = (frame * lat_rows + lat) * lon_cols + block * BLOCK + col
    return (source == wanted).astype(F32).astype(BF16)


def halves(first, second):
    low = jnp.concatenate([first[:, :HALF_WIDTH], second[:, :HALF_WIDTH]], 1)
    high = jnp.concatenate([first[:, HALF_WIDTH:], second[:, HALF_WIDTH:]], 1)
    return low, high


def normalised(x, gain_ref):
    inverse = lax.rsqrt(jnp.mean(x * x, -1, keepdims=True) + EPS)
    return (x * inverse * gain_ref[...].reshape(1, x.shape[1])).astype(BF16)


def order_kernel(tokens_ref, order_ref, x_ref):
    frames, lat_rows, lon_cols, width = tokens_ref.shape
    cells = frames * lat_rows * lon_cols
    order = block_order(lat_rows, lon_cols, cells, lax.rem(lax.axis_index("lon"), 2))
    order_ref[...] = order
    x = dot(order, tokens_ref[...].astype(F32).reshape(cells, width).astype(BF16)).astype(BF16)
    x_ref[...] = x


def project_kernel(
    count_ref, scale_in, order_ref, x_ref, gain_ref, grad_ref, qkv_ref, out_weight_ref,
    kv_own_ref, qg_own_ref, kv_other_ref, qg_other_ref, edge_ref, corner_ref,
    raw_ref, inverse_ref, scale_ref,
):
    frames, lat_rows, lon_cols, width = grad_ref.shape
    cells = frames * lat_rows * lon_cols
    blocks = lon_cols // BLOCK
    parity = lax.rem(lax.axis_index("lon"), 2)
    upper = lax.rem(lax.axis_index("lat"), 2) == 1
    all_scales = scale_in[...].reshape(1, HEADS) * (1.0 / math.sqrt(HEAD_DIM))
    for h in range(HALF):
        mine = jnp.where(
            upper, all_scales[:, HALF + h : HALF + h + 1], all_scales[:, h : h + 1]
        )
        scale_ref[h : h + 1] = jnp.broadcast_to(mine, (1, 4 * CELLS))
    counts = count_ref[0]
    order = order_ref[...]
    normed = normalised(x_ref[...].astype(F32), gain_ref)
    query, key, value = (dot(normed, qkv_ref[c]) for c in range(3))
    head_width = HEADS * HEAD_DIM
    raw_ref[:, :head_width] = query
    raw_ref[:, head_width:] = key
    grad = dot_last(
        grad_ref[...].astype(F32).reshape(cells, width).astype(BF16), out_weight_ref[...]
    ).astype(BF16)
    grad = dot(order, grad)
    query_inverse = lax.rsqrt(head_means(query * query) + EPS)
    key_inverse = lax.rsqrt(head_means(key * key) + EPS)
    inverse_ref[:, :head_width] = query_inverse
    inverse_ref[:, head_width:] = key_inverse
    query = query * query_inverse
    key = key * key_inverse
    place = lax.broadcasted_iota(jnp.int32, (CELLS, 1), 0)
    live = []
    for slot in range(blocks):
        flip = blocks - 1 - slot
        live.append(
            place
            < jnp.where(parity == 1, counts[:, flip : flip + 1], counts[:, slot : slot + 1])
        )
    key = jnp.where(jnp.concatenate(live, 0), key, DEAD_KEY)
    shape = (blocks, CELLS, PAIR_WIDTH)
    low, high = halves(key, value)
    kv_own_ref[...] = jnp.where(upper, high, low).astype(BF16).reshape(shape)
    kv_other_ref[...] = jnp.where(upper, low, high).astype(BF16).reshape(shape)
    edge_ref[...] = kv_own_ref[0]
    corner_ref[...] = kv_other_ref[0]
    low, high = halves(query, grad)
    qg_own_ref[...] = jnp.where(upper, high, low).astype(BF16).reshape(shape)
    qg_other_ref[...] = jnp.where(upper, low, high).astype(BF16).reshape(shape)


def lane_tile(j):
    return slice((j // 2) * TILE, (j // 2 + 1) * TILE)


class Place:
    def __init__(self, rows):
        self.rows = rows
        tm, frames = lax.axis_index("tm"), lax.axis_size("tm")
        odd = lax.rem(tm, 2) == 1
        near, far = jnp.where(odd, tm - 1, tm + 1), jnp.where(odd, tm + 1, tm - 1)
        self.there = [None] + [((at >= 0) & (at < frames)) for at in (near, far)]
        self.upper = lax.rem(lax.axis_index("lat"), 2)

    def bias(self, frame, row, lanes):
        there = self.there[frame]
        total = 0.0 if there is None else jnp.where(there, 0.0, DROPPED)
        if row < 2:
            return total
        pair, pairs = lax.axis_index("lat") // 2, lax.axis_size("lat") // 2
        if row == 2:
            inside, wanted = pair > 0, self.upper
        else:
            inside, wanted = pair < pairs - 1, 1 - self.upper
        lane_row = (lax.broadcasted_iota(jnp.int32, (1, lanes), 1) // CELLS) % 2
        seen = (lane_row == wanted) & inside
        return total + jnp.where(seen, 0.0, DROPPED)


def head_scales(scale_ref, lanes):
    return [scale_ref[h : h + 1, lanes] for h in range(HALF)]


def key_bias(keys):
    return jnp.where(keys[:, 0:1].astype(F32) < 0.5 * DEAD_KEY, 0.0, DROPPED)


def score(keys, bias, weights_ref, lanes, scale_ref, sums):
    to_exp2 = [s * math.log2(math.e) for s in head_scales(scale_ref, lanes)]
    count = keys.shape[0]
    exps, probs = [], []
    for h in range(HALF):
        scores = dot(keys[:, lane_tile(h)], weights_ref[h, :, lanes])
        grad_prob = dot(keys[:, lane_tile(HALF + h)], weights_ref[HALF + h, :, lanes])
        masked = jnp.exp2(scores * to_exp2[h] + bias)
        if sums is not None:
            shape = (count // 8, 8, masked.shape[1])
            sums[h] = sums[h] + jnp.sum(masked.reshape(shape), 0)
            inner = (masked * grad_prob).reshape(shape)
            sums[HALF + h] = sums[HALF + h] + jnp.sum(inner, 0)
        exps.append(masked)
        probs.append(grad_prob)
    return exps, probs


ALL = slice(0, 4 * CELLS)
FIRST = slice(0, 2 * CELLS)
LAST = slice(2 * CELLS, 4 * CELLS)


def score_groups(place, frames, kv_refs, weights_ref, scale_ref, sums, e_mid, p_mid, e_left, p_left):
    rows = place.rows
    side = [jnp.zeros((8, 2 * CELLS), F32) for _ in range(2 * HALF)]
    for index, ref in enumerate(kv_refs):
        frame, row = frames[index // rows], index % rows
        keys = ref[1:3].reshape(2 * CELLS, PAIR_WIDTH)
        bias = key_bias(keys) + place.bias(frame, row, 4 * CELLS)
        exps, probs = score(keys, bias, weights_ref, ALL, scale_ref, sums)
        for h in range(HALF):
            e_mid[h, index * 2 * CELLS : (index + 1) * 2 * CELLS] = exps[h]
            p_mid[h, index * 2 * CELLS : (index + 1) * 2 * CELLS] = probs[h]
    for index in range(0, len(kv_refs), 2):
        frame, row = frames[index // rows], index % rows
        pair = [kv_refs[index][0], kv_refs[index + 1][0]]
        bias = jnp.concatenate(
            [
                jnp.broadcast_to(
                    key_bias(keys) + place.bias(frame, row + i, 2 * CELLS), (CELLS, 2 * CELLS)
                )
                for i, keys in enumerate(pair)
            ],
            0,
        )
        keys = jnp.concatenate(pair, 0)
        exps, probs = score(keys, bias, weights_ref, FIRST, scale_ref, side)
        for h in range(HALF):
            e_left[h, index * CELLS : (index + 2) * CELLS] = exps[h]
            p_left[h, index * CELLS : (index + 2) * CELLS] = probs[h]
    return [jnp.concatenate([a[:, FIRST] + b, a[:, LAST]], 1) for a, b in zip(sums, side)]


def query_tables(qg_ref, weights, backward):
    rows = jnp.concatenate([qg_ref[0], qg_ref[2], qg_ref[1], qg_ref[3]], 0).astype(F32)
    cols = rows.T
    count = rows.shape[0]
    lane_half = lax.broadcasted_iota(jnp.int32, (count, TILE), 1) // HEAD_DIM
    row_half = lax.broadcasted_iota(jnp.int32, (TILE, count), 0) // HEAD_DIM
    for j in range(2 * HALF):
        backward[j] = jnp.where(lane_half == j % 2, rows[:, lane_tile(j)], 0.0).astype(BF16)
        weights[j] = jnp.where(row_half == j % 2, cols[lane_tile(j)], 0.0).astype(BF16)


def own_score_kernel(rows, scale_ref, qg_ref, *refs):
    kv_refs, refs = refs[:rows], refs[rows:]
    weights, backward, sums_ref, e_mid, p_mid, e_left, p_left = refs
    queries = 4 * CELLS
    query_tables(qg_ref, weights, backward)
    sums = [jnp.zeros((8, queries), F32) for _ in range(2 * HALF)]
    sums = score_groups(
        Place(rows), (0,), kv_refs, weights, scale_ref, sums,
        e_mid, p_mid, e_left, p_left,
    )
    for j in range(2 * HALF):
        sums_ref[j] = sums[j]


def away_score_kernel(rows, scale_ref, weights, sums_in, *refs):
    kv_refs, refs = refs[: 2 * rows], refs[2 * rows :]
    sums_ref, e_mid, p_mid, e_left, p_left = refs
    sums = [sums_in[j] for j in range(2 * HALF)]
    sums = score_groups(
        Place(rows), (1, 2), kv_refs, weights, scale_ref, sums,
        e_mid, p_mid, e_left, p_left,
    )
    for j in range(2 * HALF):
        sums_ref[j] = sums[j]


def grad_parts(exps, probs, inverse, delta, scales):
    grads, halves_of = [], []
    for h in range(HALF):
        prob = exps[h] * inverse[h]
        halves_of.append(prob.astype(BF16))
        grads.append((prob * (probs[h] - delta[h]) * scales[h]).astype(BF16))
    return grads + halves_of


def key_grads(pieces, backward, lanes):
    outs = []
    for tile in range(TILES):
        both = jnp.concatenate([pieces[2 * tile], pieces[2 * tile + 1]], 1)
        rows = jnp.concatenate(
            [backward[2 * tile, lanes], backward[2 * tile + 1, lanes]], 0
        )
        outs.append(dot(both, rows))
    return jnp.concatenate(outs, 1)


def query_grads(keys, grads, h):
    own = slice((h % 2) * HEAD_DIM, (h % 2 + 1) * HEAD_DIM)
    return dot_first(keys[:, lane_tile(h)], grads)[own]


def side_bias(place, frame, row, keys):
    return jnp.concatenate(
        [
            jnp.broadcast_to(
                key_bias(keys[i]) + place.bias(frame, row + i, 2 * CELLS), (CELLS, 2 * CELLS)
            )
            for i in range(2)
        ],
        0,
    )


def sibling_kernel(
    rows, scale_ref, weights, backward, sums_in, keys_ref, part_ref, stats_ref, dq_ref
):
    place = Place(rows)
    side = [jnp.zeros((8, 2 * CELLS), F32) for _ in range(2 * HALF)]
    made = []
    for index in range(0, 3 * rows, 2):
        bias = side_bias(
            place, index // rows, index % rows, [keys_ref[index], keys_ref[index + 1]]
        )
        keys = keys_ref[index : index + 2].reshape(2 * CELLS, PAIR_WIDTH)
        made.append(score(keys, bias, weights, LAST, scale_ref, side))
    inverse, delta = [], []
    for h in range(HALF):
        total, inner = (
            jnp.concatenate([sums_in[j, :, FIRST], sums_in[j, :, LAST] + side[j]], 1)
            for j in (h, HALF + h)
        )
        inverse.append(1.0 / jnp.sum(total, 0, keepdims=True))
        delta.append(jnp.sum(inner, 0, keepdims=True) * inverse[h])
        stats_ref[h : h + 1] = inverse[h]
        stats_ref[HALF + h : HALF + h + 1] = delta[h]
    inverse = [a[:, LAST] for a in inverse]
    delta = [a[:, LAST] for a in delta]
    scales = head_scales(scale_ref, LAST)
    grads = []
    for index in range(0, 3 * rows, 2):
        pieces = grad_parts(*made[index // 2], inverse, delta, scales)
        grads.append(pieces[:HALF])
        if index < rows:
            part = key_grads(pieces, backward, LAST)
            part_ref[index : index + 2] = part.reshape(2, CELLS, PAIR_WIDTH)
    keys = keys_ref[...].reshape(3 * rows * CELLS, PAIR_WIDTH)
    for h in range(HALF):
        dq_ref[h * HEAD_DIM : (h + 1) * HEAD_DIM] = query_grads(
            keys, jnp.concatenate([g[h] for g in grads], 0), h
        )


def cross_score_kernel(rows, scale_ref, *refs):
    qg_refs, refs = refs[:2], refs[2:]
    kv_refs, sibling_ref, refs = refs[:rows], refs[rows], refs[rows + 1 :]
    backward, e_mid, p_mid, e_side, p_side, weights = refs
    place = Place(rows)
    for side in range(2):
        query_tables(qg_refs[side], weights.at[side], backward.at[side])
    for row in range(rows):
        keys = kv_refs[row][1:3].reshape(2 * CELLS, PAIR_WIDTH)
        bias = key_bias(keys) + place.bias(0, row, 4 * CELLS)
        at = slice(row * 2 * CELLS, (row + 1) * 2 * CELLS)
        for side in range(2):
            exps, probs = score(keys, bias, weights.at[side], ALL, scale_ref, None)
            for h in range(HALF):
                e_mid[side, h, at] = exps[h]
                p_mid[side, h, at] = probs[h]
    for row in range(0, rows, 2):
        at = slice(row * CELLS, (row + 2) * CELLS)
        for edge, lanes in ((0, FIRST), (1, LAST)):
            if edge == 0:
                pair = [kv_refs[row][0], kv_refs[row + 1][0]]
            else:
                pair = [sibling_ref[row], sibling_ref[row + 1]]
            bias = side_bias(place, 0, row, pair)
            keys = jnp.concatenate(pair, 0)
            for side in range(2):
                exps, probs = score(keys, bias, weights.at[side], lanes, scale_ref, None)
                for h in range(HALF):
                    e_side[side, edge, h, at] = exps[h]
                    p_side[side, edge, h, at] = probs[h]


def cross_stats(rows, stats_refs, lanes):
    place = Place(rows)
    both = []
    for side, ref in enumerate(stats_refs):
        there = jnp.where(place.there[1 + side], 1.0, 0.0)
        inverse = [ref[h : h + 1, lanes] * there for h in range(HALF)]
        both.append((inverse, [ref[HALF + h : HALF + h + 1, lanes] for h in range(HALF)]))
    return both


def cross_sibling_kernel(
    rows, scale_ref, near_stats, far_stats, backward, e_side, p_side, part_in, part_ref
):
    scales = head_scales(scale_ref, LAST)
    stats = cross_stats(rows, (near_stats, far_stats), LAST)
    for row in range(0, rows, 2):
        at = slice(row * CELLS, (row + 2) * CELLS)
        total = part_in[row : row + 2].reshape(2 * CELLS, PAIR_WIDTH)
        for side in range(2):
            pieces = grad_parts(
                [e_side[side, 1, h, at] for h in range(HALF)],
                [p_side[side, 1, h, at] for h in range(HALF)],
                *stats[side], scales,
            )
            total = total + key_grads(pieces, backward.at[side], LAST)
        part_ref[row : row + 2] = total.reshape(2, CELLS, PAIR_WIDTH).astype(BF16)


def cross_back_kernel(
    rows, scale_ref, near_stats, far_stats, backward, e_mid, p_mid, e_side, p_side,
    own_ref, total_ref,
):
    scales = head_scales(scale_ref, ALL)
    stats = cross_stats(rows, (near_stats, far_stats), ALL)
    for row in range(rows):
        at = slice(row * 2 * CELLS, (row + 1) * 2 * CELLS)
        total = own_ref[row, 1:3].reshape(2 * CELLS, PAIR_WIDTH)
        for side in range(2):
            pieces = grad_parts(
                [e_mid[side, h, at] for h in range(HALF)],
                [p_mid[side, h, at] for h in range(HALF)],
                *stats[side], scales,
            )
            total = total + key_grads(pieces, backward.at[side], ALL)
        total_ref[row, 1:3] = total.reshape(2, CELLS, PAIR_WIDTH)
    scales = head_scales(scale_ref, FIRST)
    stats = cross_stats(rows, (near_stats, far_stats), FIRST)
    for row in range(0, rows, 2):
        at = slice(row * CELLS, (row + 2) * CELLS)
        total = own_ref[row : row + 2, 0].reshape(2 * CELLS, PAIR_WIDTH)
        for side in range(2):
            pieces = grad_parts(
                [e_side[side, 0, h, at] for h in range(HALF)],
                [p_side[side, 0, h, at] for h in range(HALF)],
                *stats[side], scales,
            )
            total = total + key_grads(pieces, backward.at[side], FIRST)
        total_ref[row : row + 2, 0] = total.reshape(2, CELLS, PAIR_WIDTH)


def own_back_kernel(
    rows, scale_ref, stats_ref, backward, e_mid, p_mid, e_left, p_left,
    away_e_mid, away_p_mid, away_e_left, away_p_left, dq_sibling, *refs,
):
    kv_refs, refs = refs[: 3 * rows], refs[3 * rows :]
    own_ref, dq_own_ref, dq_other_ref, d_mid, d_left = refs
    scales = head_scales(scale_ref, ALL)
    inverse = [stats_ref[h : h + 1] for h in range(HALF)]
    delta = [stats_ref[HALF + h : HALF + h + 1] for h in range(HALF)]
    for index in range(3 * rows):
        at = slice(index * 2 * CELLS, (index + 1) * 2 * CELLS)
        if index < rows:
            exps, probs, start = e_mid, p_mid, index * 2 * CELLS
        else:
            exps, probs, start = away_e_mid, away_p_mid, (index - rows) * 2 * CELLS
        cut = slice(start, start + 2 * CELLS)
        pieces = grad_parts(
            [exps[h, cut] for h in range(HALF)], [probs[h, cut] for h in range(HALF)],
            inverse, delta, scales,
        )
        for h in range(HALF):
            d_mid[h, at] = pieces[h]
        if index < rows:
            part = key_grads(pieces, backward, ALL)
            own_ref[index, 1:3] = part.reshape(2, CELLS, PAIR_WIDTH)
    scales = head_scales(scale_ref, FIRST)
    inverse = [a[:, FIRST] for a in inverse]
    delta = [a[:, FIRST] for a in delta]
    for index in range(0, 3 * rows, 2):
        at = slice(index * CELLS, (index + 2) * CELLS)
        if index < rows:
            exps, probs, start = e_left, p_left, index * CELLS
        else:
            exps, probs, start = away_e_left, away_p_left, (index - rows) * CELLS
        cut = slice(start, start + 2 * CELLS)
        pieces = grad_parts(
            [exps[h, cut] for h in range(HALF)], [probs[h, cut] for h in range(HALF)],
            inverse, delta, scales,
        )
        for h in range(HALF):
            d_left[h, at] = pieces[h]
        if index < rows:
            part = key_grads(pieces, backward, FIRST)
            own_ref[index : index + 2, 0] = part.reshape(2, CELLS, PAIR_WIDTH)
    mid = jnp.concatenate([ref[1:3].reshape(2 * CELLS, PAIR_WIDTH) for ref in kv_refs], 0)
    left = jnp.concatenate([ref[0] for ref in kv_refs], 0)
    columns = []
    for h in range(HALF):
        made = query_grads(mid, d_mid[h], h)
        first = query_grads(left, d_left[h], h)
        last = dq_sibling[h * HEAD_DIM : (h + 1) * HEAD_DIM]
        columns.append(made + jnp.concatenate([first, last], 1))
    dq = jnp.concatenate(columns, 0).T
    dq_own_ref[...] = jnp.concatenate([dq[:CELLS], dq[2 * CELLS : 3 * CELLS]], 1)
    dq_other_ref[...] = jnp.concatenate([dq[CELLS : 2 * CELLS], dq[3 * CELLS :]], 1).astype(BF16)


def column_out_kernel(total_ref, sibling_ref, dq_other_ref, inner_ref, to_lat_ref, edge_ref, corner_ref):
    inner_ref[0] = total_ref[0, 1]
    inner_ref[1] = total_ref[0, 2] + sibling_ref[0].astype(F32)
    to_lat_ref[0] = total_ref[1, 1].astype(BF16)
    to_lat_ref[2] = dq_other_ref[...]
    to_lat_ref[1] = (total_ref[1, 2] + sibling_ref[1].astype(F32)).astype(BF16)
    edge_ref[...] = total_ref[0, 0].astype(BF16)
    corner_ref[...] = total_ref[1, 0].astype(BF16)


def finish_kernel(
    inner_ref, dq_ref, other_ref, edge_ref, corner_ref,
    raw_ref, inverse_ref, x_ref, order_ref, gain_ref, qkv_ref, out_ref,
):
    frames, lat_rows, lon_cols, width = out_ref.shape
    cells = frames * lat_rows * lon_cols
    parity = lax.rem(lax.axis_index("lon"), 2)
    upper = lax.rem(lax.axis_index("lat"), 2) == 1

    def joined(mine, theirs):
        return jnp.where(
            upper, jnp.concatenate([theirs, mine], 1), jnp.concatenate([mine, theirs], 1)
        )

    def by_slot(packed):
        return jnp.concatenate([packed[:, :HALF_WIDTH], packed[:, HALF_WIDTH:]], 0)

    def with_edge(inner, edge):
        return jnp.concatenate([inner[0] + edge.astype(F32), inner[1]], 0)

    dkv_mine = with_edge(inner_ref[...], edge_ref[...])
    dkv_theirs = with_edge(other_ref[:2].astype(F32), corner_ref[...])
    grads = [
        joined(by_slot(dq_ref[...]), by_slot(other_ref[2].astype(F32))),
        joined(dkv_mine[:, :HALF_WIDTH], dkv_theirs[:, :HALF_WIDTH]),
        joined(dkv_mine[:, HALF_WIDTH:], dkv_theirs[:, HALF_WIDTH:]),
    ]
    head_width = HEADS * HEAD_DIM
    grad_normed = dot_last(grads[2].astype(BF16), qkv_ref[2])
    for c in range(2):
        raw = raw_ref[:, c * head_width : (c + 1) * head_width]
        inverse = inverse_ref[:, c * head_width : (c + 1) * head_width]
        inner = head_means(raw * grads[c])
        grad_raw = inverse * grads[c] - inverse * inverse * inverse * raw * inner
        grad_normed = grad_normed + dot_last(grad_raw.astype(BF16), qkv_ref[c])
    order = order_ref[...]
    x = x_ref[...].astype(F32)
    inverse = lax.rsqrt(jnp.mean(x * x, -1, keepdims=True) + EPS)
    grad = gain_ref[...].reshape(1, width) * grad_normed
    inner = jnp.mean(x * grad, -1, keepdims=True)
    grad = (inverse * grad - inverse * inverse * inverse * x * inner).astype(BF16)
    grad = dot_first(order, grad)
    out_ref[...] = grad.reshape(out_ref.shape).astype(BF16)


VMEM = pl.BlockSpec(memory_space=pltpu.VMEM)


def kernel_call(
    body, name, outs, args, scratch=(), limit_mib=16, micros=1.0
):
    return pl.pallas_call(
        body,
        name=name,
        out_shape=[jax.ShapeDtypeStruct(shape, dtype) for shape, dtype in outs],
        in_specs=[VMEM] * len(args),
        out_specs=[VMEM] * len(outs),
        scratch_shapes=list(scratch),
        compiler_params=pltpu.CompilerParams(vmem_limit_bytes=limit_mib * 1024 * 1024),
        cost_estimate=pl.CostEstimate(
            flops=int(micros * FLOPS_PER_US), bytes_accessed=0, transcendentals=0
        ),
    )(*args)


def per_device(tokens, key_count, norm_gain, qkv_weight, out_weight, logit_scale, grad_out):
    frames, lat_rows, lon_cols, width = tokens.shape
    assert frames == BLOCK and lat_rows == BLOCK and lon_cols == 2 * BLOCK
    assert lax.axis_size("lat") % 2 == 0 and lax.axis_size("lon") % 2 == 0
    cells = frames * lat_rows * lon_cols
    blocks = lon_cols // BLOCK
    head_width = HEADS * HEAD_DIM
    qg_shape = ((blocks, CELLS, PAIR_WIDTH), BF16)
    edge_shape = ((CELLS, PAIR_WIDTH), BF16)

    order, x = kernel_call(
        order_kernel, "order", [((cells, cells), BF16), ((cells, width), BF16)], [tokens],
        micros=10.0,
    )
    kv_own, qg_own, kv_other, qg_other, edge, corner, raw, inverse, scales = kernel_call(
        project_kernel, "project",
        [qg_shape, qg_shape, qg_shape, qg_shape, edge_shape, edge_shape, ((cells, 2 * head_width), F32), ((cells, 2 * head_width), F32),
         ((HALF, 4 * CELLS), F32)],
        [key_count, logit_scale, order, x, norm_gain, grad_out, qkv_weight, out_weight],
        micros=40.0,
    )
    edge = pair_swap(edge, "lon", 1)
    corner = corner_swap(corner)
    kv_other = pair_swap(kv_other, "lat", 0)
    kv_rows = [
        jnp.concatenate([edge[None], kv_own], 0),
        jnp.concatenate([corner[None], kv_other], 0),
    ]
    qg_other, kv_other = lax.optimization_barrier((qg_other, kv_other))
    qg_other = pair_swap(qg_other, "lat", 0)
    upper = lax.rem(lax.axis_index("lat"), 2) == 1
    wide = lax.axis_size("lat") > 2
    if wide:
        even = jnp.where(upper, kv_rows[1], kv_rows[0])
        odd = jnp.where(upper, kv_rows[0], kv_rows[1])
        kv_rows += [shift_by(odd, "lat", 2), shift_by(even, "lat", -2)]
    rows = len(kv_rows)
    kv_away = [frame_swap(kv, phase) for phase in range(2) for kv in kv_rows]
    qg_both = jnp.concatenate([qg_own, qg_other], 0)
    qg_away = [frame_swap(qg_both, phase) for phase in range(2)]

    queries = 4 * CELLS
    tables = [((2 * HALF, TILE, queries), BF16), ((2 * HALF, queries, TILE), BF16)]
    sums_shape = ((2 * HALF, 8, queries), F32)

    def kept(groups):
        mid = ((HALF, groups * 2 * CELLS, queries), F32)
        left = ((HALF, groups * CELLS, 2 * CELLS), F32)
        return [mid, mid, left, left]

    weights, backward, sums, *own_kept = kernel_call(
        functools.partial(own_score_kernel, rows), "own_score",
        tables + [sums_shape] + kept(rows),
        [scales, qg_both, *kv_rows], micros=1.5,
    )
    siblings = jnp.stack([kv[2] for kv in kv_rows + kv_away], 0)
    siblings = pair_swap(siblings, "lon", 0)
    sums, *away_kept = kernel_call(
        functools.partial(away_score_kernel, rows), "away_score",
        [sums_shape] + kept(2 * rows), [scales, weights, sums, *kv_away],
        micros=20.0,
    )
    half_part = (rows, CELLS, PAIR_WIDTH)
    sibling_part, stats, dq_sibling = kernel_call(
        functools.partial(sibling_kernel, rows), "sibling",
        [(half_part, F32), ((2 * HALF, queries), F32), ((HALF_WIDTH, 2 * CELLS), F32)],
        [scales, weights, backward, sums, siblings], micros=1.5,
    )
    near_stats, far_stats = frame_swap(stats, 0), frame_swap(stats, 1)
    cross_mid = ((2, HALF, rows * 2 * CELLS, queries), F32)
    cross_side = ((2, 2, HALF, rows * CELLS, 2 * CELLS), F32)
    cross_backward, e_mid, p_mid, e_side, p_side = kernel_call(
        functools.partial(cross_score_kernel, rows), "cross_score",
        [((2,) + tables[1][0], BF16), cross_mid, cross_mid, cross_side, cross_side],
        [scales, *qg_away, *kv_rows, siblings], micros=2.0,
        scratch=[pltpu.VMEM((2,) + tables[0][0], BF16)],
    )
    part = (rows, blocks + 1, CELLS, PAIR_WIDTH)
    packed = (CELLS, 2 * HALF_WIDTH)
    own_part, dq_own, dq_other = kernel_call(
        functools.partial(own_back_kernel, rows), "own_back",
        [(part, F32), (packed, F32), (packed, BF16)],
        [scales, stats, backward, *own_kept, *away_kept, dq_sibling, *kv_rows, *kv_away],
        micros=2.0,
        scratch=[
            pltpu.VMEM((HALF, 3 * rows * 2 * CELLS, queries), BF16),
            pltpu.VMEM((HALF, 3 * rows * CELLS, 2 * CELLS), BF16),
        ],
    )
    (sibling_part,) = kernel_call(
        functools.partial(cross_sibling_kernel, rows), "cross_sibling", [(half_part, BF16)],
        [scales, near_stats, far_stats, cross_backward, e_side, p_side, sibling_part],
        micros=0.5,
    )
    sibling_part = pair_swap(sibling_part, "lon", 0)
    (total,) = kernel_call(
        functools.partial(cross_back_kernel, rows), "cross_back", [(part, F32)],
        [scales, near_stats, far_stats, cross_backward, e_mid, p_mid, e_side, p_side,
         own_part],
        micros=1.5,
    )
    if wide:
        total = total.at[:, blocks].add(sibling_part.astype(F32))
        sibling_part = jnp.zeros_like(sibling_part)
        to_odd = shift_by(total[2].astype(BF16), "lat", -2).astype(F32)
        to_even = shift_by(total[3].astype(BF16), "lat", 2).astype(F32)
        total = total[:2] + jnp.stack(
            [jnp.where(upper, to_odd, to_even), jnp.where(upper, to_even, to_odd)], 0
        )
    inner, to_lat, edge, corner = kernel_call(
        column_out_kernel, "column_out",
        [((blocks, CELLS, PAIR_WIDTH), F32), ((blocks + 1, CELLS, PAIR_WIDTH), BF16),
         edge_shape, edge_shape],
        [total, sibling_part, dq_other],
    )
    edge = pair_swap(edge, "lon", 1)
    corner = corner_swap(corner)
    other = pair_swap(to_lat, "lat", 0)
    (grad_tokens,) = kernel_call(
        finish_kernel, "finish", [(tokens.shape, BF16)],
        [inner, dq_own, other, edge, corner, raw, inverse, x, order, norm_gain, qkv_weight],
        micros=2.0,
    )
    return grad_tokens


def solution(mesh):
    in_specs = (
        P("tm", "lat", "lon", None),
        P("tm", "lat", "lon"),
        P(),
        P(),
        P(),
        P(),
        P("tm", "lat", "lon", None),
    )
    out_specs = P("tm", "lat", "lon", None)
    return jax.shard_map(
        per_device, mesh=mesh, in_specs=in_specs, out_specs=out_specs, check_vma=False
    )
```

```python
import functools
import math

import jax
import jax.numpy as jnp
from jax import lax
from jax.experimental import pallas as pl
from jax.experimental.pallas import tpu as pltpu
from jax.sharding import PartitionSpec as P

HEADS = 6
HEAD_DIM = 64
BLOCK = 4
CELLS = BLOCK * BLOCK * BLOCK
HALF = HEADS // 2
HALF_WIDTH = HALF * HEAD_DIM
PAIR_WIDTH = 2 * HALF_WIDTH
TILE = 2 * HEAD_DIM
TILES = PAIR_WIDTH // TILE
DEAD_KEY = 64.0
DROPPED = -1e30
FLOPS_PER_US = 1e9

EPS = 1e-06
F32 = jnp.float32
BF16 = jnp.bfloat16


def partner_of(device, count, phase):
    return device + 1 if device % 2 == phase else device - 1


def pair_swap(array, axis, phase):
    count = lax.axis_size(axis)
    pairs = [(device, partner_of(device, count, phase) % count) for device in range(count)]
    return lax.ppermute(array, axis, pairs)


def frame_swap(array, phase):
    frames, lons = lax.axis_size("tm"), lax.axis_size("lon")
    pairs = []
    for frame in range(frames):
        for lon in range(lons):
            to = (partner_of(frame, frames, phase), lon)
            if not 0 <= to[0] < frames:
                to = (frame, partner_of(lon, lons, 0))
            pairs.append((frame * lons + lon, to[0] * lons + to[1]))
    return lax.ppermute(array, ("tm", "lon"), pairs)


def corner_swap(array):
    lats, lons = lax.axis_size("lat"), lax.axis_size("lon")
    pairs = []
    for lat in range(lats):
        for lon in range(lons):
            to = partner_of(lat, lats, 0) * lons + partner_of(lon, lons, 1) % lons
            pairs.append((lat * lons + lon, to))
    return lax.ppermute(array, ("lat", "lon"), pairs)


def shift_by(array, axis, step):
    count = lax.axis_size(axis)
    pairs = [(i, i + step) for i in range(count) if 0 <= i + step < count]
    return lax.ppermute(array, axis, pairs)


def dot(a, b):
    return lax.dot_general(a, b, (((1,), (0,)), ((), ())), preferred_element_type=F32)


def dot_last(a, b):
    return lax.dot_general(a, b, (((1,), (1,)), ((), ())), preferred_element_type=F32)


def dot_first(a, b):
    return lax.dot_general(a, b, (((0,), (0,)), ((), ())), preferred_element_type=F32)


def head_means(values):
    rows = lax.broadcasted_iota(jnp.int32, (TILE, TILE), 0) // HEAD_DIM
    cols = lax.broadcasted_iota(jnp.int32, (TILE, TILE), 1) // HEAD_DIM
    ones = (rows == cols).astype(F32).astype(BF16)
    high = values.astype(BF16)
    low = (values - high.astype(F32)).astype(BF16)
    pieces = []
    for start in range(0, values.shape[1], TILE):
        cut = slice(start, start + TILE)
        pieces.append(dot(high[:, cut], ones) + dot(low[:, cut], ones))
    return jnp.concatenate(pieces, 1) * (1.0 / HEAD_DIM)


def block_order(lat_rows, lon_cols, count, parity):
    blocks = lon_cols // BLOCK
    row = lax.broadcasted_iota(jnp.int32, (count, count), 0)
    source = lax.broadcasted_iota(jnp.int32, (count, count), 1)
    slot = row // CELLS
    place = row % CELLS
    frame = place // (BLOCK * BLOCK)
    lat = (place // BLOCK) % BLOCK
    col = place % BLOCK
    block = jnp.where(parity == 1, blocks - 1 - slot, slot)
    wanted = (frame * lat_rows + lat) * lon_cols + block * BLOCK + col
    return (source == wanted).astype(F32).astype(BF16)


def halves(first, second):
    low = jnp.concatenate([first[:, :HALF_WIDTH], second[:, :HALF_WIDTH]], 1)
    high = jnp.concatenate([first[:, HALF_WIDTH:], second[:, HALF_WIDTH:]], 1)
    return low, high


def normalised(x, gain_ref):
    inverse = lax.rsqrt(jnp.mean(x * x, -1, keepdims=True) + EPS)
    return (x * inverse * gain_ref[...].reshape(1, x.shape[1])).astype(BF16)


def order_kernel(tokens_ref, order_ref, x_ref):
    frames, lat_rows, lon_cols, width = tokens_ref.shape
    cells = frames * lat_rows * lon_cols
    order = block_order(lat_rows, lon_cols, cells, lax.rem(lax.axis_index("lon"), 2))
    order_ref[...] = order
    x = dot(order, tokens_ref[...].astype(F32).reshape(cells, width).astype(BF16)).astype(BF16)
    x_ref[...] = x


def key_value_kernel(
    count_ref, x_ref, gain_ref, qkv_ref,
    kv_own_ref, kv_other_ref, edge_ref, corner_ref, normed_ref, raw_ref, inverse_ref,
):
    cells = x_ref.shape[0]
    blocks = cells // CELLS
    parity = lax.rem(lax.axis_index("lon"), 2)
    upper = lax.rem(lax.axis_index("lat"), 2) == 1
    normed = normalised(x_ref[...].astype(F32), gain_ref)
    normed_ref[...] = normed
    key, value = dot(normed, qkv_ref[1]), dot(normed, qkv_ref[2])
    raw_ref[...] = key
    inverse = lax.rsqrt(head_means(key * key) + EPS)
    inverse_ref[...] = inverse
    place = lax.broadcasted_iota(jnp.int32, (CELLS, 1), 0)
    counts = count_ref[0]
    live = []
    for slot in range(blocks):
        flip = blocks - 1 - slot
        live.append(
            place
            < jnp.where(parity == 1, counts[:, flip : flip + 1], counts[:, slot : slot + 1])
        )
    key = jnp.where(jnp.concatenate(live, 0), key * inverse, DEAD_KEY)
    shape = (blocks, CELLS, PAIR_WIDTH)
    low, high = halves(key, value)
    kv_own_ref[...] = jnp.where(upper, high, low).astype(BF16).reshape(shape)
    kv_other_ref[...] = jnp.where(upper, low, high).astype(BF16).reshape(shape)
    edge_ref[...] = kv_own_ref[0]
    corner_ref[...] = kv_other_ref[0]


def query_grad_kernel(
    scale_in, order_ref, normed_ref, grad_ref, qkv_ref, out_weight_ref,
    qg_own_ref, qg_other_ref, raw_ref, inverse_ref, scale_ref,
):
    cells, width = normed_ref.shape
    upper = lax.rem(lax.axis_index("lat"), 2) == 1
    all_scales = scale_in[...].reshape(1, HEADS) * (1.0 / math.sqrt(HEAD_DIM))
    for h in range(HALF):
        mine = jnp.where(
            upper, all_scales[:, HALF + h : HALF + h + 1], all_scales[:, h : h + 1]
        )
        scale_ref[h : h + 1] = jnp.broadcast_to(mine, (1, 4 * CELLS))
    query = dot(normed_ref[...], qkv_ref[0])
    raw_ref[...] = query
    inverse = lax.rsqrt(head_means(query * query) + EPS)
    inverse_ref[...] = inverse
    grad = dot_last(
        grad_ref[...].astype(F32).reshape(cells, width).astype(BF16), out_weight_ref[...]
    ).astype(BF16)
    low, high = halves(query * inverse, dot(order_ref[...], grad))
    shape = (cells // CELLS, CELLS, PAIR_WIDTH)
    qg_own_ref[...] = jnp.where(upper, high, low).astype(BF16).reshape(shape)
    qg_other_ref[...] = jnp.where(upper, low, high).astype(BF16).reshape(shape)


def join_kernel(kv_in, kv_ref):
    kv_ref[...] = kv_in[...]


def lane_tile(j):
    return slice((j // 2) * TILE, (j // 2 + 1) * TILE)


class Place:
    def __init__(self, rows):
        self.rows = rows
        tm, frames = lax.axis_index("tm"), lax.axis_size("tm")
        odd = lax.rem(tm, 2) == 1
        near, far = jnp.where(odd, tm - 1, tm + 1), jnp.where(odd, tm + 1, tm - 1)
        self.there = [None] + [((at >= 0) & (at < frames)) for at in (near, far)]
        self.upper = lax.rem(lax.axis_index("lat"), 2)

    def bias(self, frame, row, lanes):
        there = self.there[frame]
        total = 0.0 if there is None else jnp.where(there, 0.0, DROPPED)
        if row < 2:
            return total
        pair, pairs = lax.axis_index("lat") // 2, lax.axis_size("lat") // 2
        if row == 2:
            inside, wanted = pair > 0, self.upper
        else:
            inside, wanted = pair < pairs - 1, 1 - self.upper
        lane_row = (lax.broadcasted_iota(jnp.int32, (1, lanes), 1) // CELLS) % 2
        seen = (lane_row == wanted) & inside
        return total + jnp.where(seen, 0.0, DROPPED)


def head_scales(scale_ref, lanes):
    return [scale_ref[h : h + 1, lanes] for h in range(HALF)]


def key_bias(keys):
    return jnp.where(keys[:, 0:1].astype(F32) < 0.5 * DEAD_KEY, 0.0, DROPPED)


def score(keys, bias, weights_ref, lanes, scale_ref, sums):
    to_exp2 = [s * math.log2(math.e) for s in head_scales(scale_ref, lanes)]
    count = keys.shape[0]
    exps, probs = [], []
    for h in range(HALF):
        scores = dot(keys[:, lane_tile(h)], weights_ref[h, :, lanes])
        grad_prob = dot(keys[:, lane_tile(HALF + h)], weights_ref[HALF + h, :, lanes])
        masked = jnp.exp2(scores * to_exp2[h] + bias)
        if sums is not None:
            shape = (count // 8, 8, masked.shape[1])
            sums[h] = sums[h] + jnp.sum(masked.reshape(shape), 0)
            inner = (masked * grad_prob).reshape(shape)
            sums[HALF + h] = sums[HALF + h] + jnp.sum(inner, 0)
        exps.append(masked)
        probs.append(grad_prob)
    return exps, probs


ALL = slice(0, 4 * CELLS)
FIRST = slice(0, 2 * CELLS)
LAST = slice(2 * CELLS, 4 * CELLS)


def score_groups(place, frames, kv_refs, weights_ref, scale_ref, sums, e_mid, p_mid, e_left, p_left):
    rows = place.rows
    side = [jnp.zeros((8, 2 * CELLS), F32) for _ in range(2 * HALF)]
    for index, ref in enumerate(kv_refs):
        frame, row = frames[index // rows], index % rows
        keys = ref[1:3].reshape(2 * CELLS, PAIR_WIDTH)
        bias = key_bias(keys) + place.bias(frame, row, 4 * CELLS)
        exps, probs = score(keys, bias, weights_ref, ALL, scale_ref, sums)
        for h in range(HALF):
            e_mid[h, index * 2 * CELLS : (index + 1) * 2 * CELLS] = exps[h]
            p_mid[h, index * 2 * CELLS : (index + 1) * 2 * CELLS] = probs[h]
    for index in range(0, len(kv_refs), 2):
        frame, row = frames[index // rows], index % rows
        pair = [kv_refs[index][0], kv_refs[index + 1][0]]
        bias = jnp.concatenate(
            [
                jnp.broadcast_to(
                    key_bias(keys) + place.bias(frame, row + i, 2 * CELLS), (CELLS, 2 * CELLS)
                )
                for i, keys in enumerate(pair)
            ],
            0,
        )
        keys = jnp.concatenate(pair, 0)
        exps, probs = score(keys, bias, weights_ref, FIRST, scale_ref, side)
        for h in range(HALF):
            e_left[h, index * CELLS : (index + 2) * CELLS] = exps[h]
            p_left[h, index * CELLS : (index + 2) * CELLS] = probs[h]
    return [jnp.concatenate([a[:, FIRST] + b, a[:, LAST]], 1) for a, b in zip(sums, side)]


def query_tables(qg_ref, weights, backward):
    rows = jnp.concatenate([qg_ref[0], qg_ref[2], qg_ref[1], qg_ref[3]], 0).astype(F32)
    cols = rows.T
    count = rows.shape[0]
    lane_half = lax.broadcasted_iota(jnp.int32, (count, TILE), 1) // HEAD_DIM
    row_half = lax.broadcasted_iota(jnp.int32, (TILE, count), 0) // HEAD_DIM
    for j in range(2 * HALF):
        backward[j] = jnp.where(lane_half == j % 2, rows[:, lane_tile(j)], 0.0).astype(BF16)
        weights[j] = jnp.where(row_half == j % 2, cols[lane_tile(j)], 0.0).astype(BF16)


def own_score_kernel(rows, scale_ref, qg_ref, *refs):
    kv_refs, refs = refs[:rows], refs[rows:]
    weights, backward, sums_ref, e_mid, p_mid, e_left, p_left = refs
    queries = 4 * CELLS
    query_tables(qg_ref, weights, backward)
    sums = [jnp.zeros((8, queries), F32) for _ in range(2 * HALF)]
    sums = score_groups(
        Place(rows), (0,), kv_refs, weights, scale_ref, sums,
        e_mid, p_mid, e_left, p_left,
    )
    for j in range(2 * HALF):
        sums_ref[j] = sums[j]


def away_score_kernel(rows, scale_ref, weights, sums_in, *refs):
    kv_refs, refs = refs[: 2 * rows], refs[2 * rows :]
    sums_ref, e_mid, p_mid, e_left, p_left = refs
    sums = [sums_in[j] for j in range(2 * HALF)]
    sums = score_groups(
        Place(rows), (1, 2), kv_refs, weights, scale_ref, sums,
        e_mid, p_mid, e_left, p_left,
    )
    for j in range(2 * HALF):
        sums_ref[j] = sums[j]


def grad_parts(exps, probs, inverse, delta, scales):
    grads, halves_of = [], []
    for h in range(HALF):
        prob = exps[h] * inverse[h]
        halves_of.append(prob.astype(BF16))
        grads.append((prob * (probs[h] - delta[h]) * scales[h]).astype(BF16))
    return grads + halves_of


def key_grads(pieces, backward, lanes):
    outs = []
    for tile in range(TILES):
        both = jnp.concatenate([pieces[2 * tile], pieces[2 * tile + 1]], 1)
        rows = jnp.concatenate(
            [backward[2 * tile, lanes], backward[2 * tile + 1, lanes]], 0
        )
        outs.append(dot(both, rows))
    return jnp.concatenate(outs, 1)


def query_grads(keys, grads, h):
    own = slice((h % 2) * HEAD_DIM, (h % 2 + 1) * HEAD_DIM)
    return dot_first(keys[:, lane_tile(h)], grads)[own]


def side_bias(place, frame, row, keys):
    return jnp.concatenate(
        [
            jnp.broadcast_to(
                key_bias(keys[i]) + place.bias(frame, row + i, 2 * CELLS), (CELLS, 2 * CELLS)
            )
            for i in range(2)
        ],
        0,
    )


def sibling_kernel(
    rows, scale_ref, weights, backward, sums_in, keys_ref, part_ref, stats_ref, dq_ref
):
    place = Place(rows)
    side = [jnp.zeros((8, 2 * CELLS), F32) for _ in range(2 * HALF)]
    made = []
    for index in range(0, 3 * rows, 2):
        bias = side_bias(
            place, index // rows, index % rows, [keys_ref[index], keys_ref[index + 1]]
        )
        keys = keys_ref[index : index + 2].reshape(2 * CELLS, PAIR_WIDTH)
        made.append(score(keys, bias, weights, LAST, scale_ref, side))
    inverse, delta = [], []
    for h in range(HALF):
        total, inner = (
            jnp.concatenate([sums_in[j, :, FIRST], sums_in[j, :, LAST] + side[j]], 1)
            for j in (h, HALF + h)
        )
        inverse.append(1.0 / jnp.sum(total, 0, keepdims=True))
        delta.append(jnp.sum(inner, 0, keepdims=True) * inverse[h])
        stats_ref[h : h + 1] = inverse[h]
        stats_ref[HALF + h : HALF + h + 1] = delta[h]
    inverse = [a[:, LAST] for a in inverse]
    delta = [a[:, LAST] for a in delta]
    scales = head_scales(scale_ref, LAST)
    grads = []
    for index in range(0, 3 * rows, 2):
        pieces = grad_parts(*made[index // 2], inverse, delta, scales)
        grads.append(pieces[:HALF])
        if index < rows:
            part = key_grads(pieces, backward, LAST)
            part_ref[index : index + 2] = part.reshape(2, CELLS, PAIR_WIDTH)
    keys = keys_ref[...].reshape(3 * rows * CELLS, PAIR_WIDTH)
    for h in range(HALF):
        dq_ref[h * HEAD_DIM : (h + 1) * HEAD_DIM] = query_grads(
            keys, jnp.concatenate([g[h] for g in grads], 0), h
        )


def cross_score_kernel(rows, scale_ref, *refs):
    qg_refs, refs = refs[:2], refs[2:]
    kv_refs, sibling_ref, refs = refs[:rows], refs[rows], refs[rows + 1 :]
    backward, e_mid, p_mid, e_side, p_side, weights = refs
    place = Place(rows)
    for side in range(2):
        query_tables(qg_refs[side], weights.at[side], backward.at[side])
    for row in range(rows):
        keys = kv_refs[row][1:3].reshape(2 * CELLS, PAIR_WIDTH)
        bias = key_bias(keys) + place.bias(0, row, 4 * CELLS)
        at = slice(row * 2 * CELLS, (row + 1) * 2 * CELLS)
        for side in range(2):
            exps, probs = score(keys, bias, weights.at[side], ALL, scale_ref, None)
            for h in range(HALF):
                e_mid[side, h, at] = exps[h]
                p_mid[side, h, at] = probs[h]
    for row in range(0, rows, 2):
        at = slice(row * CELLS, (row + 2) * CELLS)
        for edge, lanes in ((0, FIRST), (1, LAST)):
            if edge == 0:
                pair = [kv_refs[row][0], kv_refs[row + 1][0]]
            else:
                pair = [sibling_ref[row], sibling_ref[row + 1]]
            bias = side_bias(place, 0, row, pair)
            keys = jnp.concatenate(pair, 0)
            for side in range(2):
                exps, probs = score(keys, bias, weights.at[side], lanes, scale_ref, None)
                for h in range(HALF):
                    e_side[side, edge, h, at] = exps[h]
                    p_side[side, edge, h, at] = probs[h]


def cross_stats(rows, stats_refs, lanes):
    place = Place(rows)
    both = []
    for side, ref in enumerate(stats_refs):
        there = jnp.where(place.there[1 + side], 1.0, 0.0)
        inverse = [ref[h : h + 1, lanes] * there for h in range(HALF)]
        both.append((inverse, [ref[HALF + h : HALF + h + 1, lanes] for h in range(HALF)]))
    return both


def cross_sibling_kernel(
    rows, scale_ref, near_stats, far_stats, backward, e_side, p_side, part_in, part_ref
):
    scales = head_scales(scale_ref, LAST)
    stats = cross_stats(rows, (near_stats, far_stats), LAST)
    for row in range(0, rows, 2):
        at = slice(row * CELLS, (row + 2) * CELLS)
        total = part_in[row : row + 2].reshape(2 * CELLS, PAIR_WIDTH)
        for side in range(2):
            pieces = grad_parts(
                [e_side[side, 1, h, at] for h in range(HALF)],
                [p_side[side, 1, h, at] for h in range(HALF)],
                *stats[side], scales,
            )
            total = total + key_grads(pieces, backward.at[side], LAST)
        part_ref[row : row + 2] = total.reshape(2, CELLS, PAIR_WIDTH).astype(BF16)


def cross_back_kernel(
    rows, scale_ref, near_stats, far_stats, backward, e_mid, p_mid, e_side, p_side,
    own_ref, total_ref,
):
    scales = head_scales(scale_ref, ALL)
    stats = cross_stats(rows, (near_stats, far_stats), ALL)
    for row in range(rows):
        at = slice(row * 2 * CELLS, (row + 1) * 2 * CELLS)
        total = own_ref[row, 1:3].reshape(2 * CELLS, PAIR_WIDTH)
        for side in range(2):
            pieces = grad_parts(
                [e_mid[side, h, at] for h in range(HALF)],
                [p_mid[side, h, at] for h in range(HALF)],
                *stats[side], scales,
            )
            total = total + key_grads(pieces, backward.at[side], ALL)
        total_ref[row, 1:3] = total.reshape(2, CELLS, PAIR_WIDTH)
    scales = head_scales(scale_ref, FIRST)
    stats = cross_stats(rows, (near_stats, far_stats), FIRST)
    for row in range(0, rows, 2):
        at = slice(row * CELLS, (row + 2) * CELLS)
        total = own_ref[row : row + 2, 0].reshape(2 * CELLS, PAIR_WIDTH)
        for side in range(2):
            pieces = grad_parts(
                [e_side[side, 0, h, at] for h in range(HALF)],
                [p_side[side, 0, h, at] for h in range(HALF)],
                *stats[side], scales,
            )
            total = total + key_grads(pieces, backward.at[side], FIRST)
        total_ref[row : row + 2, 0] = total.reshape(2, CELLS, PAIR_WIDTH)


def own_back_kernel(
    rows, scale_ref, stats_ref, backward, e_mid, p_mid, e_left, p_left,
    away_e_mid, away_p_mid, away_e_left, away_p_left, dq_sibling, *refs,
):
    kv_refs, refs = refs[: 3 * rows], refs[3 * rows :]
    own_ref, dq_own_ref, dq_other_ref, d_mid, d_left = refs
    scales = head_scales(scale_ref, ALL)
    inverse = [stats_ref[h : h + 1] for h in range(HALF)]
    delta = [stats_ref[HALF + h : HALF + h + 1] for h in range(HALF)]
    for index in range(3 * rows):
        at = slice(index * 2 * CELLS, (index + 1) * 2 * CELLS)
        if index < rows:
            exps, probs, start = e_mid, p_mid, index * 2 * CELLS
        else:
            exps, probs, start = away_e_mid, away_p_mid, (index - rows) * 2 * CELLS
        cut = slice(start, start + 2 * CELLS)
        pieces = grad_parts(
            [exps[h, cut] for h in range(HALF)], [probs[h, cut] for h in range(HALF)],
            inverse, delta, scales,
        )
        for h in range(HALF):
            d_mid[h, at] = pieces[h]
        if index < rows:
            part = key_grads(pieces, backward, ALL)
            own_ref[index, 1:3] = part.reshape(2, CELLS, PAIR_WIDTH)
    scales = head_scales(scale_ref, FIRST)
    inverse = [a[:, FIRST] for a in inverse]
    delta = [a[:, FIRST] for a in delta]
    for index in range(0, 3 * rows, 2):
        at = slice(index * CELLS, (index + 2) * CELLS)
        if index < rows:
            exps, probs, start = e_left, p_left, index * CELLS
        else:
            exps, probs, start = away_e_left, away_p_left, (index - rows) * CELLS
        cut = slice(start, start + 2 * CELLS)
        pieces = grad_parts(
            [exps[h, cut] for h in range(HALF)], [probs[h, cut] for h in range(HALF)],
            inverse, delta, scales,
        )
        for h in range(HALF):
            d_left[h, at] = pieces[h]
        if index < rows:
            part = key_grads(pieces, backward, FIRST)
            own_ref[index : index + 2, 0] = part.reshape(2, CELLS, PAIR_WIDTH)
    mid = jnp.concatenate([ref[1:3].reshape(2 * CELLS, PAIR_WIDTH) for ref in kv_refs], 0)
    left = jnp.concatenate([ref[0] for ref in kv_refs], 0)
    columns = []
    for h in range(HALF):
        made = query_grads(mid, d_mid[h], h)
        first = query_grads(left, d_left[h], h)
        last = dq_sibling[h * HEAD_DIM : (h + 1) * HEAD_DIM]
        columns.append(made + jnp.concatenate([first, last], 1))
    dq = jnp.concatenate(columns, 0).T
    dq_own_ref[...] = jnp.concatenate([dq[:CELLS], dq[2 * CELLS : 3 * CELLS]], 1)
    dq_other_ref[...] = jnp.concatenate([dq[CELLS : 2 * CELLS], dq[3 * CELLS :]], 1).astype(BF16)


def column_out_kernel(total_ref, sibling_ref, dq_other_ref, inner_ref, to_lat_ref, edge_ref, corner_ref):
    inner_ref[0] = total_ref[0, 1]
    inner_ref[1] = total_ref[0, 2] + sibling_ref[0].astype(F32)
    to_lat_ref[0] = total_ref[1, 1].astype(BF16)
    to_lat_ref[2] = dq_other_ref[...]
    to_lat_ref[1] = (total_ref[1, 2] + sibling_ref[1].astype(F32)).astype(BF16)
    edge_ref[...] = total_ref[0, 0].astype(BF16)
    corner_ref[...] = total_ref[1, 0].astype(BF16)


def finish_kernel(
    inner_ref, dq_ref, other_ref, edge_ref, corner_ref,
    query_raw, query_inverse, key_raw, key_inverse, x_ref, order_ref, gain_ref, qkv_ref, out_ref,
):
    frames, lat_rows, lon_cols, width = out_ref.shape
    cells = frames * lat_rows * lon_cols
    parity = lax.rem(lax.axis_index("lon"), 2)
    upper = lax.rem(lax.axis_index("lat"), 2) == 1

    def joined(mine, theirs):
        return jnp.where(
            upper, jnp.concatenate([theirs, mine], 1), jnp.concatenate([mine, theirs], 1)
        )

    def by_slot(packed):
        return jnp.concatenate([packed[:, :HALF_WIDTH], packed[:, HALF_WIDTH:]], 0)

    def with_edge(inner, edge):
        return jnp.concatenate([inner[0] + edge.astype(F32), inner[1]], 0)

    dkv_mine = with_edge(inner_ref[...], edge_ref[...])
    dkv_theirs = with_edge(other_ref[:2].astype(F32), corner_ref[...])
    grads = [
        joined(by_slot(dq_ref[...]), by_slot(other_ref[2].astype(F32))),
        joined(dkv_mine[:, :HALF_WIDTH], dkv_theirs[:, :HALF_WIDTH]),
        joined(dkv_mine[:, HALF_WIDTH:], dkv_theirs[:, HALF_WIDTH:]),
    ]
    grad_normed = dot_last(grads[2].astype(BF16), qkv_ref[2])
    for c, (raw, inverse) in enumerate(((query_raw, query_inverse), (key_raw, key_inverse))):
        raw, inverse = raw[...], inverse[...]
        inner = head_means(raw * grads[c])
        grad_raw = inverse * grads[c] - inverse * inverse * inverse * raw * inner
        grad_normed = grad_normed + dot_last(grad_raw.astype(BF16), qkv_ref[c])
    order = order_ref[...]
    x = x_ref[...].astype(F32)
    inverse = lax.rsqrt(jnp.mean(x * x, -1, keepdims=True) + EPS)
    grad = gain_ref[...].reshape(1, width) * grad_normed
    inner = jnp.mean(x * grad, -1, keepdims=True)
    grad = (inverse * grad - inverse * inverse * inverse * x * inner).astype(BF16)
    grad = dot_first(order, grad)
    out_ref[...] = grad.reshape(out_ref.shape).astype(BF16)


VMEM = pl.BlockSpec(memory_space=pltpu.VMEM)


def kernel_call(
    body, name, outs, args, scratch=(), limit_mib=16, micros=1.0
):
    return pl.pallas_call(
        body,
        name=name,
        out_shape=[jax.ShapeDtypeStruct(shape, dtype) for shape, dtype in outs],
        in_specs=[VMEM] * len(args),
        out_specs=[VMEM] * len(outs),
        scratch_shapes=list(scratch),
        compiler_params=pltpu.CompilerParams(vmem_limit_bytes=limit_mib * 1024 * 1024),
        cost_estimate=pl.CostEstimate(
            flops=int(micros * FLOPS_PER_US), bytes_accessed=0, transcendentals=0
        ),
    )(*args)


def per_device(tokens, key_count, norm_gain, qkv_weight, out_weight, logit_scale, grad_out):
    frames, lat_rows, lon_cols, width = tokens.shape
    assert frames == BLOCK and lat_rows == BLOCK and lon_cols == 2 * BLOCK
    assert lax.axis_size("lat") % 2 == 0 and lax.axis_size("lon") % 2 == 0
    cells = frames * lat_rows * lon_cols
    blocks = lon_cols // BLOCK
    head_width = HEADS * HEAD_DIM
    qg_shape = ((blocks, CELLS, PAIR_WIDTH), BF16)
    edge_shape = ((CELLS, PAIR_WIDTH), BF16)

    order, x = kernel_call(
        order_kernel, "order", [((cells, cells), BF16), ((cells, width), BF16)], [tokens],
        micros=10.0,
    )
    projected = ((cells, head_width), F32)
    kv_own, kv_other, edge, corner, normed, key_raw, key_inverse = kernel_call(
        key_value_kernel, "key_value",
        [qg_shape, qg_shape, edge_shape, edge_shape, ((cells, width), BF16), projected, projected],
        [key_count, x, norm_gain, qkv_weight], micros=2.0,
    )
    edge = pair_swap(edge, "lon", 1)
    corner = corner_swap(corner)
    kv_other = pair_swap(kv_other, "lat", 0)
    qg_own, qg_other, query_raw, query_inverse, scales = kernel_call(
        query_grad_kernel, "query_grad",
        [qg_shape, qg_shape, projected, projected, ((HALF, 4 * CELLS), F32)],
        [logit_scale, order, normed, grad_out, qkv_weight, out_weight], micros=5.0,
    )
    qg_other = pair_swap(qg_other, "lat", 0)
    (kv_other,) = kernel_call(join_kernel, "join", [qg_shape], [kv_other], micros=3.0)
    kv_rows = [
        jnp.concatenate([edge[None], kv_own], 0),
        jnp.concatenate([corner[None], kv_other], 0),
    ]
    upper = lax.rem(lax.axis_index("lat"), 2) == 1
    wide = lax.axis_size("lat") > 2
    if wide:
        even = jnp.where(upper, kv_rows[1], kv_rows[0])
        odd = jnp.where(upper, kv_rows[0], kv_rows[1])
        kv_rows += [shift_by(odd, "lat", 2), shift_by(even, "lat", -2)]
    rows = len(kv_rows)
    kv_away = [frame_swap(kv, phase) for phase in range(2) for kv in kv_rows]
    qg_both = jnp.concatenate([qg_own, qg_other], 0)
    qg_away = [frame_swap(qg_both, phase) for phase in range(2)]

    queries = 4 * CELLS
    tables = [((2 * HALF, TILE, queries), BF16), ((2 * HALF, queries, TILE), BF16)]
    sums_shape = ((2 * HALF, 8, queries), F32)

    def kept(groups):
        mid = ((HALF, groups * 2 * CELLS, queries), F32)
        left = ((HALF, groups * CELLS, 2 * CELLS), F32)
        return [mid, mid, left, left]

    weights, backward, sums, *own_kept = kernel_call(
        functools.partial(own_score_kernel, rows), "own_score",
        tables + [sums_shape] + kept(rows),
        [scales, qg_both, *kv_rows], micros=1.5,
    )
    siblings = jnp.stack([kv[2] for kv in kv_rows + kv_away], 0)
    siblings = pair_swap(siblings, "lon", 0)
    sums, *away_kept = kernel_call(
        functools.partial(away_score_kernel, rows), "away_score",
        [sums_shape] + kept(2 * rows), [scales, weights, sums, *kv_away],
        micros=20.0,
    )
    half_part = (rows, CELLS, PAIR_WIDTH)
    sibling_part, stats, dq_sibling = kernel_call(
        functools.partial(sibling_kernel, rows), "sibling",
        [(half_part, F32), ((2 * HALF, queries), F32), ((HALF_WIDTH, 2 * CELLS), F32)],
        [scales, weights, backward, sums, siblings], micros=1.5,
    )
    near_stats, far_stats = frame_swap(stats, 0), frame_swap(stats, 1)
    cross_mid = ((2, HALF, rows * 2 * CELLS, queries), F32)
    cross_side = ((2, 2, HALF, rows * CELLS, 2 * CELLS), F32)
    cross_backward, e_mid, p_mid, e_side, p_side = kernel_call(
        functools.partial(cross_score_kernel, rows), "cross_score",
        [((2,) + tables[1][0], BF16), cross_mid, cross_mid, cross_side, cross_side],
        [scales, *qg_away, *kv_rows, siblings], micros=2.0,
        scratch=[pltpu.VMEM((2,) + tables[0][0], BF16)],
    )
    part = (rows, blocks + 1, CELLS, PAIR_WIDTH)
    packed = (CELLS, 2 * HALF_WIDTH)
    own_part, dq_own, dq_other = kernel_call(
        functools.partial(own_back_kernel, rows), "own_back",
        [(part, F32), (packed, F32), (packed, BF16)],
        [scales, stats, backward, *own_kept, *away_kept, dq_sibling, *kv_rows, *kv_away],
        micros=2.0,
        scratch=[
            pltpu.VMEM((HALF, 3 * rows * 2 * CELLS, queries), BF16),
            pltpu.VMEM((HALF, 3 * rows * CELLS, 2 * CELLS), BF16),
        ],
    )
    (sibling_part,) = kernel_call(
        functools.partial(cross_sibling_kernel, rows), "cross_sibling", [(half_part, BF16)],
        [scales, near_stats, far_stats, cross_backward, e_side, p_side, sibling_part],
        micros=0.5,
    )
    sibling_part = pair_swap(sibling_part, "lon", 0)
    (total,) = kernel_call(
        functools.partial(cross_back_kernel, rows), "cross_back", [(part, F32)],
        [scales, near_stats, far_stats, cross_backward, e_mid, p_mid, e_side, p_side,
         own_part],
        micros=1.5,
    )
    if wide:
        total = total.at[:, blocks].add(sibling_part.astype(F32))
        sibling_part = jnp.zeros_like(sibling_part)
        to_odd = shift_by(total[2].astype(BF16), "lat", -2).astype(F32)
        to_even = shift_by(total[3].astype(BF16), "lat", 2).astype(F32)
        total = total[:2] + jnp.stack(
            [jnp.where(upper, to_odd, to_even), jnp.where(upper, to_even, to_odd)], 0
        )
    inner, to_lat, edge, corner = kernel_call(
        column_out_kernel, "column_out",
        [((blocks, CELLS, PAIR_WIDTH), F32), ((blocks + 1, CELLS, PAIR_WIDTH), BF16),
         edge_shape, edge_shape],
        [total, sibling_part, dq_other],
    )
    edge = pair_swap(edge, "lon", 1)
    corner = corner_swap(corner)
    other = pair_swap(to_lat, "lat", 0)
    (grad_tokens,) = kernel_call(
        finish_kernel, "finish", [(tokens.shape, BF16)],
        [inner, dq_own, other, edge, corner, query_raw, query_inverse, key_raw, key_inverse,
         x, order, norm_gain, qkv_weight],
        micros=2.0,
    )
    return grad_tokens


def solution(mesh):
    in_specs = (
        P("tm", "lat", "lon", None),
        P("tm", "lat", "lon"),
        P(),
        P(),
        P(),
        P(),
        P("tm", "lat", "lon", None),
    )
    out_specs = P("tm", "lat", "lon", None)
    return jax.shard_map(
        per_device, mesh=mesh, in_specs=in_specs, out_specs=out_specs, check_vma=False
    )
```

```python
import functools
import math

import jax
import jax.numpy as jnp
from jax import lax
from jax.experimental import pallas as pl
from jax.experimental.pallas import tpu as pltpu
from jax.sharding import PartitionSpec as P

HEADS = 6
HEAD_DIM = 64
BLOCK = 4
CELLS = BLOCK * BLOCK * BLOCK
HALF = HEADS // 2
HALF_WIDTH = HALF * HEAD_DIM
PAIR_WIDTH = 2 * HALF_WIDTH
TILE = 2 * HEAD_DIM
TILES = PAIR_WIDTH // TILE
DEAD_KEY = 64.0
DROPPED = -1e30
FLOPS_PER_US = 1e9

EPS = 1e-06
F32 = jnp.float32
BF16 = jnp.bfloat16


def partner_of(device, count, phase):
    return device + 1 if device % 2 == phase else device - 1


def pair_swap(array, axis, phase):
    count = lax.axis_size(axis)
    pairs = [(device, partner_of(device, count, phase) % count) for device in range(count)]
    return lax.ppermute(array, axis, pairs)


def frame_swap(array, phase):
    frames, lons = lax.axis_size("tm"), lax.axis_size("lon")
    pairs = []
    for frame in range(frames):
        for lon in range(lons):
            to = (partner_of(frame, frames, phase), lon)
            if not 0 <= to[0] < frames:
                to = (frame, partner_of(lon, lons, 0))
            pairs.append((frame * lons + lon, to[0] * lons + to[1]))
    return lax.ppermute(array, ("tm", "lon"), pairs)


def corner_swap(array):
    lats, lons = lax.axis_size("lat"), lax.axis_size("lon")
    pairs = []
    for lat in range(lats):
        for lon in range(lons):
            to = partner_of(lat, lats, 0) * lons + partner_of(lon, lons, 1) % lons
            pairs.append((lat * lons + lon, to))
    return lax.ppermute(array, ("lat", "lon"), pairs)


def shift_by(array, axis, step):
    count = lax.axis_size(axis)
    pairs = [(i, i + step) for i in range(count) if 0 <= i + step < count]
    return lax.ppermute(array, axis, pairs)


def dot(a, b):
    return lax.dot_general(a, b, (((1,), (0,)), ((), ())), preferred_element_type=F32)


def dot_last(a, b):
    return lax.dot_general(a, b, (((1,), (1,)), ((), ())), preferred_element_type=F32)


def dot_first(a, b):
    return lax.dot_general(a, b, (((0,), (0,)), ((), ())), preferred_element_type=F32)


def head_means(values):
    rows = lax.broadcasted_iota(jnp.int32, (TILE, TILE), 0) // HEAD_DIM
    cols = lax.broadcasted_iota(jnp.int32, (TILE, TILE), 1) // HEAD_DIM
    ones = (rows == cols).astype(F32).astype(BF16)
    high = values.astype(BF16)
    low = (values - high.astype(F32)).astype(BF16)
    pieces = []
    for start in range(0, values.shape[1], TILE):
        cut = slice(start, start + TILE)
        pieces.append(dot(high[:, cut], ones) + dot(low[:, cut], ones))
    return jnp.concatenate(pieces, 1) * (1.0 / HEAD_DIM)


def block_order(lat_rows, lon_cols, count, parity):
    blocks = lon_cols // BLOCK
    row = lax.broadcasted_iota(jnp.int32, (count, count), 0)
    source = lax.broadcasted_iota(jnp.int32, (count, count), 1)
    slot = row // CELLS
    place = row % CELLS
    frame = place // (BLOCK * BLOCK)
    lat = (place // BLOCK) % BLOCK
    col = place % BLOCK
    block = jnp.where(parity == 1, blocks - 1 - slot, slot)
    wanted = (frame * lat_rows + lat) * lon_cols + block * BLOCK + col
    return (source == wanted).astype(F32).astype(BF16)


def halves(first, second):
    low = jnp.concatenate([first[:, :HALF_WIDTH], second[:, :HALF_WIDTH]], 1)
    high = jnp.concatenate([first[:, HALF_WIDTH:], second[:, HALF_WIDTH:]], 1)
    return low, high


def normalised(x, gain_ref):
    inverse = lax.rsqrt(jnp.mean(x * x, -1, keepdims=True) + EPS)
    return (x * inverse * gain_ref[...].reshape(1, x.shape[1])).astype(BF16)


def order_kernel(tokens_ref, order_ref, x_ref):
    frames, lat_rows, lon_cols, width = tokens_ref.shape
    cells = frames * lat_rows * lon_cols
    order = block_order(lat_rows, lon_cols, cells, lax.rem(lax.axis_index("lon"), 2))
    order_ref[...] = order
    x = dot(order, tokens_ref[...].astype(F32).reshape(cells, width).astype(BF16)).astype(BF16)
    x_ref[...] = x


def key_value_kernel(
    count_ref, x_ref, gain_ref, qkv_ref,
    kv_own_ref, kv_other_ref, edge_ref, normed_ref, raw_ref, inverse_ref,
):
    cells = x_ref.shape[0]
    blocks = cells // CELLS
    parity = lax.rem(lax.axis_index("lon"), 2)
    upper = lax.rem(lax.axis_index("lat"), 2) == 1
    normed = normalised(x_ref[...].astype(F32), gain_ref)
    normed_ref[...] = normed
    key, value = dot(normed, qkv_ref[1]), dot(normed, qkv_ref[2])
    raw_ref[...] = key
    inverse = lax.rsqrt(head_means(key * key) + EPS)
    inverse_ref[...] = inverse
    place = lax.broadcasted_iota(jnp.int32, (CELLS, 1), 0)
    counts = count_ref[0]
    live = []
    for slot in range(blocks):
        flip = blocks - 1 - slot
        live.append(
            place
            < jnp.where(parity == 1, counts[:, flip : flip + 1], counts[:, slot : slot + 1])
        )
    key = jnp.where(jnp.concatenate(live, 0), key * inverse, DEAD_KEY)
    shape = (blocks, CELLS, PAIR_WIDTH)
    low, high = halves(key, value)
    kv_own_ref[...] = jnp.where(upper, high, low).astype(BF16).reshape(shape)
    kv_other_ref[...] = jnp.where(upper, low, high).astype(BF16).reshape(shape)
    edge_ref[...] = kv_own_ref[0]


def query_grad_kernel(
    scale_in, order_ref, normed_ref, grad_ref, qkv_ref, out_weight_ref, kv_other_ref,
    qg_own_ref, qg_other_ref, corner_ref, raw_ref, inverse_ref, scale_ref,
):
    corner_ref[...] = kv_other_ref[0]
    cells, width = normed_ref.shape
    upper = lax.rem(lax.axis_index("lat"), 2) == 1
    all_scales = scale_in[...].reshape(1, HEADS) * (1.0 / math.sqrt(HEAD_DIM))
    for h in range(HALF):
        mine = jnp.where(
            upper, all_scales[:, HALF + h : HALF + h + 1], all_scales[:, h : h + 1]
        )
        scale_ref[h : h + 1] = jnp.broadcast_to(mine, (1, 4 * CELLS))
    query = dot(normed_ref[...], qkv_ref[0])
    raw_ref[...] = query
    inverse = lax.rsqrt(head_means(query * query) + EPS)
    inverse_ref[...] = inverse
    grad = dot_last(
        grad_ref[...].astype(F32).reshape(cells, width).astype(BF16), out_weight_ref[...]
    ).astype(BF16)
    low, high = halves(query * inverse, dot(order_ref[...], grad))
    shape = (cells // CELLS, CELLS, PAIR_WIDTH)
    qg_own_ref[...] = jnp.where(upper, high, low).astype(BF16).reshape(shape)
    qg_other_ref[...] = jnp.where(upper, low, high).astype(BF16).reshape(shape)


def join_kernel(kv_in, kv_ref):
    kv_ref[...] = kv_in[...]


def lane_tile(j):
    return slice((j // 2) * TILE, (j // 2 + 1) * TILE)


class Place:
    def __init__(self, rows):
        self.rows = rows
        tm, frames = lax.axis_index("tm"), lax.axis_size("tm")
        odd = lax.rem(tm, 2) == 1
        near, far = jnp.where(odd, tm - 1, tm + 1), jnp.where(odd, tm + 1, tm - 1)
        self.there = [None] + [((at >= 0) & (at < frames)) for at in (near, far)]
        self.upper = lax.rem(lax.axis_index("lat"), 2)

    def bias(self, frame, row, lanes):
        there = self.there[frame]
        total = 0.0 if there is None else jnp.where(there, 0.0, DROPPED)
        if row < 2:
            return total
        pair, pairs = lax.axis_index("lat") // 2, lax.axis_size("lat") // 2
        if row == 2:
            inside, wanted = pair > 0, self.upper
        else:
            inside, wanted = pair < pairs - 1, 1 - self.upper
        lane_row = (lax.broadcasted_iota(jnp.int32, (1, lanes), 1) // CELLS) % 2
        seen = (lane_row == wanted) & inside
        return total + jnp.where(seen, 0.0, DROPPED)


def head_scales(scale_ref, lanes):
    return [scale_ref[h : h + 1, lanes] for h in range(HALF)]


def key_bias(keys):
    return jnp.where(keys[:, 0:1].astype(F32) < 0.5 * DEAD_KEY, 0.0, DROPPED)


def score(keys, bias, weights_ref, lanes, scale_ref, sums):
    to_exp2 = [s * math.log2(math.e) for s in head_scales(scale_ref, lanes)]
    count = keys.shape[0]
    exps, probs = [], []
    for h in range(HALF):
        scores = dot(keys[:, lane_tile(h)], weights_ref[h, :, lanes])
        grad_prob = dot(keys[:, lane_tile(HALF + h)], weights_ref[HALF + h, :, lanes])
        masked = jnp.exp2(scores * to_exp2[h] + bias)
        if sums is not None:
            shape = (count // 8, 8, masked.shape[1])
            sums[h] = sums[h] + jnp.sum(masked.reshape(shape), 0)
            inner = (masked * grad_prob).reshape(shape)
            sums[HALF + h] = sums[HALF + h] + jnp.sum(inner, 0)
        exps.append(masked)
        probs.append(grad_prob)
    return exps, probs


ALL = slice(0, 4 * CELLS)
FIRST = slice(0, 2 * CELLS)
LAST = slice(2 * CELLS, 4 * CELLS)


def score_groups(place, frames, kv_refs, weights_ref, scale_ref, sums, e_mid, p_mid, e_left, p_left):
    rows = place.rows
    side = [jnp.zeros((8, 2 * CELLS), F32) for _ in range(2 * HALF)]
    for index, ref in enumerate(kv_refs):
        frame, row = frames[index // rows], index % rows
        keys = ref[1:3].reshape(2 * CELLS, PAIR_WIDTH)
        bias = key_bias(keys) + place.bias(frame, row, 4 * CELLS)
        exps, probs = score(keys, bias, weights_ref, ALL, scale_ref, sums)
        for h in range(HALF):
            e_mid[h, index * 2 * CELLS : (index + 1) * 2 * CELLS] = exps[h]
            p_mid[h, index * 2 * CELLS : (index + 1) * 2 * CELLS] = probs[h]
    for index in range(0, len(kv_refs), 2):
        frame, row = frames[index // rows], index % rows
        pair = [kv_refs[index][0], kv_refs[index + 1][0]]
        bias = jnp.concatenate(
            [
                jnp.broadcast_to(
                    key_bias(keys) + place.bias(frame, row + i, 2 * CELLS), (CELLS, 2 * CELLS)
                )
                for i, keys in enumerate(pair)
            ],
            0,
        )
        keys = jnp.concatenate(pair, 0)
        exps, probs = score(keys, bias, weights_ref, FIRST, scale_ref, side)
        for h in range(HALF):
            e_left[h, index * CELLS : (index + 2) * CELLS] = exps[h]
            p_left[h, index * CELLS : (index + 2) * CELLS] = probs[h]
    return [jnp.concatenate([a[:, FIRST] + b, a[:, LAST]], 1) for a, b in zip(sums, side)]


def query_tables(qg_ref, weights, backward):
    rows = jnp.concatenate([qg_ref[0], qg_ref[2], qg_ref[1], qg_ref[3]], 0).astype(F32)
    cols = rows.T
    count = rows.shape[0]
    lane_half = lax.broadcasted_iota(jnp.int32, (count, TILE), 1) // HEAD_DIM
    row_half = lax.broadcasted_iota(jnp.int32, (TILE, count), 0) // HEAD_DIM
    for j in range(2 * HALF):
        backward[j] = jnp.where(lane_half == j % 2, rows[:, lane_tile(j)], 0.0).astype(BF16)
        weights[j] = jnp.where(row_half == j % 2, cols[lane_tile(j)], 0.0).astype(BF16)


def own_score_kernel(rows, scale_ref, qkv_ref, qg_ref, *refs):
    kv_refs, refs = refs[:rows], refs[rows:]
    turned_ref, weights, backward, sums_ref, e_mid, p_mid, e_left, p_left = refs
    for c in range(3):
        turned_ref[c] = qkv_ref[c].T
    queries = 4 * CELLS
    query_tables(qg_ref, weights, backward)
    sums = [jnp.zeros((8, queries), F32) for _ in range(2 * HALF)]
    sums = score_groups(
        Place(rows), (0,), kv_refs, weights, scale_ref, sums,
        e_mid, p_mid, e_left, p_left,
    )
    for j in range(2 * HALF):
        sums_ref[j] = sums[j]


def away_score_kernel(rows, scale_ref, weights, sums_in, *refs):
    kv_refs, refs = refs[: 2 * rows], refs[2 * rows :]
    sums_ref, e_mid, p_mid, e_left, p_left = refs
    sums = [sums_in[j] for j in range(2 * HALF)]
    sums = score_groups(
        Place(rows), (1, 2), kv_refs, weights, scale_ref, sums,
        e_mid, p_mid, e_left, p_left,
    )
    for j in range(2 * HALF):
        sums_ref[j] = sums[j]


def grad_parts(exps, probs, inverse, delta, scales):
    grads, halves_of = [], []
    for h in range(HALF):
        prob = exps[h] * inverse[h]
        halves_of.append(prob.astype(BF16))
        grads.append((prob * (probs[h] - delta[h]) * scales[h]).astype(BF16))
    return grads + halves_of


def key_grads(pieces, backward, lanes):
    outs = []
    for tile in range(TILES):
        both = jnp.concatenate([pieces[2 * tile], pieces[2 * tile + 1]], 1)
        rows = jnp.concatenate(
            [backward[2 * tile, lanes], backward[2 * tile + 1, lanes]], 0
        )
        outs.append(dot(both, rows))
    return jnp.concatenate(outs, 1)


def query_grads(keys, grads, h):
    own = slice((h % 2) * HEAD_DIM, (h % 2 + 1) * HEAD_DIM)
    return dot_first(keys[:, lane_tile(h)], grads)[own]


def side_bias(place, frame, row, keys):
    return jnp.concatenate(
        [
            jnp.broadcast_to(
                key_bias(keys[i]) + place.bias(frame, row + i, 2 * CELLS), (CELLS, 2 * CELLS)
            )
            for i in range(2)
        ],
        0,
    )


def sibling_kernel(
    rows, scale_ref, weights, backward, sums_in, keys_ref, part_ref, stats_ref, dq_ref
):
    place = Place(rows)
    side = [jnp.zeros((8, 2 * CELLS), F32) for _ in range(2 * HALF)]
    made = []
    for index in range(0, 3 * rows, 2):
        bias = side_bias(
            place, index // rows, index % rows, [keys_ref[index], keys_ref[index + 1]]
        )
        keys = keys_ref[index : index + 2].reshape(2 * CELLS, PAIR_WIDTH)
        made.append(score(keys, bias, weights, LAST, scale_ref, side))
    inverse, delta = [], []
    for h in range(HALF):
        total, inner = (
            jnp.concatenate([sums_in[j, :, FIRST], sums_in[j, :, LAST] + side[j]], 1)
            for j in (h, HALF + h)
        )
        inverse.append(1.0 / jnp.sum(total, 0, keepdims=True))
        delta.append(jnp.sum(inner, 0, keepdims=True) * inverse[h])
        stats_ref[h : h + 1] = inverse[h]
        stats_ref[HALF + h : HALF + h + 1] = delta[h]
    inverse = [a[:, LAST] for a in inverse]
    delta = [a[:, LAST] for a in delta]
    scales = head_scales(scale_ref, LAST)
    grads = []
    for index in range(0, 3 * rows, 2):
        pieces = grad_parts(*made[index // 2], inverse, delta, scales)
        grads.append(pieces[:HALF])
        if index < rows:
            part = key_grads(pieces, backward, LAST)
            part_ref[index : index + 2] = part.reshape(2, CELLS, PAIR_WIDTH)
    keys = keys_ref[...].reshape(3 * rows * CELLS, PAIR_WIDTH)
    for h in range(HALF):
        dq_ref[h * HEAD_DIM : (h + 1) * HEAD_DIM] = query_grads(
            keys, jnp.concatenate([g[h] for g in grads], 0), h
        )


def cross_score_kernel(rows, scale_ref, *refs):
    qg_refs, refs = refs[:2], refs[2:]
    kv_refs, sibling_ref, refs = refs[:rows], refs[rows], refs[rows + 1 :]
    backward, e_mid, p_mid, e_side, p_side, weights = refs
    place = Place(rows)
    for side in range(2):
        query_tables(qg_refs[side], weights.at[side], backward.at[side])
    for row in range(rows):
        keys = kv_refs[row][1:3].reshape(2 * CELLS, PAIR_WIDTH)
        bias = key_bias(keys) + place.bias(0, row, 4 * CELLS)
        at = slice(row * 2 * CELLS, (row + 1) * 2 * CELLS)
        for side in range(2):
            exps, probs = score(keys, bias, weights.at[side], ALL, scale_ref, None)
            for h in range(HALF):
                e_mid[side, h, at] = exps[h]
                p_mid[side, h, at] = probs[h]
    for row in range(0, rows, 2):
        at = slice(row * CELLS, (row + 2) * CELLS)
        for edge, lanes in ((0, FIRST), (1, LAST)):
            if edge == 0:
                pair = [kv_refs[row][0], kv_refs[row + 1][0]]
            else:
                pair = [sibling_ref[row], sibling_ref[row + 1]]
            bias = side_bias(place, 0, row, pair)
            keys = jnp.concatenate(pair, 0)
            for side in range(2):
                exps, probs = score(keys, bias, weights.at[side], lanes, scale_ref, None)
                for h in range(HALF):
                    e_side[side, edge, h, at] = exps[h]
                    p_side[side, edge, h, at] = probs[h]


def cross_stats(rows, stats_refs, lanes):
    place = Place(rows)
    both = []
    for side, ref in enumerate(stats_refs):
        there = jnp.where(place.there[1 + side], 1.0, 0.0)
        inverse = [ref[h : h + 1, lanes] * there for h in range(HALF)]
        both.append((inverse, [ref[HALF + h : HALF + h + 1, lanes] for h in range(HALF)]))
    return both


def cross_sibling_kernel(
    rows, scale_ref, near_stats, far_stats, backward, e_side, p_side, part_in, part_ref
):
    scales = head_scales(scale_ref, LAST)
    stats = cross_stats(rows, (near_stats, far_stats), LAST)
    for row in range(0, rows, 2):
        at = slice(row * CELLS, (row + 2) * CELLS)
        total = part_in[row : row + 2].reshape(2 * CELLS, PAIR_WIDTH)
        for side in range(2):
            pieces = grad_parts(
                [e_side[side, 1, h, at] for h in range(HALF)],
                [p_side[side, 1, h, at] for h in range(HALF)],
                *stats[side], scales,
            )
            total = total + key_grads(pieces, backward.at[side], LAST)
        part_ref[row : row + 2] = total.reshape(2, CELLS, PAIR_WIDTH).astype(BF16)


def cross_back_kernel(
    rows, scale_ref, near_stats, far_stats, backward, e_mid, p_mid, e_side, p_side,
    own_ref, total_ref,
):
    scales = head_scales(scale_ref, ALL)
    stats = cross_stats(rows, (near_stats, far_stats), ALL)
    for row in range(rows):
        at = slice(row * 2 * CELLS, (row + 1) * 2 * CELLS)
        total = own_ref[row, 1:3].reshape(2 * CELLS, PAIR_WIDTH)
        for side in range(2):
            pieces = grad_parts(
                [e_mid[side, h, at] for h in range(HALF)],
                [p_mid[side, h, at] for h in range(HALF)],
                *stats[side], scales,
            )
            total = total + key_grads(pieces, backward.at[side], ALL)
        total_ref[row, 1:3] = total.reshape(2, CELLS, PAIR_WIDTH)
    scales = head_scales(scale_ref, FIRST)
    stats = cross_stats(rows, (near_stats, far_stats), FIRST)
    for row in range(0, rows, 2):
        at = slice(row * CELLS, (row + 2) * CELLS)
        total = own_ref[row : row + 2, 0].reshape(2 * CELLS, PAIR_WIDTH)
        for side in range(2):
            pieces = grad_parts(
                [e_side[side, 0, h, at] for h in range(HALF)],
                [p_side[side, 0, h, at] for h in range(HALF)],
                *stats[side], scales,
            )
            total = total + key_grads(pieces, backward.at[side], FIRST)
        total_ref[row : row + 2, 0] = total.reshape(2, CELLS, PAIR_WIDTH)


def own_back_kernel(
    rows, scale_ref, stats_ref, backward, e_mid, p_mid, e_left, p_left,
    away_e_mid, away_p_mid, away_e_left, away_p_left, dq_sibling, *refs,
):
    kv_refs, refs = refs[: 3 * rows], refs[3 * rows :]
    own_ref, dq_own_ref, dq_other_ref, d_mid, d_left = refs
    scales = head_scales(scale_ref, ALL)
    inverse = [stats_ref[h : h + 1] for h in range(HALF)]
    delta = [stats_ref[HALF + h : HALF + h + 1] for h in range(HALF)]
    for index in range(3 * rows):
        at = slice(index * 2 * CELLS, (index + 1) * 2 * CELLS)
        if index < rows:
            exps, probs, start = e_mid, p_mid, index * 2 * CELLS
        else:
            exps, probs, start = away_e_mid, away_p_mid, (index - rows) * 2 * CELLS
        cut = slice(start, start + 2 * CELLS)
        pieces = grad_parts(
            [exps[h, cut] for h in range(HALF)], [probs[h, cut] for h in range(HALF)],
            inverse, delta, scales,
        )
        for h in range(HALF):
            d_mid[h, at] = pieces[h]
        if index < rows:
            part = key_grads(pieces, backward, ALL)
            own_ref[index, 1:3] = part.reshape(2, CELLS, PAIR_WIDTH)
    scales = head_scales(scale_ref, FIRST)
    inverse = [a[:, FIRST] for a in inverse]
    delta = [a[:, FIRST] for a in delta]
    for index in range(0, 3 * rows, 2):
        at = slice(index * CELLS, (index + 2) * CELLS)
        if index < rows:
            exps, probs, start = e_left, p_left, index * CELLS
        else:
            exps, probs, start = away_e_left, away_p_left, (index - rows) * CELLS
        cut = slice(start, start + 2 * CELLS)
        pieces = grad_parts(
            [exps[h, cut] for h in range(HALF)], [probs[h, cut] for h in range(HALF)],
            inverse, delta, scales,
        )
        for h in range(HALF):
            d_left[h, at] = pieces[h]
        if index < rows:
            part = key_grads(pieces, backward, FIRST)
            own_ref[index : index + 2, 0] = part.reshape(2, CELLS, PAIR_WIDTH)
    mid = jnp.concatenate([ref[1:3].reshape(2 * CELLS, PAIR_WIDTH) for ref in kv_refs], 0)
    left = jnp.concatenate([ref[0] for ref in kv_refs], 0)
    columns = []
    for h in range(HALF):
        made = query_grads(mid, d_mid[h], h)
        first = query_grads(left, d_left[h], h)
        last = dq_sibling[h * HEAD_DIM : (h + 1) * HEAD_DIM]
        columns.append(made + jnp.concatenate([first, last], 1))
    dq = jnp.concatenate(columns, 0).T
    dq_own_ref[...] = jnp.concatenate([dq[:CELLS], dq[2 * CELLS : 3 * CELLS]], 1)
    dq_other_ref[...] = jnp.concatenate([dq[CELLS : 2 * CELLS], dq[3 * CELLS :]], 1).astype(BF16)


def column_out_kernel(total_ref, sibling_ref, dq_other_ref, inner_ref, to_lat_ref, edge_ref, corner_ref):
    inner_ref[0] = total_ref[0, 1]
    inner_ref[1] = total_ref[0, 2] + sibling_ref[0].astype(F32)
    to_lat_ref[0] = total_ref[1, 1].astype(BF16)
    to_lat_ref[2] = dq_other_ref[...]
    to_lat_ref[1] = (total_ref[1, 2] + sibling_ref[1].astype(F32)).astype(BF16)
    edge_ref[...] = total_ref[0, 0].astype(BF16)
    corner_ref[...] = total_ref[1, 0].astype(BF16)


def finish_kernel(
    inner_ref, dq_ref, other_ref, edge_ref, corner_ref,
    query_raw, query_inverse, key_raw, key_inverse, x_ref, order_ref, gain_ref, turned_ref, out_ref,
):
    frames, lat_rows, lon_cols, width = out_ref.shape
    cells = frames * lat_rows * lon_cols
    parity = lax.rem(lax.axis_index("lon"), 2)
    upper = lax.rem(lax.axis_index("lat"), 2) == 1

    def joined(mine, theirs):
        return jnp.where(
            upper, jnp.concatenate([theirs, mine], 1), jnp.concatenate([mine, theirs], 1)
        )

    def by_slot(packed):
        return jnp.concatenate([packed[:, :HALF_WIDTH], packed[:, HALF_WIDTH:]], 0)

    def with_edge(inner, edge):
        return jnp.concatenate([inner[0] + edge.astype(F32), inner[1]], 0)

    dkv_mine = with_edge(inner_ref[...], edge_ref[...])
    dkv_theirs = with_edge(other_ref[:2].astype(F32), corner_ref[...])
    grads = [
        joined(by_slot(dq_ref[...]), by_slot(other_ref[2].astype(F32))),
        joined(dkv_mine[:, :HALF_WIDTH], dkv_theirs[:, :HALF_WIDTH]),
        joined(dkv_mine[:, HALF_WIDTH:], dkv_theirs[:, HALF_WIDTH:]),
    ]
    grad_normed = dot(grads[2].astype(BF16), turned_ref[2])
    for c, (raw, inverse) in enumerate(((query_raw, query_inverse), (key_raw, key_inverse))):
        raw, inverse = raw[...], inverse[...]
        inner = head_means(raw * grads[c])
        grad_raw = inverse * grads[c] - inverse * inverse * inverse * raw * inner
        grad_normed = grad_normed + dot(grad_raw.astype(BF16), turned_ref[c])
    order = order_ref[...]
    x = x_ref[...].astype(F32)
    inverse = lax.rsqrt(jnp.mean(x * x, -1, keepdims=True) + EPS)
    grad = gain_ref[...].reshape(1, width) * grad_normed
    inner = jnp.mean(x * grad, -1, keepdims=True)
    grad = (inverse * grad - inverse * inverse * inverse * x * inner).astype(BF16)
    grad = dot_first(order, grad)
    out_ref[...] = grad.reshape(out_ref.shape).astype(BF16)


VMEM = pl.BlockSpec(memory_space=pltpu.VMEM)


def kernel_call(
    body, name, outs, args, scratch=(), limit_mib=16, micros=1.0
):
    return pl.pallas_call(
        body,
        name=name,
        out_shape=[jax.ShapeDtypeStruct(shape, dtype) for shape, dtype in outs],
        in_specs=[VMEM] * len(args),
        out_specs=[VMEM] * len(outs),
        scratch_shapes=list(scratch),
        compiler_params=pltpu.CompilerParams(vmem_limit_bytes=limit_mib * 1024 * 1024),
        cost_estimate=pl.CostEstimate(
            flops=int(micros * FLOPS_PER_US), bytes_accessed=0, transcendentals=0
        ),
    )(*args)


def per_device(tokens, key_count, norm_gain, qkv_weight, out_weight, logit_scale, grad_out):
    frames, lat_rows, lon_cols, width = tokens.shape
    assert frames == BLOCK and lat_rows == BLOCK and lon_cols == 2 * BLOCK
    assert lax.axis_size("lat") % 2 == 0 and lax.axis_size("lon") % 2 == 0
    cells = frames * lat_rows * lon_cols
    blocks = lon_cols // BLOCK
    head_width = HEADS * HEAD_DIM
    qg_shape = ((blocks, CELLS, PAIR_WIDTH), BF16)
    edge_shape = ((CELLS, PAIR_WIDTH), BF16)

    order, x = kernel_call(
        order_kernel, "order", [((cells, cells), BF16), ((cells, width), BF16)], [tokens],
        micros=10.0,
    )
    projected = ((cells, head_width), F32)
    kv_own, kv_other, edge, normed, key_raw, key_inverse = kernel_call(
        key_value_kernel, "key_value",
        [qg_shape, qg_shape, edge_shape, ((cells, width), BF16), projected, projected],
        [key_count, x, norm_gain, qkv_weight], micros=2.0,
    )
    edge = pair_swap(edge, "lon", 1)
    kv_made, kv_other = kv_other, pair_swap(kv_other, "lat", 0)
    qg_own, qg_other, corner, query_raw, query_inverse, scales = kernel_call(
        query_grad_kernel, "query_grad",
        [qg_shape, qg_shape, edge_shape, projected, projected, ((HALF, 4 * CELLS), F32)],
        [logit_scale, order, normed, grad_out, qkv_weight, out_weight, kv_made], micros=5.0,
    )
    corner = corner_swap(corner)
    qg_other = pair_swap(qg_other, "lat", 0)
    (kv_other,) = kernel_call(join_kernel, "join", [qg_shape], [kv_other], micros=3.0)
    kv_rows = [
        jnp.concatenate([edge[None], kv_own], 0),
        jnp.concatenate([corner[None], kv_other], 0),
    ]
    upper = lax.rem(lax.axis_index("lat"), 2) == 1
    wide = lax.axis_size("lat") > 2
    if wide:
        even = jnp.where(upper, kv_rows[1], kv_rows[0])
        odd = jnp.where(upper, kv_rows[0], kv_rows[1])
        kv_rows += [shift_by(odd, "lat", 2), shift_by(even, "lat", -2)]
    rows = len(kv_rows)
    kv_away = [frame_swap(kv, phase) for phase in range(2) for kv in kv_rows]
    qg_both = jnp.concatenate([qg_own, qg_other], 0)
    qg_away = [frame_swap(qg_both, phase) for phase in range(2)]

    queries = 4 * CELLS
    tables = [((2 * HALF, TILE, queries), BF16), ((2 * HALF, queries, TILE), BF16)]
    sums_shape = ((2 * HALF, 8, queries), F32)

    def kept(groups):
        mid = ((HALF, groups * 2 * CELLS, queries), F32)
        left = ((HALF, groups * CELLS, 2 * CELLS), F32)
        return [mid, mid, left, left]

    turned, weights, backward, sums, *own_kept = kernel_call(
        functools.partial(own_score_kernel, rows), "own_score",
        [((3, head_width, width), BF16)] + tables + [sums_shape] + kept(rows),
        [scales, qkv_weight, qg_both, *kv_rows], micros=1.5,
    )
    siblings = jnp.stack([kv[2] for kv in kv_rows + kv_away], 0)
    siblings = pair_swap(siblings, "lon", 0)
    sums, *away_kept = kernel_call(
        functools.partial(away_score_kernel, rows), "away_score",
        [sums_shape] + kept(2 * rows), [scales, weights, sums, *kv_away],
        micros=20.0,
    )
    half_part = (rows, CELLS, PAIR_WIDTH)
    sibling_part, stats, dq_sibling = kernel_call(
        functools.partial(sibling_kernel, rows), "sibling",
        [(half_part, F32), ((2 * HALF, queries), F32), ((HALF_WIDTH, 2 * CELLS), F32)],
        [scales, weights, backward, sums, siblings], micros=1.5,
    )
    near_stats, far_stats = frame_swap(stats, 0), frame_swap(stats, 1)
    cross_mid = ((2, HALF, rows * 2 * CELLS, queries), F32)
    cross_side = ((2, 2, HALF, rows * CELLS, 2 * CELLS), F32)
    cross_backward, e_mid, p_mid, e_side, p_side = kernel_call(
        functools.partial(cross_score_kernel, rows), "cross_score",
        [((2,) + tables[1][0], BF16), cross_mid, cross_mid, cross_side, cross_side],
        [scales, *qg_away, *kv_rows, siblings], micros=2.0,
        scratch=[pltpu.VMEM((2,) + tables[0][0], BF16)],
    )
    part = (rows, blocks + 1, CELLS, PAIR_WIDTH)
    packed = (CELLS, 2 * HALF_WIDTH)
    own_part, dq_own, dq_other = kernel_call(
        functools.partial(own_back_kernel, rows), "own_back",
        [(part, F32), (packed, F32), (packed, BF16)],
        [scales, stats, backward, *own_kept, *away_kept, dq_sibling, *kv_rows, *kv_away],
        micros=2.0,
        scratch=[
            pltpu.VMEM((HALF, 3 * rows * 2 * CELLS, queries), BF16),
            pltpu.VMEM((HALF, 3 * rows * CELLS, 2 * CELLS), BF16),
        ],
    )
    (sibling_part,) = kernel_call(
        functools.partial(cross_sibling_kernel, rows), "cross_sibling", [(half_part, BF16)],
        [scales, near_stats, far_stats, cross_backward, e_side, p_side, sibling_part],
        micros=0.5,
    )
    sibling_part = pair_swap(sibling_part, "lon", 0)
    (total,) = kernel_call(
        functools.partial(cross_back_kernel, rows), "cross_back", [(part, F32)],
        [scales, near_stats, far_stats, cross_backward, e_mid, p_mid, e_side, p_side,
         own_part],
        micros=1.5,
    )
    if wide:
        total = total.at[:, blocks].add(sibling_part.astype(F32))
        sibling_part = jnp.zeros_like(sibling_part)
        to_odd = shift_by(total[2].astype(BF16), "lat", -2).astype(F32)
        to_even = shift_by(total[3].astype(BF16), "lat", 2).astype(F32)
        total = total[:2] + jnp.stack(
            [jnp.where(upper, to_odd, to_even), jnp.where(upper, to_even, to_odd)], 0
        )
    inner, to_lat, edge, corner = kernel_call(
        column_out_kernel, "column_out",
        [((blocks, CELLS, PAIR_WIDTH), F32), ((blocks + 1, CELLS, PAIR_WIDTH), BF16),
         edge_shape, edge_shape],
        [total, sibling_part, dq_other],
    )
    edge = pair_swap(edge, "lon", 1)
    corner = corner_swap(corner)
    other = pair_swap(to_lat, "lat", 0)
    (grad_tokens,) = kernel_call(
        finish_kernel, "finish", [(tokens.shape, BF16)],
        [inner, dq_own, other, edge, corner, query_raw, query_inverse, key_raw, key_inverse,
         x, order, norm_gain, turned],
        micros=2.0,
    )
    return grad_tokens


def solution(mesh):
    in_specs = (
        P("tm", "lat", "lon", None),
        P("tm", "lat", "lon"),
        P(),
        P(),
        P(),
        P(),
        P("tm", "lat", "lon", None),
    )
    out_specs = P("tm", "lat", "lon", None)
    return jax.shard_map(
        per_device, mesh=mesh, in_specs=in_specs, out_specs=out_specs, check_vma=False
    )
```

```python
import functools
import math

import jax
import jax.numpy as jnp
from jax import lax
from jax.experimental import pallas as pl
from jax.experimental.pallas import tpu as pltpu
from jax.sharding import PartitionSpec as P

HEADS = 6
HEAD_DIM = 64
BLOCK = 4
CELLS = BLOCK * BLOCK * BLOCK
HALF = HEADS // 2
HALF_WIDTH = HALF * HEAD_DIM
PAIR_WIDTH = 2 * HALF_WIDTH
TILE = 2 * HEAD_DIM
TILES = PAIR_WIDTH // TILE
DEAD_KEY = 64.0
DROPPED = -1e30
FLOPS_PER_US = 1e9

EPS = 1e-06
F32 = jnp.float32
BF16 = jnp.bfloat16


def partner_of(device, count, phase):
    return device + 1 if device % 2 == phase else device - 1


def pair_swap(array, axis, phase):
    count = lax.axis_size(axis)
    pairs = [(device, partner_of(device, count, phase) % count) for device in range(count)]
    return lax.ppermute(array, axis, pairs)


def frame_swap(array, phase):
    frames, lons = lax.axis_size("tm"), lax.axis_size("lon")
    pairs = []
    for frame in range(frames):
        for lon in range(lons):
            to = (partner_of(frame, frames, phase), lon)
            if not 0 <= to[0] < frames:
                to = (frame, partner_of(lon, lons, 0))
            pairs.append((frame * lons + lon, to[0] * lons + to[1]))
    return lax.ppermute(array, ("tm", "lon"), pairs)


def corner_swap(array):
    lats, lons = lax.axis_size("lat"), lax.axis_size("lon")
    pairs = []
    for lat in range(lats):
        for lon in range(lons):
            to = partner_of(lat, lats, 0) * lons + partner_of(lon, lons, 1) % lons
            pairs.append((lat * lons + lon, to))
    return lax.ppermute(array, ("lat", "lon"), pairs)


def shift_by(array, axis, step):
    count = lax.axis_size(axis)
    pairs = [(i, i + step) for i in range(count) if 0 <= i + step < count]
    return lax.ppermute(array, axis, pairs)


def dot(a, b):
    return lax.dot_general(a, b, (((1,), (0,)), ((), ())), preferred_element_type=F32)


def dot_last(a, b):
    return lax.dot_general(a, b, (((1,), (1,)), ((), ())), preferred_element_type=F32)


def dot_first(a, b):
    return lax.dot_general(a, b, (((0,), (0,)), ((), ())), preferred_element_type=F32)


def head_means(values):
    rows = lax.broadcasted_iota(jnp.int32, (TILE, TILE), 0) // HEAD_DIM
    cols = lax.broadcasted_iota(jnp.int32, (TILE, TILE), 1) // HEAD_DIM
    ones = (rows == cols).astype(F32).astype(BF16)
    high = values.astype(BF16)
    low = (values - high.astype(F32)).astype(BF16)
    pieces = []
    for start in range(0, values.shape[1], TILE):
        cut = slice(start, min(start + TILE, values.shape[1]))
        square = ones[: cut.stop - start, : cut.stop - start]
        pieces.append(dot(high[:, cut], square) + dot(low[:, cut], square))
    return jnp.concatenate(pieces, 1) * (1.0 / HEAD_DIM)


def block_order(lat_rows, lon_cols, count, parity):
    blocks = lon_cols // BLOCK
    row = lax.broadcasted_iota(jnp.int32, (count, count), 0)
    source = lax.broadcasted_iota(jnp.int32, (count, count), 1)
    slot = row // CELLS
    place = row % CELLS
    frame = place // (BLOCK * BLOCK)
    lat = (place // BLOCK) % BLOCK
    col = place % BLOCK
    block = jnp.where(parity == 1, blocks - 1 - slot, slot)
    wanted = (frame * lat_rows + lat) * lon_cols + block * BLOCK + col
    return (source == wanted).astype(F32).astype(BF16)


def halves(first, second):
    low = jnp.concatenate([first[:, :HALF_WIDTH], second[:, :HALF_WIDTH]], 1)
    high = jnp.concatenate([first[:, HALF_WIDTH:], second[:, HALF_WIDTH:]], 1)
    return low, high


def normalised(x, gain_ref):
    inverse = lax.rsqrt(jnp.mean(x * x, -1, keepdims=True) + EPS)
    return (x * inverse * gain_ref[...].reshape(1, x.shape[1])).astype(BF16)


def order_kernel(tokens_ref, order_ref, x_ref):
    frames, lat_rows, lon_cols, width = tokens_ref.shape
    cells = frames * lat_rows * lon_cols
    order = block_order(lat_rows, lon_cols, cells, lax.rem(lax.axis_index("lon"), 2))
    order_ref[...] = order
    x = dot(order, tokens_ref[...].astype(F32).reshape(cells, width).astype(BF16)).astype(BF16)
    x_ref[...] = x


def key_value_kernel(
    count_ref, x_ref, gain_ref, qkv_ref,
    kv_own_ref, kv_other_ref, edge_ref, normed_ref, raw_ref, inverse_ref,
):
    cells = x_ref.shape[0]
    blocks = cells // CELLS
    parity = lax.rem(lax.axis_index("lon"), 2)
    upper = lax.rem(lax.axis_index("lat"), 2) == 1
    normed = normalised(x_ref[...].astype(F32), gain_ref)
    normed_ref[...] = normed
    key, value = dot(normed, qkv_ref[1]), dot(normed, qkv_ref[2])
    raw_ref[...] = key
    inverse = lax.rsqrt(head_means(key * key) + EPS)
    inverse_ref[...] = inverse
    place = lax.broadcasted_iota(jnp.int32, (CELLS, 1), 0)
    counts = count_ref[0]
    live = []
    for slot in range(blocks):
        flip = blocks - 1 - slot
        live.append(
            place
            < jnp.where(parity == 1, counts[:, flip : flip + 1], counts[:, slot : slot + 1])
        )
    key = jnp.where(jnp.concatenate(live, 0), key * inverse, DEAD_KEY)
    shape = (blocks, CELLS, PAIR_WIDTH)
    low, high = halves(key, value)
    kv_own_ref[...] = jnp.where(upper, high, low).astype(BF16).reshape(shape)
    kv_other_ref[...] = jnp.where(upper, low, high).astype(BF16).reshape(shape)
    edge_ref[...] = kv_own_ref[0]


def query_grad_kernel(
    scale_in, order_ref, normed_ref, grad_ref, qkv_ref, out_weight_ref, kv_other_ref,
    qg_own_ref, qg_other_ref, corner_ref, raw_ref, inverse_ref, scale_ref,
):
    corner_ref[...] = kv_other_ref[0]
    cells, width = normed_ref.shape
    upper = lax.rem(lax.axis_index("lat"), 2) == 1
    all_scales = scale_in[...].reshape(1, HEADS) * (1.0 / math.sqrt(HEAD_DIM))
    for h in range(HALF):
        mine = jnp.where(
            upper, all_scales[:, HALF + h : HALF + h + 1], all_scales[:, h : h + 1]
        )
        scale_ref[h : h + 1] = jnp.broadcast_to(mine, (1, 4 * CELLS))
    query = dot(normed_ref[...], qkv_ref[0])
    raw_ref[...] = query
    inverse = lax.rsqrt(head_means(query * query) + EPS)
    inverse_ref[...] = inverse
    grad = dot_last(
        grad_ref[...].astype(F32).reshape(cells, width).astype(BF16), out_weight_ref[...]
    ).astype(BF16)
    low, high = halves(query * inverse, dot(order_ref[...], grad))
    shape = (cells // CELLS, CELLS, PAIR_WIDTH)
    qg_own_ref[...] = jnp.where(upper, high, low).astype(BF16).reshape(shape)
    qg_other_ref[...] = jnp.where(upper, low, high).astype(BF16).reshape(shape)


def join_kernel(kv_in, kv_ref):
    kv_ref[...] = kv_in[...]


def lane_tile(j):
    return slice((j // 2) * TILE, (j // 2 + 1) * TILE)


class Place:
    def __init__(self, rows):
        self.rows = rows
        tm, frames = lax.axis_index("tm"), lax.axis_size("tm")
        odd = lax.rem(tm, 2) == 1
        near, far = jnp.where(odd, tm - 1, tm + 1), jnp.where(odd, tm + 1, tm - 1)
        self.there = [None] + [((at >= 0) & (at < frames)) for at in (near, far)]
        self.upper = lax.rem(lax.axis_index("lat"), 2)

    def bias(self, frame, row, lanes):
        there = self.there[frame]
        total = 0.0 if there is None else jnp.where(there, 0.0, DROPPED)
        if row < 2:
            return total
        pair, pairs = lax.axis_index("lat") // 2, lax.axis_size("lat") // 2
        if row == 2:
            inside, wanted = pair > 0, self.upper
        else:
            inside, wanted = pair < pairs - 1, 1 - self.upper
        lane_row = (lax.broadcasted_iota(jnp.int32, (1, lanes), 1) // CELLS) % 2
        seen = (lane_row == wanted) & inside
        return total + jnp.where(seen, 0.0, DROPPED)


def head_scales(scale_ref, lanes):
    return [scale_ref[h : h + 1, lanes] for h in range(HALF)]


def key_bias(keys):
    return jnp.where(keys[:, 0:1].astype(F32) < 0.5 * DEAD_KEY, 0.0, DROPPED)


def score(keys, bias, weights_ref, lanes, scale_ref, sums):
    to_exp2 = [s * math.log2(math.e) for s in head_scales(scale_ref, lanes)]
    count = keys.shape[0]
    exps, probs = [], []
    for h in range(HALF):
        scores = dot(keys[:, lane_tile(h)], weights_ref[h, :, lanes])
        grad_prob = dot(keys[:, lane_tile(HALF + h)], weights_ref[HALF + h, :, lanes])
        masked = jnp.exp2(scores * to_exp2[h] + bias)
        if sums is not None:
            shape = (count // 8, 8, masked.shape[1])
            sums[h] = sums[h] + jnp.sum(masked.reshape(shape), 0)
            inner = (masked * grad_prob).reshape(shape)
            sums[HALF + h] = sums[HALF + h] + jnp.sum(inner, 0)
        exps.append(masked)
        probs.append(grad_prob)
    return exps, probs


ALL = slice(0, 4 * CELLS)
FIRST = slice(0, 2 * CELLS)
LAST = slice(2 * CELLS, 4 * CELLS)


def score_groups(place, groups, kv_refs, weights_ref, scale_ref, sums, e_mid, p_mid, e_left, p_left):
    side = [jnp.zeros((8, 2 * CELLS), F32) for _ in range(2 * HALF)]
    for index, (group, ref) in enumerate(zip(groups, kv_refs)):
        keys = ref[1:3].reshape(2 * CELLS, PAIR_WIDTH)
        bias = key_bias(keys) + place.bias(*group, 4 * CELLS)
        exps, probs = score(keys, bias, weights_ref, ALL, scale_ref, sums)
        for h in range(HALF):
            e_mid[h, index * 2 * CELLS : (index + 1) * 2 * CELLS] = exps[h]
            p_mid[h, index * 2 * CELLS : (index + 1) * 2 * CELLS] = probs[h]
    for index in range(0, len(kv_refs), 2):
        pair = [kv_refs[index][0], kv_refs[index + 1][0]]
        bias = side_bias(place, groups[index : index + 2], pair)
        keys = jnp.concatenate(pair, 0)
        exps, probs = score(keys, bias, weights_ref, FIRST, scale_ref, side)
        for h in range(HALF):
            e_left[h, index * CELLS : (index + 2) * CELLS] = exps[h]
            p_left[h, index * CELLS : (index + 2) * CELLS] = probs[h]
    return [jnp.concatenate([a[:, FIRST] + b, a[:, LAST]], 1) for a, b in zip(sums, side)]


def side_bias(place, groups, keys):
    return jnp.concatenate(
        [
            jnp.broadcast_to(
                key_bias(keys[i]) + place.bias(*groups[i], 2 * CELLS), (CELLS, 2 * CELLS)
            )
            for i in range(2)
        ],
        0,
    )


def away_groups(rows):
    return [(1, 0), (2, 0)], [(frame, row) for frame in (1, 2) for row in range(1, rows)]


def query_tables(qg_ref, weights, backward):
    rows = jnp.concatenate([qg_ref[0], qg_ref[2], qg_ref[1], qg_ref[3]], 0).astype(F32)
    cols = rows.T
    count = rows.shape[0]
    lane_half = lax.broadcasted_iota(jnp.int32, (count, TILE), 1) // HEAD_DIM
    row_half = lax.broadcasted_iota(jnp.int32, (TILE, count), 0) // HEAD_DIM
    for j in range(2 * HALF):
        backward[j] = jnp.where(lane_half == j % 2, rows[:, lane_tile(j)], 0.0).astype(BF16)
        weights[j] = jnp.where(row_half == j % 2, cols[lane_tile(j)], 0.0).astype(BF16)


def own_score_kernel(rows, scale_ref, qkv_ref, qg_ref, *refs):
    kv_refs, refs = refs[:rows], refs[rows:]
    turned_ref, weights, backward, sums_ref, e_mid, p_mid, e_left, p_left = refs
    for c in range(3):
        turned_ref[c] = qkv_ref[c].T
    queries = 4 * CELLS
    query_tables(qg_ref, weights, backward)
    sums = [jnp.zeros((8, queries), F32) for _ in range(2 * HALF)]
    sums = score_groups(
        Place(rows), [(0, row) for row in range(rows)], kv_refs, weights, scale_ref, sums,
        e_mid, p_mid, e_left, p_left,
    )
    for j in range(2 * HALF):
        sums_ref[j] = sums[j]


def away_score_kernel(rows, part, scale_ref, weights, sums_in, *refs):
    groups = away_groups(rows)[part]
    kv_refs, refs = refs[: len(groups)], refs[len(groups) :]
    sums_ref, e_mid, p_mid, e_left, p_left = refs
    sums = [sums_in[j] for j in range(2 * HALF)]
    sums = score_groups(
        Place(rows), groups, kv_refs, weights, scale_ref, sums, e_mid, p_mid, e_left, p_left
    )
    for j in range(2 * HALF):
        sums_ref[j] = sums[j]


def grad_parts(exps, probs, inverse, delta, scales):
    grads, halves_of = [], []
    for h in range(HALF):
        prob = exps[h] * inverse[h]
        halves_of.append(prob.astype(BF16))
        grads.append((prob * (probs[h] - delta[h]) * scales[h]).astype(BF16))
    return grads + halves_of


def key_grads(pieces, backward, lanes):
    outs = []
    for tile in range(TILES):
        both = jnp.concatenate([pieces[2 * tile], pieces[2 * tile + 1]], 1)
        rows = jnp.concatenate(
            [backward[2 * tile, lanes], backward[2 * tile + 1, lanes]], 0
        )
        outs.append(dot(both, rows))
    return jnp.concatenate(outs, 1)


def query_grads(keys, grads, h):
    own = slice((h % 2) * HEAD_DIM, (h % 2 + 1) * HEAD_DIM)
    return dot_first(keys[:, lane_tile(h)], grads)[own]


def sibling_kernel(
    rows, scale_ref, weights, backward, sums_in, early_ref, late_ref, part_ref, stats_ref, dq_ref
):
    place = Place(rows)
    side = [jnp.zeros((8, 2 * CELLS), F32) for _ in range(2 * HALF)]
    first, second = away_groups(rows)
    groups = [(0, row) for row in range(rows)] + first + second
    pairs = [early_ref[i : i + 2] for i in range(0, rows + 2, 2)]
    pairs += [late_ref[i : i + 2] for i in range(0, len(second), 2)]
    made = []
    for index, pair in enumerate(pairs):
        bias = side_bias(place, groups[2 * index : 2 * index + 2], pair)
        keys = pair.reshape(2 * CELLS, PAIR_WIDTH)
        made.append(score(keys, bias, weights, LAST, scale_ref, side))
    inverse, delta = [], []
    for h in range(HALF):
        total, inner = (
            jnp.concatenate([sums_in[j, :, FIRST], sums_in[j, :, LAST] + side[j]], 1)
            for j in (h, HALF + h)
        )
        inverse.append(1.0 / jnp.sum(total, 0, keepdims=True))
        delta.append(jnp.sum(inner, 0, keepdims=True) * inverse[h])
        stats_ref[h : h + 1] = inverse[h]
        stats_ref[HALF + h : HALF + h + 1] = delta[h]
    inverse = [a[:, LAST] for a in inverse]
    delta = [a[:, LAST] for a in delta]
    scales = head_scales(scale_ref, LAST)
    grads = []
    for index in range(0, 3 * rows, 2):
        pieces = grad_parts(*made[index // 2], inverse, delta, scales)
        grads.append(pieces[:HALF])
        if index < rows:
            part = key_grads(pieces, backward, LAST)
            part_ref[index : index + 2] = part.reshape(2, CELLS, PAIR_WIDTH)
    keys = jnp.concatenate(pairs, 0).reshape(3 * rows * CELLS, PAIR_WIDTH)
    for h in range(HALF):
        dq_ref[h * HEAD_DIM : (h + 1) * HEAD_DIM] = query_grads(
            keys, jnp.concatenate([g[h] for g in grads], 0), h
        )


def cross_score_kernel(rows, scale_ref, *refs):
    qg_refs, refs = refs[:2], refs[2:]
    kv_refs, sibling_ref, refs = refs[:rows], refs[rows], refs[rows + 1 :]
    backward, e_mid, p_mid, e_side, p_side, weights = refs
    place = Place(rows)
    for side in range(2):
        query_tables(qg_refs[side], weights.at[side], backward.at[side])
    for row in range(rows):
        keys = kv_refs[row][1:3].reshape(2 * CELLS, PAIR_WIDTH)
        bias = key_bias(keys) + place.bias(0, row, 4 * CELLS)
        at = slice(row * 2 * CELLS, (row + 1) * 2 * CELLS)
        for side in range(2):
            exps, probs = score(keys, bias, weights.at[side], ALL, scale_ref, None)
            for h in range(HALF):
                e_mid[side, h, at] = exps[h]
                p_mid[side, h, at] = probs[h]
    for row in range(0, rows, 2):
        at = slice(row * CELLS, (row + 2) * CELLS)
        for edge, lanes in ((0, FIRST), (1, LAST)):
            if edge == 0:
                pair = [kv_refs[row][0], kv_refs[row + 1][0]]
            else:
                pair = [sibling_ref[row], sibling_ref[row + 1]]
            bias = side_bias(place, [(0, row), (0, row + 1)], pair)
            keys = jnp.concatenate(pair, 0)
            for side in range(2):
                exps, probs = score(keys, bias, weights.at[side], lanes, scale_ref, None)
                for h in range(HALF):
                    e_side[side, edge, h, at] = exps[h]
                    p_side[side, edge, h, at] = probs[h]


def cross_stats(rows, stats_refs, lanes):
    place = Place(rows)
    both = []
    for side, ref in enumerate(stats_refs):
        there = jnp.where(place.there[1 + side], 1.0, 0.0)
        inverse = [ref[h : h + 1, lanes] * there for h in range(HALF)]
        both.append((inverse, [ref[HALF + h : HALF + h + 1, lanes] for h in range(HALF)]))
    return both


def cross_sibling_kernel(
    rows, scale_ref, near_stats, far_stats, backward, e_side, p_side, part_in, part_ref
):
    scales = head_scales(scale_ref, LAST)
    stats = cross_stats(rows, (near_stats, far_stats), LAST)
    for row in range(0, rows, 2):
        at = slice(row * CELLS, (row + 2) * CELLS)
        total = part_in[row : row + 2].reshape(2 * CELLS, PAIR_WIDTH)
        for side in range(2):
            pieces = grad_parts(
                [e_side[side, 1, h, at] for h in range(HALF)],
                [p_side[side, 1, h, at] for h in range(HALF)],
                *stats[side], scales,
            )
            total = total + key_grads(pieces, backward.at[side], LAST)
        part_ref[row : row + 2] = total.reshape(2, CELLS, PAIR_WIDTH).astype(BF16)


def cross_back_kernel(
    rows, scale_ref, near_stats, far_stats, backward, e_mid, p_mid, e_side, p_side,
    own_ref, total_ref,
):
    scales = head_scales(scale_ref, ALL)
    stats = cross_stats(rows, (near_stats, far_stats), ALL)
    for row in range(rows):
        at = slice(row * 2 * CELLS, (row + 1) * 2 * CELLS)
        total = own_ref[row, 1:3].reshape(2 * CELLS, PAIR_WIDTH)
        for side in range(2):
            pieces = grad_parts(
                [e_mid[side, h, at] for h in range(HALF)],
                [p_mid[side, h, at] for h in range(HALF)],
                *stats[side], scales,
            )
            total = total + key_grads(pieces, backward.at[side], ALL)
        total_ref[row, 1:3] = total.reshape(2, CELLS, PAIR_WIDTH)
    scales = head_scales(scale_ref, FIRST)
    stats = cross_stats(rows, (near_stats, far_stats), FIRST)
    for row in range(0, rows, 2):
        at = slice(row * CELLS, (row + 2) * CELLS)
        total = own_ref[row : row + 2, 0].reshape(2 * CELLS, PAIR_WIDTH)
        for side in range(2):
            pieces = grad_parts(
                [e_side[side, 0, h, at] for h in range(HALF)],
                [p_side[side, 0, h, at] for h in range(HALF)],
                *stats[side], scales,
            )
            total = total + key_grads(pieces, backward.at[side], FIRST)
        total_ref[row : row + 2, 0] = total.reshape(2, CELLS, PAIR_WIDTH)


def own_back_kernel(
    rows, scale_ref, stats_ref, backward, e_mid, p_mid, e_left, p_left,
    first_e_mid, first_p_mid, first_e_left, first_p_left,
    second_e_mid, second_p_mid, second_e_left, second_p_left, dq_sibling, *refs,
):
    kv_refs, refs = refs[: 3 * rows], refs[3 * rows :]
    own_ref, dq_own_ref, dq_other_ref, d_mid, d_left = refs
    scales = head_scales(scale_ref, ALL)
    inverse = [stats_ref[h : h + 1] for h in range(HALF)]
    delta = [stats_ref[HALF + h : HALF + h + 1] for h in range(HALF)]
    for index in range(3 * rows):
        at = slice(index * 2 * CELLS, (index + 1) * 2 * CELLS)
        if index < rows:
            exps, probs, start = e_mid, p_mid, index * 2 * CELLS
        elif index < rows + 2:
            exps, probs, start = first_e_mid, first_p_mid, (index - rows) * 2 * CELLS
        else:
            exps, probs, start = second_e_mid, second_p_mid, (index - rows - 2) * 2 * CELLS
        cut = slice(start, start + 2 * CELLS)
        pieces = grad_parts(
            [exps[h, cut] for h in range(HALF)], [probs[h, cut] for h in range(HALF)],
            inverse, delta, scales,
        )
        for h in range(HALF):
            d_mid[h, at] = pieces[h]
        if index < rows:
            part = key_grads(pieces, backward, ALL)
            own_ref[index, 1:3] = part.reshape(2, CELLS, PAIR_WIDTH)
    scales = head_scales(scale_ref, FIRST)
    inverse = [a[:, FIRST] for a in inverse]
    delta = [a[:, FIRST] for a in delta]
    for index in range(0, 3 * rows, 2):
        at = slice(index * CELLS, (index + 2) * CELLS)
        if index < rows:
            exps, probs, start = e_left, p_left, index * CELLS
        elif index < rows + 2:
            exps, probs, start = first_e_left, first_p_left, (index - rows) * CELLS
        else:
            exps, probs, start = second_e_left, second_p_left, (index - rows - 2) * CELLS
        cut = slice(start, start + 2 * CELLS)
        pieces = grad_parts(
            [exps[h, cut] for h in range(HALF)], [probs[h, cut] for h in range(HALF)],
            inverse, delta, scales,
        )
        for h in range(HALF):
            d_left[h, at] = pieces[h]
        if index < rows:
            part = key_grads(pieces, backward, FIRST)
            own_ref[index : index + 2, 0] = part.reshape(2, CELLS, PAIR_WIDTH)
    mid = jnp.concatenate([ref[1:3].reshape(2 * CELLS, PAIR_WIDTH) for ref in kv_refs], 0)
    left = jnp.concatenate([ref[0] for ref in kv_refs], 0)
    columns = []
    for h in range(HALF):
        made = query_grads(mid, d_mid[h], h)
        first = query_grads(left, d_left[h], h)
        last = dq_sibling[h * HEAD_DIM : (h + 1) * HEAD_DIM]
        columns.append(made + jnp.concatenate([first, last], 1))
    dq = jnp.concatenate(columns, 0).T
    dq_own_ref[...] = jnp.concatenate([dq[:CELLS], dq[2 * CELLS : 3 * CELLS]], 1)
    dq_other_ref[...] = jnp.concatenate([dq[CELLS : 2 * CELLS], dq[3 * CELLS :]], 1).astype(BF16)


def column_out_kernel(total_ref, sibling_ref, dq_other_ref, inner_ref, to_lat_ref, edge_ref, corner_ref):
    inner_ref[0] = total_ref[0, 1]
    inner_ref[1] = total_ref[0, 2] + sibling_ref[0].astype(F32)
    to_lat_ref[0] = total_ref[1, 1].astype(BF16)
    to_lat_ref[2] = dq_other_ref[...]
    to_lat_ref[1] = (total_ref[1, 2] + sibling_ref[1].astype(F32)).astype(BF16)
    edge_ref[...] = total_ref[0, 0].astype(BF16)
    corner_ref[...] = total_ref[1, 0].astype(BF16)


def heads_back(query, inner, edge, raws, inverses, weights):
    pair = jnp.concatenate([inner[0] + edge, inner[1]], 0)
    query = jnp.concatenate([query[:, :HALF_WIDTH], query[:, HALF_WIDTH:]], 0)
    grads = (query, pair[:, :HALF_WIDTH], pair[:, HALF_WIDTH:])
    total = dot(grads[2].astype(BF16), weights[2])
    for c in range(2):
        mean = head_means(raws[c] * grads[c])
        cubed = inverses[c] * inverses[c] * inverses[c]
        grad_raw = inverses[c] * grads[c] - cubed * raws[c] * mean
        total = total + dot(grad_raw.astype(BF16), weights[c])
    return total


def own_finish_kernel(
    inner_ref, dq_ref, edge_ref, query_raw, query_inverse, key_raw, key_inverse, turned_ref,
    total_ref, raws_ref, inverses_ref, weights_ref,
):
    upper = lax.rem(lax.axis_index("lat"), 2) == 1

    def split(array):
        low, high = array[:, :HALF_WIDTH], array[:, HALF_WIDTH:]
        return jnp.where(upper, high, low), jnp.where(upper, low, high)

    raws, other_raws = zip(split(query_raw[...]), split(key_raw[...]))
    inverses, other_inverses = zip(split(query_inverse[...]), split(key_inverse[...]))
    weights = []
    for c in range(3):
        low, high = turned_ref[c, :HALF_WIDTH], turned_ref[c, HALF_WIDTH:]
        weights.append(jnp.where(upper, high, low))
        weights_ref[c] = jnp.where(upper, low, high)
    for c in range(2):
        raws_ref[c] = other_raws[c]
        inverses_ref[c] = other_inverses[c]
    total_ref[...] = heads_back(
        dq_ref[...], inner_ref[...], edge_ref[...].astype(F32), raws, inverses, weights
    )


def finish_kernel(
    total_ref, other_ref, corner_ref, raws_ref, inverses_ref, weights_ref,
    x_ref, order_ref, gain_ref, out_ref,
):
    grad_normed = total_ref[...] + heads_back(
        other_ref[2].astype(F32), other_ref[:2].astype(F32), corner_ref[...].astype(F32),
        (raws_ref[0], raws_ref[1]), (inverses_ref[0], inverses_ref[1]), weights_ref,
    )
    order = order_ref[...]
    x = x_ref[...].astype(F32)
    inverse = lax.rsqrt(jnp.mean(x * x, -1, keepdims=True) + EPS)
    grad = gain_ref[...].reshape(1, x.shape[1]) * grad_normed
    mean = jnp.mean(x * grad, -1, keepdims=True)
    grad = (inverse * grad - inverse * inverse * inverse * x * mean).astype(BF16)
    out_ref[...] = dot_first(order, grad).reshape(out_ref.shape).astype(BF16)


VMEM = pl.BlockSpec(memory_space=pltpu.VMEM)


def kernel_call(
    body, name, outs, args, scratch=(), limit_mib=16, micros=1.0
):
    return pl.pallas_call(
        body,
        name=name,
        out_shape=[jax.ShapeDtypeStruct(shape, dtype) for shape, dtype in outs],
        in_specs=[VMEM] * len(args),
        out_specs=[VMEM] * len(outs),
        scratch_shapes=list(scratch),
        compiler_params=pltpu.CompilerParams(vmem_limit_bytes=limit_mib * 1024 * 1024),
        cost_estimate=pl.CostEstimate(
            flops=int(micros * FLOPS_PER_US), bytes_accessed=0, transcendentals=0
        ),
    )(*args)


def per_device(tokens, key_count, norm_gain, qkv_weight, out_weight, logit_scale, grad_out):
    frames, lat_rows, lon_cols, width = tokens.shape
    assert frames == BLOCK and lat_rows == BLOCK and lon_cols == 2 * BLOCK
    assert lax.axis_size("lat") % 2 == 0 and lax.axis_size("lon") % 2 == 0
    cells = frames * lat_rows * lon_cols
    blocks = lon_cols // BLOCK
    head_width = HEADS * HEAD_DIM
    qg_shape = ((blocks, CELLS, PAIR_WIDTH), BF16)
    edge_shape = ((CELLS, PAIR_WIDTH), BF16)

    order, x = kernel_call(
        order_kernel, "order", [((cells, cells), BF16), ((cells, width), BF16)], [tokens],
        micros=10.0,
    )
    projected = ((cells, head_width), F32)
    kv_own, kv_other, edge, normed, key_raw, key_inverse = kernel_call(
        key_value_kernel, "key_value",
        [qg_shape, qg_shape, edge_shape, ((cells, width), BF16), projected, projected],
        [key_count, x, norm_gain, qkv_weight], micros=2.0,
    )
    edge = pair_swap(edge, "lon", 1)
    kv_made, kv_other = kv_other, pair_swap(kv_other, "lat", 0)
    qg_own, qg_other, corner, query_raw, query_inverse, scales = kernel_call(
        query_grad_kernel, "query_grad",
        [qg_shape, qg_shape, edge_shape, projected, projected, ((HALF, 4 * CELLS), F32)],
        [logit_scale, order, normed, grad_out, qkv_weight, out_weight, kv_made], micros=5.0,
    )
    corner = corner_swap(corner)
    qg_other = pair_swap(qg_other, "lat", 0)
    (kv_other,) = kernel_call(join_kernel, "join", [qg_shape], [kv_other], micros=3.0)
    kv_rows = [
        jnp.concatenate([edge[None], kv_own], 0),
        jnp.concatenate([corner[None], kv_other], 0),
    ]
    upper = lax.rem(lax.axis_index("lat"), 2) == 1
    wide = lax.axis_size("lat") > 2
    if wide:
        even = jnp.where(upper, kv_rows[1], kv_rows[0])
        odd = jnp.where(upper, kv_rows[0], kv_rows[1])
        kv_rows += [shift_by(odd, "lat", 2), shift_by(even, "lat", -2)]
    rows = len(kv_rows)
    kv_away = [frame_swap(kv, phase) for phase in range(2) for kv in kv_rows]
    qg_both = jnp.concatenate([qg_own, qg_other], 0)
    qg_away = [frame_swap(qg_both, phase) for phase in range(2)]

    queries = 4 * CELLS
    tables = [((2 * HALF, TILE, queries), BF16), ((2 * HALF, queries, TILE), BF16)]
    sums_shape = ((2 * HALF, 8, queries), F32)

    def kept(groups):
        mid = ((HALF, groups * 2 * CELLS, queries), F32)
        left = ((HALF, groups * CELLS, 2 * CELLS), F32)
        return [mid, mid, left, left]

    turned, weights, backward, sums, *own_kept = kernel_call(
        functools.partial(own_score_kernel, rows), "own_score",
        [((3, head_width, width), BF16)] + tables + [sums_shape] + kept(rows),
        [scales, qkv_weight, qg_both, *kv_rows], micros=1.5,
    )
    kv_parts = [[kv_away[(frame - 1) * rows + row] for frame, row in part]
                for part in away_groups(rows)]
    early = pair_swap(jnp.stack([kv[2] for kv in kv_rows + kv_parts[0]], 0), "lon", 0)
    late = pair_swap(jnp.stack([kv[2] for kv in kv_parts[1]], 0), "lon", 0)
    away_kept = []
    for which, kvs in enumerate(kv_parts):
        sums, *made = kernel_call(
            functools.partial(away_score_kernel, rows, which), "away_score",
            [sums_shape] + kept(len(kvs)), [scales, weights, sums, *kvs],
            micros=(1.5, 20.0)[which],
        )
        away_kept += made
    half_part = (rows, CELLS, PAIR_WIDTH)
    sibling_part, stats, dq_sibling = kernel_call(
        functools.partial(sibling_kernel, rows), "sibling",
        [(half_part, F32), ((2 * HALF, queries), F32), ((HALF_WIDTH, 2 * CELLS), F32)],
        [scales, weights, backward, sums, early, late], micros=1.5,
    )
    near_stats, far_stats = frame_swap(stats, 0), frame_swap(stats, 1)
    cross_mid = ((2, HALF, rows * 2 * CELLS, queries), F32)
    cross_side = ((2, 2, HALF, rows * CELLS, 2 * CELLS), F32)
    cross_backward, e_mid, p_mid, e_side, p_side = kernel_call(
        functools.partial(cross_score_kernel, rows), "cross_score",
        [((2,) + tables[1][0], BF16), cross_mid, cross_mid, cross_side, cross_side],
        [scales, *qg_away, *kv_rows, early], micros=2.0,
        scratch=[pltpu.VMEM((2,) + tables[0][0], BF16)],
    )
    part = (rows, blocks + 1, CELLS, PAIR_WIDTH)
    packed = (CELLS, 2 * HALF_WIDTH)
    own_part, dq_own, dq_other = kernel_call(
        functools.partial(own_back_kernel, rows), "own_back",
        [(part, F32), (packed, F32), (packed, BF16)],
        [scales, stats, backward, *own_kept, *away_kept, dq_sibling, *kv_rows,
         *kv_parts[0], *kv_parts[1]],
        micros=2.0,
        scratch=[
            pltpu.VMEM((HALF, 3 * rows * 2 * CELLS, queries), BF16),
            pltpu.VMEM((HALF, 3 * rows * CELLS, 2 * CELLS), BF16),
        ],
    )
    (sibling_part,) = kernel_call(
        functools.partial(cross_sibling_kernel, rows), "cross_sibling", [(half_part, BF16)],
        [scales, near_stats, far_stats, cross_backward, e_side, p_side, sibling_part],
        micros=0.5,
    )
    sibling_part = pair_swap(sibling_part, "lon", 0)
    (total,) = kernel_call(
        functools.partial(cross_back_kernel, rows), "cross_back", [(part, F32)],
        [scales, near_stats, far_stats, cross_backward, e_mid, p_mid, e_side, p_side,
         own_part],
        micros=1.5,
    )
    if wide:
        total = total.at[:, blocks].add(sibling_part.astype(F32))
        sibling_part = jnp.zeros_like(sibling_part)
        to_odd = shift_by(total[2].astype(BF16), "lat", -2).astype(F32)
        to_even = shift_by(total[3].astype(BF16), "lat", 2).astype(F32)
        total = total[:2] + jnp.stack(
            [jnp.where(upper, to_odd, to_even), jnp.where(upper, to_even, to_odd)], 0
        )
    inner, to_lat, edge, corner = kernel_call(
        column_out_kernel, "column_out",
        [((blocks, CELLS, PAIR_WIDTH), F32), ((blocks + 1, CELLS, PAIR_WIDTH), BF16),
         edge_shape, edge_shape],
        [total, sibling_part, dq_other],
    )
    edge = pair_swap(edge, "lon", 1)
    corner = corner_swap(corner)
    other = pair_swap(to_lat, "lat", 0)
    halved = ((2, cells, HALF_WIDTH), F32)
    summed, raws, inverses, weights = kernel_call(
        own_finish_kernel, "own_finish",
        [((cells, width), F32), halved, halved, ((3, HALF_WIDTH, width), BF16)],
        [inner, dq_own, edge, query_raw, query_inverse, key_raw, key_inverse, turned],
        micros=1.0,
    )
    (grad_tokens,) = kernel_call(
        finish_kernel, "finish", [(tokens.shape, BF16)],
        [summed, other, corner, raws, inverses, weights, x, order, norm_gain], micros=2.0,
    )
    return grad_tokens


def solution(mesh):
    in_specs = (
        P("tm", "lat", "lon", None),
        P("tm", "lat", "lon"),
        P(),
        P(),
        P(),
        P(),
        P("tm", "lat", "lon", None),
    )
    out_specs = P("tm", "lat", "lon", None)
    return jax.shard_map(
        per_device, mesh=mesh, in_specs=in_specs, out_specs=out_specs, check_vma=False
    )
```

```python
import functools
import math

import jax
import jax.numpy as jnp
from jax import lax
from jax.experimental import pallas as pl
from jax.experimental.pallas import tpu as pltpu
from jax.sharding import PartitionSpec as P

HEADS = 6
HEAD_DIM = 64
BLOCK = 4
CELLS = BLOCK * BLOCK * BLOCK
HALF = HEADS // 2
HALF_WIDTH = HALF * HEAD_DIM
PAIR_WIDTH = 2 * HALF_WIDTH
TILE = 2 * HEAD_DIM
TILES = PAIR_WIDTH // TILE
DEAD_KEY = 64.0
DROPPED = -1e30
FLOPS_PER_US = 1e9

EPS = 1e-06
F32 = jnp.float32
BF16 = jnp.bfloat16


def partner_of(device, count, phase):
    return device + 1 if device % 2 == phase else device - 1


def pair_swap(array, axis, phase):
    count = lax.axis_size(axis)
    pairs = [(device, partner_of(device, count, phase) % count) for device in range(count)]
    return lax.ppermute(array, axis, pairs)


def frame_swap(array, phase):
    frames, lons = lax.axis_size("tm"), lax.axis_size("lon")
    pairs = []
    for frame in range(frames):
        for lon in range(lons):
            to = (partner_of(frame, frames, phase), lon)
            if not 0 <= to[0] < frames:
                to = (frame, partner_of(lon, lons, 0))
            pairs.append((frame * lons + lon, to[0] * lons + to[1]))
    return lax.ppermute(array, ("tm", "lon"), pairs)


def corner_swap(array):
    lats, lons = lax.axis_size("lat"), lax.axis_size("lon")
    pairs = []
    for lat in range(lats):
        for lon in range(lons):
            to = partner_of(lat, lats, 0) * lons + partner_of(lon, lons, 1) % lons
            pairs.append((lat * lons + lon, to))
    return lax.ppermute(array, ("lat", "lon"), pairs)


def shift_by(array, axis, step):
    count = lax.axis_size(axis)
    pairs = [(i, i + step) for i in range(count) if 0 <= i + step < count]
    return lax.ppermute(array, axis, pairs)


def dot(a, b):
    return lax.dot_general(a, b, (((1,), (0,)), ((), ())), preferred_element_type=F32)


def dot_last(a, b):
    return lax.dot_general(a, b, (((1,), (1,)), ((), ())), preferred_element_type=F32)


def dot_first(a, b):
    return lax.dot_general(a, b, (((0,), (0,)), ((), ())), preferred_element_type=F32)


def head_means(values):
    rows = lax.broadcasted_iota(jnp.int32, (TILE, TILE), 0) // HEAD_DIM
    cols = lax.broadcasted_iota(jnp.int32, (TILE, TILE), 1) // HEAD_DIM
    ones = (rows == cols).astype(F32).astype(BF16)
    high = values.astype(BF16)
    low = (values - high.astype(F32)).astype(BF16)
    pieces = []
    for start in range(0, values.shape[1], TILE):
        cut = slice(start, min(start + TILE, values.shape[1]))
        square = ones[: cut.stop - start, : cut.stop - start]
        pieces.append(dot(high[:, cut], square) + dot(low[:, cut], square))
    return jnp.concatenate(pieces, 1) * (1.0 / HEAD_DIM)


def block_order(lat_rows, lon_cols, count, parity):
    blocks = lon_cols // BLOCK
    row = lax.broadcasted_iota(jnp.int32, (count, count), 0)
    source = lax.broadcasted_iota(jnp.int32, (count, count), 1)
    slot = row // CELLS
    place = row % CELLS
    frame = place // (BLOCK * BLOCK)
    lat = (place // BLOCK) % BLOCK
    col = place % BLOCK
    block = jnp.where(parity == 1, blocks - 1 - slot, slot)
    wanted = (frame * lat_rows + lat) * lon_cols + block * BLOCK + col
    return (source == wanted).astype(F32).astype(BF16)


def halves(first, second):
    low = jnp.concatenate([first[:, :HALF_WIDTH], second[:, :HALF_WIDTH]], 1)
    high = jnp.concatenate([first[:, HALF_WIDTH:], second[:, HALF_WIDTH:]], 1)
    return low, high


def normalised(x, gain_ref):
    inverse = lax.rsqrt(jnp.mean(x * x, -1, keepdims=True) + EPS)
    return (x * inverse * gain_ref[...].reshape(1, x.shape[1])).astype(BF16)


def order_kernel(tokens_ref, order_ref, x_ref):
    frames, lat_rows, lon_cols, width = tokens_ref.shape
    cells = frames * lat_rows * lon_cols
    order = block_order(lat_rows, lon_cols, cells, lax.rem(lax.axis_index("lon"), 2))
    order_ref[...] = order
    x = dot(order, tokens_ref[...].astype(F32).reshape(cells, width).astype(BF16)).astype(BF16)
    x_ref[...] = x


def key_value_kernel(
    count_ref, x_ref, gain_ref, qkv_ref,
    kv_own_ref, kv_other_ref, edge_ref, normed_ref, raw_ref, inverse_ref,
):
    cells = x_ref.shape[0]
    blocks = cells // CELLS
    parity = lax.rem(lax.axis_index("lon"), 2)
    upper = lax.rem(lax.axis_index("lat"), 2) == 1
    normed = normalised(x_ref[...].astype(F32), gain_ref)
    normed_ref[...] = normed
    key, value = dot(normed, qkv_ref[1]), dot(normed, qkv_ref[2])
    raw_ref[...] = key
    inverse = lax.rsqrt(head_means(key * key) + EPS)
    inverse_ref[...] = inverse
    place = lax.broadcasted_iota(jnp.int32, (CELLS, 1), 0)
    counts = count_ref[0]
    live = []
    for slot in range(blocks):
        flip = blocks - 1 - slot
        live.append(
            place
            < jnp.where(parity == 1, counts[:, flip : flip + 1], counts[:, slot : slot + 1])
        )
    key = jnp.where(jnp.concatenate(live, 0), key * inverse, DEAD_KEY)
    shape = (blocks, CELLS, PAIR_WIDTH)
    low, high = halves(key, value)
    kv_own_ref[...] = jnp.where(upper, high, low).astype(BF16).reshape(shape)
    kv_other_ref[...] = jnp.where(upper, low, high).astype(BF16).reshape(shape)
    edge_ref[...] = kv_own_ref[0]


def query_grad_kernel(
    scale_in, order_ref, normed_ref, grad_ref, qkv_ref, out_weight_ref, kv_other_ref,
    qg_own_ref, qg_other_ref, corner_ref, raw_ref, inverse_ref, scale_ref,
):
    corner_ref[...] = kv_other_ref[0]
    cells, width = normed_ref.shape
    upper = lax.rem(lax.axis_index("lat"), 2) == 1
    all_scales = scale_in[...].reshape(1, HEADS) * (1.0 / math.sqrt(HEAD_DIM))
    for h in range(HALF):
        mine = jnp.where(
            upper, all_scales[:, HALF + h : HALF + h + 1], all_scales[:, h : h + 1]
        )
        scale_ref[h : h + 1] = jnp.broadcast_to(mine, (1, 4 * CELLS))
    query = dot(normed_ref[...], qkv_ref[0])
    raw_ref[...] = query
    inverse = lax.rsqrt(head_means(query * query) + EPS)
    inverse_ref[...] = inverse
    grad = dot_last(
        grad_ref[...].astype(F32).reshape(cells, width).astype(BF16), out_weight_ref[...]
    ).astype(BF16)
    low, high = halves(query * inverse, dot(order_ref[...], grad))
    shape = (cells // CELLS, CELLS, PAIR_WIDTH)
    qg_own_ref[...] = jnp.where(upper, high, low).astype(BF16).reshape(shape)
    qg_other_ref[...] = jnp.where(upper, low, high).astype(BF16).reshape(shape)


def join_kernel(kv_in, kv_ref):
    kv_ref[...] = kv_in[...]


def lane_tile(j):
    return slice((j // 2) * TILE, (j // 2 + 1) * TILE)


class Place:
    def __init__(self, rows):
        self.rows = rows
        tm, frames = lax.axis_index("tm"), lax.axis_size("tm")
        odd = lax.rem(tm, 2) == 1
        near, far = jnp.where(odd, tm - 1, tm + 1), jnp.where(odd, tm + 1, tm - 1)
        self.there = [None] + [((at >= 0) & (at < frames)) for at in (near, far)]
        self.upper = lax.rem(lax.axis_index("lat"), 2)

    def bias(self, frame, row, lanes):
        there = self.there[frame]
        total = 0.0 if there is None else jnp.where(there, 0.0, DROPPED)
        if row < 2:
            return total
        pair, pairs = lax.axis_index("lat") // 2, lax.axis_size("lat") // 2
        if row == 2:
            inside, wanted = pair > 0, self.upper
        else:
            inside, wanted = pair < pairs - 1, 1 - self.upper
        lane_row = (lax.broadcasted_iota(jnp.int32, (1, lanes), 1) // CELLS) % 2
        seen = (lane_row == wanted) & inside
        return total + jnp.where(seen, 0.0, DROPPED)


def head_scales(scale_ref, lanes):
    return [scale_ref[h : h + 1, lanes] for h in range(HALF)]


def key_bias(keys):
    return jnp.where(keys[:, 0:1].astype(F32) < 0.5 * DEAD_KEY, 0.0, DROPPED)


def score(keys, bias, weights_ref, lanes, scale_ref, sums):
    to_exp2 = [s * math.log2(math.e) for s in head_scales(scale_ref, lanes)]
    count = keys.shape[0]
    exps, probs = [], []
    for h in range(HALF):
        scores = dot(keys[:, lane_tile(h)], weights_ref[h, :, lanes])
        grad_prob = dot(keys[:, lane_tile(HALF + h)], weights_ref[HALF + h, :, lanes])
        masked = jnp.exp2(scores * to_exp2[h] + bias)
        if sums is not None:
            shape = (count // 8, 8, masked.shape[1])
            sums[h] = sums[h] + jnp.sum(masked.reshape(shape), 0)
            inner = (masked * grad_prob).reshape(shape)
            sums[HALF + h] = sums[HALF + h] + jnp.sum(inner, 0)
        exps.append(masked)
        probs.append(grad_prob)
    return exps, probs


ALL = slice(0, 4 * CELLS)
FIRST = slice(0, 2 * CELLS)
LAST = slice(2 * CELLS, 4 * CELLS)


def score_groups(place, groups, kv_refs, weights_ref, scale_ref, sums, e_mid, p_mid, e_left, p_left):
    side = [jnp.zeros((8, 2 * CELLS), F32) for _ in range(2 * HALF)]
    for index, (group, ref) in enumerate(zip(groups, kv_refs)):
        keys = ref[1:3].reshape(2 * CELLS, PAIR_WIDTH)
        bias = key_bias(keys) + place.bias(*group, 4 * CELLS)
        exps, probs = score(keys, bias, weights_ref, ALL, scale_ref, sums)
        for h in range(HALF):
            e_mid[h, index * 2 * CELLS : (index + 1) * 2 * CELLS] = exps[h]
            p_mid[h, index * 2 * CELLS : (index + 1) * 2 * CELLS] = probs[h]
    for index in range(0, len(kv_refs), 2):
        pair = [kv_refs[index][0], kv_refs[index + 1][0]]
        bias = side_bias(place, groups[index : index + 2], pair)
        keys = jnp.concatenate(pair, 0)
        exps, probs = score(keys, bias, weights_ref, FIRST, scale_ref, side)
        for h in range(HALF):
            e_left[h, index * CELLS : (index + 2) * CELLS] = exps[h]
            p_left[h, index * CELLS : (index + 2) * CELLS] = probs[h]
    return [jnp.concatenate([a[:, FIRST] + b, a[:, LAST]], 1) for a, b in zip(sums, side)]


def side_bias(place, groups, keys):
    return jnp.concatenate(
        [
            jnp.broadcast_to(
                key_bias(keys[i]) + place.bias(*groups[i], 2 * CELLS), (CELLS, 2 * CELLS)
            )
            for i in range(2)
        ],
        0,
    )


def away_groups(rows):
    return [(1, 0), (2, 0)], [(frame, row) for frame in (1, 2) for row in range(1, rows)]


def query_tables(qg_ref, weights, backward):
    rows = jnp.concatenate([qg_ref[0], qg_ref[2], qg_ref[1], qg_ref[3]], 0).astype(F32)
    cols = rows.T
    count = rows.shape[0]
    lane_half = lax.broadcasted_iota(jnp.int32, (count, TILE), 1) // HEAD_DIM
    row_half = lax.broadcasted_iota(jnp.int32, (TILE, count), 0) // HEAD_DIM
    for j in range(2 * HALF):
        backward[j] = jnp.where(lane_half == j % 2, rows[:, lane_tile(j)], 0.0).astype(BF16)
        weights[j] = jnp.where(row_half == j % 2, cols[lane_tile(j)], 0.0).astype(BF16)


def own_score_kernel(rows, scale_ref, qkv_ref, qg_ref, *refs):
    kv_refs, refs = refs[:rows], refs[rows:]
    turned_ref, weights, backward, sums_ref, e_mid, p_mid, e_left, p_left = refs
    for c in range(3):
        turned_ref[c] = qkv_ref[c].T
    queries = 4 * CELLS
    query_tables(qg_ref, weights, backward)
    sums = [jnp.zeros((8, queries), F32) for _ in range(2 * HALF)]
    sums = score_groups(
        Place(rows), [(0, row) for row in range(rows)], kv_refs, weights, scale_ref, sums,
        e_mid, p_mid, e_left, p_left,
    )
    for j in range(2 * HALF):
        sums_ref[j] = sums[j]


def away_score_kernel(rows, part, scale_ref, weights, sums_in, *refs):
    groups = away_groups(rows)[part]
    kv_refs, refs = refs[: len(groups)], refs[len(groups) :]
    sums_ref, e_mid, p_mid, e_left, p_left = refs
    sums = [sums_in[j] for j in range(2 * HALF)]
    sums = score_groups(
        Place(rows), groups, kv_refs, weights, scale_ref, sums, e_mid, p_mid, e_left, p_left
    )
    for j in range(2 * HALF):
        sums_ref[j] = sums[j]


def grad_parts(exps, probs, inverse, delta, scales):
    grads, halves_of = [], []
    for h in range(HALF):
        prob = exps[h] * inverse[h]
        halves_of.append(prob.astype(BF16))
        grads.append((prob * (probs[h] - delta[h]) * scales[h]).astype(BF16))
    return grads + halves_of


def key_grads(pieces, backward, lanes):
    outs = []
    for tile in range(TILES):
        both = jnp.concatenate([pieces[2 * tile], pieces[2 * tile + 1]], 1)
        rows = jnp.concatenate(
            [backward[2 * tile, lanes], backward[2 * tile + 1, lanes]], 0
        )
        outs.append(dot(both, rows))
    return jnp.concatenate(outs, 1)


def query_grads(keys, grads, h):
    own = slice((h % 2) * HEAD_DIM, (h % 2 + 1) * HEAD_DIM)
    return dot_first(keys[:, lane_tile(h)], grads)[own]


def sibling_kernel(
    rows, scale_ref, weights, backward, sums_in, early_ref, late_ref, part_ref, stats_ref, dq_ref
):
    place = Place(rows)
    side = [jnp.zeros((8, 2 * CELLS), F32) for _ in range(2 * HALF)]
    first, second = away_groups(rows)
    groups = [(0, row) for row in range(rows)] + first + second
    pairs = [early_ref[i : i + 2] for i in range(0, rows + 2, 2)]
    pairs += [late_ref[i : i + 2] for i in range(0, len(second), 2)]
    made = []
    for index, pair in enumerate(pairs):
        bias = side_bias(place, groups[2 * index : 2 * index + 2], pair)
        keys = pair.reshape(2 * CELLS, PAIR_WIDTH)
        made.append(score(keys, bias, weights, LAST, scale_ref, side))
    inverse, delta = [], []
    for h in range(HALF):
        total, inner = (
            jnp.concatenate([sums_in[j, :, FIRST], sums_in[j, :, LAST] + side[j]], 1)
            for j in (h, HALF + h)
        )
        inverse.append(1.0 / jnp.sum(total, 0, keepdims=True))
        delta.append(jnp.sum(inner, 0, keepdims=True) * inverse[h])
        stats_ref[h : h + 1] = inverse[h]
        stats_ref[HALF + h : HALF + h + 1] = delta[h]
    inverse = [a[:, LAST] for a in inverse]
    delta = [a[:, LAST] for a in delta]
    scales = head_scales(scale_ref, LAST)
    grads = []
    for index in range(0, 3 * rows, 2):
        pieces = grad_parts(*made[index // 2], inverse, delta, scales)
        grads.append(pieces[:HALF])
        if index < rows:
            part = key_grads(pieces, backward, LAST)
            part_ref[index : index + 2] = part.reshape(2, CELLS, PAIR_WIDTH)
    keys = jnp.concatenate(pairs, 0).reshape(3 * rows * CELLS, PAIR_WIDTH)
    for h in range(HALF):
        dq_ref[h * HEAD_DIM : (h + 1) * HEAD_DIM] = query_grads(
            keys, jnp.concatenate([g[h] for g in grads], 0), h
        )


def cross_score_kernel(rows, scale_ref, *refs):
    qg_refs, refs = refs[:2], refs[2:]
    kv_refs, sibling_ref, refs = refs[:rows], refs[rows], refs[rows + 1 :]
    backward, e_mid, p_mid, e_side, p_side, weights = refs
    place = Place(rows)
    for side in range(2):
        query_tables(qg_refs[side], weights.at[side], backward.at[side])
    for row in range(rows):
        keys = kv_refs[row][1:3].reshape(2 * CELLS, PAIR_WIDTH)
        bias = key_bias(keys) + place.bias(0, row, 4 * CELLS)
        at = slice(row * 2 * CELLS, (row + 1) * 2 * CELLS)
        for side in range(2):
            exps, probs = score(keys, bias, weights.at[side], ALL, scale_ref, None)
            for h in range(HALF):
                e_mid[side, h, at] = exps[h]
                p_mid[side, h, at] = probs[h]
    for row in range(0, rows, 2):
        at = slice(row * CELLS, (row + 2) * CELLS)
        for edge, lanes in ((0, FIRST), (1, LAST)):
            if edge == 0:
                pair = [kv_refs[row][0], kv_refs[row + 1][0]]
            else:
                pair = [sibling_ref[row], sibling_ref[row + 1]]
            bias = side_bias(place, [(0, row), (0, row + 1)], pair)
            keys = jnp.concatenate(pair, 0)
            for side in range(2):
                exps, probs = score(keys, bias, weights.at[side], lanes, scale_ref, None)
                for h in range(HALF):
                    e_side[side, edge, h, at] = exps[h]
                    p_side[side, edge, h, at] = probs[h]


def cross_stats(rows, stats_refs, lanes):
    place = Place(rows)
    both = []
    for side, ref in enumerate(stats_refs):
        there = jnp.where(place.there[1 + side], 1.0, 0.0)
        inverse = [ref[h : h + 1, lanes] * there for h in range(HALF)]
        both.append((inverse, [ref[HALF + h : HALF + h + 1, lanes] for h in range(HALF)]))
    return both


def cross_sibling_kernel(
    rows, scale_ref, near_stats, far_stats, backward, e_side, p_side, part_in, part_ref
):
    scales = head_scales(scale_ref, LAST)
    stats = cross_stats(rows, (near_stats, far_stats), LAST)
    for row in range(0, rows, 2):
        at = slice(row * CELLS, (row + 2) * CELLS)
        total = part_in[row : row + 2].reshape(2 * CELLS, PAIR_WIDTH)
        for side in range(2):
            pieces = grad_parts(
                [e_side[side, 1, h, at] for h in range(HALF)],
                [p_side[side, 1, h, at] for h in range(HALF)],
                *stats[side], scales,
            )
            total = total + key_grads(pieces, backward.at[side], LAST)
        part_ref[row : row + 2] = total.reshape(2, CELLS, PAIR_WIDTH).astype(BF16)


def cross_back_kernel(
    rows, scale_ref, near_stats, far_stats, backward, e_mid, p_mid, e_side, p_side,
    own_ref, total_ref,
):
    scales = head_scales(scale_ref, ALL)
    stats = cross_stats(rows, (near_stats, far_stats), ALL)
    for row in range(rows):
        at = slice(row * 2 * CELLS, (row + 1) * 2 * CELLS)
        total = own_ref[row, 1:3].reshape(2 * CELLS, PAIR_WIDTH)
        for side in range(2):
            pieces = grad_parts(
                [e_mid[side, h, at] for h in range(HALF)],
                [p_mid[side, h, at] for h in range(HALF)],
                *stats[side], scales,
            )
            total = total + key_grads(pieces, backward.at[side], ALL)
        total_ref[row, 1:3] = total.reshape(2, CELLS, PAIR_WIDTH)
    scales = head_scales(scale_ref, FIRST)
    stats = cross_stats(rows, (near_stats, far_stats), FIRST)
    for row in range(0, rows, 2):
        at = slice(row * CELLS, (row + 2) * CELLS)
        total = own_ref[row : row + 2, 0].reshape(2 * CELLS, PAIR_WIDTH)
        for side in range(2):
            pieces = grad_parts(
                [e_side[side, 0, h, at] for h in range(HALF)],
                [p_side[side, 0, h, at] for h in range(HALF)],
                *stats[side], scales,
            )
            total = total + key_grads(pieces, backward.at[side], FIRST)
        total_ref[row : row + 2, 0] = total.reshape(2, CELLS, PAIR_WIDTH)


def own_back_kernel(
    rows, scale_ref, stats_ref, backward, e_mid, p_mid, e_left, p_left,
    first_e_mid, first_p_mid, first_e_left, first_p_left,
    second_e_mid, second_p_mid, second_e_left, second_p_left, dq_sibling, *refs,
):
    kv_refs, refs = refs[: 3 * rows], refs[3 * rows :]
    own_ref, dq_own_ref, dq_other_ref, d_mid, d_left = refs
    scales = head_scales(scale_ref, ALL)
    inverse = [stats_ref[h : h + 1] for h in range(HALF)]
    delta = [stats_ref[HALF + h : HALF + h + 1] for h in range(HALF)]
    for index in range(3 * rows):
        at = slice(index * 2 * CELLS, (index + 1) * 2 * CELLS)
        if index < rows:
            exps, probs, start = e_mid, p_mid, index * 2 * CELLS
        elif index < rows + 2:
            exps, probs, start = first_e_mid, first_p_mid, (index - rows) * 2 * CELLS
        else:
            exps, probs, start = second_e_mid, second_p_mid, (index - rows - 2) * 2 * CELLS
        cut = slice(start, start + 2 * CELLS)
        pieces = grad_parts(
            [exps[h, cut] for h in range(HALF)], [probs[h, cut] for h in range(HALF)],
            inverse, delta, scales,
        )
        for h in range(HALF):
            d_mid[h, at] = pieces[h]
        if index < rows:
            part = key_grads(pieces, backward, ALL)
            own_ref[index, 1:3] = part.reshape(2, CELLS, PAIR_WIDTH)
    scales = head_scales(scale_ref, FIRST)
    inverse = [a[:, FIRST] for a in inverse]
    delta = [a[:, FIRST] for a in delta]
    for index in range(0, 3 * rows, 2):
        at = slice(index * CELLS, (index + 2) * CELLS)
        if index < rows:
            exps, probs, start = e_left, p_left, index * CELLS
        elif index < rows + 2:
            exps, probs, start = first_e_left, first_p_left, (index - rows) * CELLS
        else:
            exps, probs, start = second_e_left, second_p_left, (index - rows - 2) * CELLS
        cut = slice(start, start + 2 * CELLS)
        pieces = grad_parts(
            [exps[h, cut] for h in range(HALF)], [probs[h, cut] for h in range(HALF)],
            inverse, delta, scales,
        )
        for h in range(HALF):
            d_left[h, at] = pieces[h]
        if index < rows:
            part = key_grads(pieces, backward, FIRST)
            own_ref[index : index + 2, 0] = part.reshape(2, CELLS, PAIR_WIDTH)
    mid = jnp.concatenate([ref[1:3].reshape(2 * CELLS, PAIR_WIDTH) for ref in kv_refs], 0)
    left = jnp.concatenate([ref[0] for ref in kv_refs], 0)
    columns = []
    for h in range(HALF):
        made = query_grads(mid, d_mid[h], h)
        first = query_grads(left, d_left[h], h)
        last = dq_sibling[h * HEAD_DIM : (h + 1) * HEAD_DIM]
        columns.append(made + jnp.concatenate([first, last], 1))
    dq = jnp.concatenate(columns, 0).T
    dq_own_ref[...] = jnp.concatenate([dq[:CELLS], dq[2 * CELLS : 3 * CELLS]], 1)
    dq_other_ref[...] = jnp.concatenate([dq[CELLS : 2 * CELLS], dq[3 * CELLS :]], 1).astype(BF16)


def column_out_kernel(total_ref, sibling_ref, dq_other_ref, inner_ref, to_lat_ref, edge_ref, corner_ref):
    inner_ref[0] = total_ref[0, 1]
    inner_ref[1] = total_ref[0, 2] + sibling_ref[0].astype(F32)
    to_lat_ref[0] = total_ref[1, 1].astype(BF16)
    to_lat_ref[2] = dq_other_ref[...]
    to_lat_ref[1] = (total_ref[1, 2] + sibling_ref[1].astype(F32)).astype(BF16)
    edge_ref[...] = total_ref[0, 0].astype(BF16)
    corner_ref[...] = total_ref[1, 0].astype(BF16)


def heads_back(query, inner, edge, raws, inverses, weights):
    pair = jnp.concatenate([inner[0] + edge, inner[1]], 0)
    query = jnp.concatenate([query[:, :HALF_WIDTH], query[:, HALF_WIDTH:]], 0)
    grads = (query, pair[:, :HALF_WIDTH], pair[:, HALF_WIDTH:])
    total = dot(grads[2].astype(BF16), weights[2])
    for c in range(2):
        mean = head_means(raws[c] * grads[c])
        cubed = inverses[c] * inverses[c] * inverses[c]
        grad_raw = inverses[c] * grads[c] - cubed * raws[c] * mean
        total = total + dot(grad_raw.astype(BF16), weights[c])
    return total


def own_finish_kernel(
    inner_ref, dq_ref, edge_ref, query_raw, query_inverse, key_raw, key_inverse, turned_ref,
    total_ref, raws_ref, inverses_ref, weights_ref,
):
    upper = lax.rem(lax.axis_index("lat"), 2) == 1

    def split(array):
        low, high = array[:, :HALF_WIDTH], array[:, HALF_WIDTH:]
        return jnp.where(upper, high, low), jnp.where(upper, low, high)

    raws, other_raws = zip(split(query_raw[...]), split(key_raw[...]))
    inverses, other_inverses = zip(split(query_inverse[...]), split(key_inverse[...]))
    weights = []
    for c in range(3):
        low, high = turned_ref[c, :HALF_WIDTH], turned_ref[c, HALF_WIDTH:]
        weights.append(jnp.where(upper, high, low))
        weights_ref[c] = jnp.where(upper, low, high)
    for c in range(2):
        raws_ref[c] = other_raws[c]
        inverses_ref[c] = other_inverses[c]
    total_ref[...] = heads_back(
        dq_ref[...], inner_ref[...], edge_ref[...].astype(F32), raws, inverses, weights
    )


def finish_kernel(
    total_ref, other_ref, corner_ref, raws_ref, inverses_ref, weights_ref,
    x_ref, order_ref, gain_ref, out_ref,
):
    grad_normed = total_ref[...] + heads_back(
        other_ref[2].astype(F32), other_ref[:2].astype(F32), corner_ref[...].astype(F32),
        (raws_ref[0], raws_ref[1]), (inverses_ref[0], inverses_ref[1]), weights_ref,
    )
    order = order_ref[...]
    x = x_ref[...].astype(F32)
    inverse = lax.rsqrt(jnp.mean(x * x, -1, keepdims=True) + EPS)
    grad = gain_ref[...].reshape(1, x.shape[1]) * grad_normed
    mean = jnp.mean(x * grad, -1, keepdims=True)
    grad = (inverse * grad - inverse * inverse * inverse * x * mean).astype(BF16)
    out_ref[...] = dot_first(order, grad).reshape(out_ref.shape).astype(BF16)


VMEM = pl.BlockSpec(memory_space=pltpu.VMEM)


def kernel_call(
    body, name, outs, args, scratch=(), limit_mib=16, micros=1.0
):
    return pl.pallas_call(
        body,
        name=name,
        out_shape=[jax.ShapeDtypeStruct(shape, dtype) for shape, dtype in outs],
        in_specs=[VMEM] * len(args),
        out_specs=[VMEM] * len(outs),
        scratch_shapes=list(scratch),
        compiler_params=pltpu.CompilerParams(vmem_limit_bytes=limit_mib * 1024 * 1024),
        cost_estimate=pl.CostEstimate(
            flops=int(micros * FLOPS_PER_US), bytes_accessed=0, transcendentals=0
        ),
    )(*args)


def per_device(tokens, key_count, norm_gain, qkv_weight, out_weight, logit_scale, grad_out):
    frames, lat_rows, lon_cols, width = tokens.shape
    assert frames == BLOCK and lat_rows == BLOCK and lon_cols == 2 * BLOCK
    assert lax.axis_size("lat") % 2 == 0 and lax.axis_size("lon") % 2 == 0
    cells = frames * lat_rows * lon_cols
    blocks = lon_cols // BLOCK
    head_width = HEADS * HEAD_DIM
    qg_shape = ((blocks, CELLS, PAIR_WIDTH), BF16)
    edge_shape = ((CELLS, PAIR_WIDTH), BF16)

    order, x = kernel_call(
        order_kernel, "order", [((cells, cells), BF16), ((cells, width), BF16)], [tokens],
        micros=10.0,
    )
    projected = ((cells, head_width), F32)
    kv_own, kv_other, edge, normed, key_raw, key_inverse = kernel_call(
        key_value_kernel, "key_value",
        [qg_shape, qg_shape, edge_shape, ((cells, width), BF16), projected, projected],
        [key_count, x, norm_gain, qkv_weight], micros=2.0,
    )
    edge = pair_swap(edge, "lon", 1)
    kv_made, kv_other = kv_other, pair_swap(kv_other, "lat", 0)
    qg_own, qg_other, corner, query_raw, query_inverse, scales = kernel_call(
        query_grad_kernel, "query_grad",
        [qg_shape, qg_shape, edge_shape, projected, projected, ((HALF, 4 * CELLS), F32)],
        [logit_scale, order, normed, grad_out, qkv_weight, out_weight, kv_made], micros=5.0,
    )
    corner = corner_swap(corner)
    (kv_other,) = kernel_call(join_kernel, "join", [qg_shape], [kv_other], micros=3.0)
    qg_other, kv_other = lax.optimization_barrier((qg_other, kv_other))
    qg_other = pair_swap(qg_other, "lat", 0)
    kv_rows = [
        jnp.concatenate([edge[None], kv_own], 0),
        jnp.concatenate([corner[None], kv_other], 0),
    ]
    upper = lax.rem(lax.axis_index("lat"), 2) == 1
    wide = lax.axis_size("lat") > 2
    if wide:
        even = jnp.where(upper, kv_rows[1], kv_rows[0])
        odd = jnp.where(upper, kv_rows[0], kv_rows[1])
        kv_rows += [shift_by(odd, "lat", 2), shift_by(even, "lat", -2)]
    rows = len(kv_rows)
    kv_away = [frame_swap(kv, phase) for phase in range(2) for kv in kv_rows]
    qg_both = jnp.concatenate([qg_own, qg_other], 0)
    qg_away = [frame_swap(qg_both, phase) for phase in range(2)]

    queries = 4 * CELLS
    tables = [((2 * HALF, TILE, queries), BF16), ((2 * HALF, queries, TILE), BF16)]
    sums_shape = ((2 * HALF, 8, queries), F32)

    def kept(groups):
        mid = ((HALF, groups * 2 * CELLS, queries), F32)
        left = ((HALF, groups * CELLS, 2 * CELLS), F32)
        return [mid, mid, left, left]

    turned, weights, backward, sums, *own_kept = kernel_call(
        functools.partial(own_score_kernel, rows), "own_score",
        [((3, head_width, width), BF16)] + tables + [sums_shape] + kept(rows),
        [scales, qkv_weight, qg_both, *kv_rows], micros=1.5,
    )
    kv_parts = [[kv_away[(frame - 1) * rows + row] for frame, row in part]
                for part in away_groups(rows)]
    early = pair_swap(jnp.stack([kv[2] for kv in kv_rows + kv_parts[0]], 0), "lon", 0)
    late = pair_swap(jnp.stack([kv[2] for kv in kv_parts[1]], 0), "lon", 0)
    away_kept = []
    for which, kvs in enumerate(kv_parts):
        sums, *made = kernel_call(
            functools.partial(away_score_kernel, rows, which), "away_score",
            [sums_shape] + kept(len(kvs)), [scales, weights, sums, *kvs],
            micros=(1.5, 20.0)[which],
        )
        away_kept += made
    half_part = (rows, CELLS, PAIR_WIDTH)
    sibling_part, stats, dq_sibling = kernel_call(
        functools.partial(sibling_kernel, rows), "sibling",
        [(half_part, F32), ((2 * HALF, queries), F32), ((HALF_WIDTH, 2 * CELLS), F32)],
        [scales, weights, backward, sums, early, late], micros=1.5,
    )
    near_stats, far_stats = frame_swap(stats, 0), frame_swap(stats, 1)
    cross_mid = ((2, HALF, rows * 2 * CELLS, queries), F32)
    cross_side = ((2, 2, HALF, rows * CELLS, 2 * CELLS), F32)
    cross_backward, e_mid, p_mid, e_side, p_side = kernel_call(
        functools.partial(cross_score_kernel, rows), "cross_score",
        [((2,) + tables[1][0], BF16), cross_mid, cross_mid, cross_side, cross_side],
        [scales, *qg_away, *kv_rows, early], micros=2.0,
        scratch=[pltpu.VMEM((2,) + tables[0][0], BF16)],
    )
    part = (rows, blocks + 1, CELLS, PAIR_WIDTH)
    packed = (CELLS, 2 * HALF_WIDTH)
    own_part, dq_own, dq_other = kernel_call(
        functools.partial(own_back_kernel, rows), "own_back",
        [(part, F32), (packed, F32), (packed, BF16)],
        [scales, stats, backward, *own_kept, *away_kept, dq_sibling, *kv_rows,
         *kv_parts[0], *kv_parts[1]],
        micros=2.0,
        scratch=[
            pltpu.VMEM((HALF, 3 * rows * 2 * CELLS, queries), BF16),
            pltpu.VMEM((HALF, 3 * rows * CELLS, 2 * CELLS), BF16),
        ],
    )
    (sibling_part,) = kernel_call(
        functools.partial(cross_sibling_kernel, rows), "cross_sibling", [(half_part, BF16)],
        [scales, near_stats, far_stats, cross_backward, e_side, p_side, sibling_part],
        micros=0.5,
    )
    sibling_part = pair_swap(sibling_part, "lon", 0)
    (total,) = kernel_call(
        functools.partial(cross_back_kernel, rows), "cross_back", [(part, F32)],
        [scales, near_stats, far_stats, cross_backward, e_mid, p_mid, e_side, p_side,
         own_part],
        micros=1.5,
    )
    if wide:
        total = total.at[:, blocks].add(sibling_part.astype(F32))
        sibling_part = jnp.zeros_like(sibling_part)
        to_odd = shift_by(total[2].astype(BF16), "lat", -2).astype(F32)
        to_even = shift_by(total[3].astype(BF16), "lat", 2).astype(F32)
        total = total[:2] + jnp.stack(
            [jnp.where(upper, to_odd, to_even), jnp.where(upper, to_even, to_odd)], 0
        )
    inner, to_lat, edge, corner = kernel_call(
        column_out_kernel, "column_out",
        [((blocks, CELLS, PAIR_WIDTH), F32), ((blocks + 1, CELLS, PAIR_WIDTH), BF16),
         edge_shape, edge_shape],
        [total, sibling_part, dq_other],
    )
    edge = pair_swap(edge, "lon", 1)
    corner = corner_swap(corner)
    other = pair_swap(to_lat, "lat", 0)
    halved = ((2, cells, HALF_WIDTH), F32)
    summed, raws, inverses, weights = kernel_call(
        own_finish_kernel, "own_finish",
        [((cells, width), F32), halved, halved, ((3, HALF_WIDTH, width), BF16)],
        [inner, dq_own, edge, query_raw, query_inverse, key_raw, key_inverse, turned],
        micros=1.0,
    )
    (grad_tokens,) = kernel_call(
        finish_kernel, "finish", [(tokens.shape, BF16)],
        [summed, other, corner, raws, inverses, weights, x, order, norm_gain], micros=2.0,
    )
    return grad_tokens


def solution(mesh):
    in_specs = (
        P("tm", "lat", "lon", None),
        P("tm", "lat", "lon"),
        P(),
        P(),
        P(),
        P(),
        P("tm", "lat", "lon", None),
    )
    out_specs = P("tm", "lat", "lon", None)
    return jax.shard_map(
        per_device, mesh=mesh, in_specs=in_specs, out_specs=out_specs, check_vma=False
    )
```

```python
import functools
import math

import jax
import jax.numpy as jnp
from jax import lax
from jax.experimental import pallas as pl
from jax.experimental.pallas import tpu as pltpu
from jax.sharding import PartitionSpec as P

HEADS = 6
HEAD_DIM = 64
BLOCK = 4
CELLS = BLOCK * BLOCK * BLOCK
HALF = HEADS // 2
HALF_WIDTH = HALF * HEAD_DIM
PAIR_WIDTH = 2 * HALF_WIDTH
TILE = 2 * HEAD_DIM
TILES = PAIR_WIDTH // TILE
DEAD_KEY = 64.0
DROPPED = -1e30
FLOPS_PER_US = 1e9

EPS = 1e-06
F32 = jnp.float32
BF16 = jnp.bfloat16


def partner_of(device, count, phase):
    return device + 1 if device % 2 == phase else device - 1


def pair_swap(array, axis, phase):
    count = lax.axis_size(axis)
    pairs = [(device, partner_of(device, count, phase) % count) for device in range(count)]
    return lax.ppermute(array, axis, pairs)


def frame_swap(array, phase):
    frames, lons = lax.axis_size("tm"), lax.axis_size("lon")
    pairs = []
    for frame in range(frames):
        for lon in range(lons):
            to = (partner_of(frame, frames, phase), lon)
            if not 0 <= to[0] < frames:
                to = (frame, partner_of(lon, lons, 0))
            pairs.append((frame * lons + lon, to[0] * lons + to[1]))
    return lax.ppermute(array, ("tm", "lon"), pairs)


def corner_swap(array):
    lats, lons = lax.axis_size("lat"), lax.axis_size("lon")
    pairs = []
    for lat in range(lats):
        for lon in range(lons):
            to = partner_of(lat, lats, 0) * lons + partner_of(lon, lons, 1) % lons
            pairs.append((lat * lons + lon, to))
    return lax.ppermute(array, ("lat", "lon"), pairs)


def shift_by(array, axis, step):
    count = lax.axis_size(axis)
    pairs = [(i, i + step) for i in range(count) if 0 <= i + step < count]
    return lax.ppermute(array, axis, pairs)


def dot(a, b):
    return lax.dot_general(a, b, (((1,), (0,)), ((), ())), preferred_element_type=F32)


def dot_last(a, b):
    return lax.dot_general(a, b, (((1,), (1,)), ((), ())), preferred_element_type=F32)


def dot_first(a, b):
    return lax.dot_general(a, b, (((0,), (0,)), ((), ())), preferred_element_type=F32)


def head_means(values):
    rows = lax.broadcasted_iota(jnp.int32, (TILE, TILE), 0) // HEAD_DIM
    cols = lax.broadcasted_iota(jnp.int32, (TILE, TILE), 1) // HEAD_DIM
    ones = (rows == cols).astype(F32).astype(BF16)
    high = values.astype(BF16)
    low = (values - high.astype(F32)).astype(BF16)
    pieces = []
    for start in range(0, values.shape[1], TILE):
        cut = slice(start, min(start + TILE, values.shape[1]))
        square = ones[: cut.stop - start, : cut.stop - start]
        pieces.append(dot(high[:, cut], square) + dot(low[:, cut], square))
    return jnp.concatenate(pieces, 1) * (1.0 / HEAD_DIM)


def block_order(lat_rows, lon_cols, count, parity):
    blocks = lon_cols // BLOCK
    row = lax.broadcasted_iota(jnp.int32, (count, count), 0)
    source = lax.broadcasted_iota(jnp.int32, (count, count), 1)
    slot = row // CELLS
    place = row % CELLS
    frame = place // (BLOCK * BLOCK)
    lat = (place // BLOCK) % BLOCK
    col = place % BLOCK
    block = jnp.where(parity == 1, blocks - 1 - slot, slot)
    wanted = (frame * lat_rows + lat) * lon_cols + block * BLOCK + col
    return (source == wanted).astype(F32).astype(BF16)


def halves(first, second):
    low = jnp.concatenate([first[:, :HALF_WIDTH], second[:, :HALF_WIDTH]], 1)
    high = jnp.concatenate([first[:, HALF_WIDTH:], second[:, HALF_WIDTH:]], 1)
    return low, high


def normalised(x, gain_ref):
    inverse = lax.rsqrt(jnp.mean(x * x, -1, keepdims=True) + EPS)
    return (x * inverse * gain_ref[...].reshape(1, x.shape[1])).astype(BF16)


def order_kernel(tokens_ref, order_ref, x_ref):
    frames, lat_rows, lon_cols, width = tokens_ref.shape
    cells = frames * lat_rows * lon_cols
    order = block_order(lat_rows, lon_cols, cells, lax.rem(lax.axis_index("lon"), 2))
    order_ref[...] = order
    x = dot(order, tokens_ref[...].astype(F32).reshape(cells, width).astype(BF16)).astype(BF16)
    x_ref[...] = x


def key_value_kernel(
    count_ref, x_ref, gain_ref, qkv_ref,
    kv_own_ref, kv_other_ref, edge_ref, normed_ref, raw_ref, inverse_ref,
):
    cells = x_ref.shape[0]
    blocks = cells // CELLS
    parity = lax.rem(lax.axis_index("lon"), 2)
    upper = lax.rem(lax.axis_index("lat"), 2) == 1
    normed = normalised(x_ref[...].astype(F32), gain_ref)
    normed_ref[...] = normed
    key, value = dot(normed, qkv_ref[1]), dot(normed, qkv_ref[2])
    raw_ref[...] = key
    inverse = lax.rsqrt(head_means(key * key) + EPS)
    inverse_ref[...] = inverse
    place = lax.broadcasted_iota(jnp.int32, (CELLS, 1), 0)
    counts = count_ref[0]
    live = []
    for slot in range(blocks):
        flip = blocks - 1 - slot
        live.append(
            place
            < jnp.where(parity == 1, counts[:, flip : flip + 1], counts[:, slot : slot + 1])
        )
    key = jnp.where(jnp.concatenate(live, 0), key * inverse, DEAD_KEY)
    shape = (blocks, CELLS, PAIR_WIDTH)
    low, high = halves(key, value)
    kv_own_ref[...] = jnp.where(upper, high, low).astype(BF16).reshape(shape)
    kv_other_ref[...] = jnp.where(upper, low, high).astype(BF16).reshape(shape)
    edge_ref[...] = kv_own_ref[0]


def query_grad_kernel(
    scale_in, order_ref, normed_ref, grad_ref, qkv_ref, out_weight_ref, kv_other_ref,
    qg_own_ref, qg_other_ref, corner_ref, raw_ref, inverse_ref, scale_ref,
):
    corner_ref[...] = kv_other_ref[0]
    cells, width = normed_ref.shape
    upper = lax.rem(lax.axis_index("lat"), 2) == 1
    all_scales = scale_in[...].reshape(1, HEADS) * (1.0 / math.sqrt(HEAD_DIM))
    for h in range(HALF):
        mine = jnp.where(
            upper, all_scales[:, HALF + h : HALF + h + 1], all_scales[:, h : h + 1]
        )
        scale_ref[h : h + 1] = jnp.broadcast_to(mine, (1, 4 * CELLS))
    query = dot(normed_ref[...], qkv_ref[0])
    raw_ref[...] = query
    inverse = lax.rsqrt(head_means(query * query) + EPS)
    inverse_ref[...] = inverse
    grad = dot_last(
        grad_ref[...].astype(F32).reshape(cells, width).astype(BF16), out_weight_ref[...]
    ).astype(BF16)
    low, high = halves(query * inverse, dot(order_ref[...], grad))
    shape = (cells // CELLS, CELLS, PAIR_WIDTH)
    qg_own_ref[...] = jnp.where(upper, high, low).astype(BF16).reshape(shape)
    qg_other_ref[...] = jnp.where(upper, low, high).astype(BF16).reshape(shape)


def join_kernel(kv_in, kv_ref):
    kv_ref[...] = kv_in[...]


def lane_tile(j):
    return slice((j // 2) * TILE, (j // 2 + 1) * TILE)


class Place:
    def __init__(self, rows):
        self.rows = rows
        tm, frames = lax.axis_index("tm"), lax.axis_size("tm")
        odd = lax.rem(tm, 2) == 1
        near, far = jnp.where(odd, tm - 1, tm + 1), jnp.where(odd, tm + 1, tm - 1)
        self.there = [None] + [((at >= 0) & (at < frames)) for at in (near, far)]
        self.upper = lax.rem(lax.axis_index("lat"), 2)

    def bias(self, frame, row, lanes):
        there = self.there[frame]
        total = 0.0 if there is None else jnp.where(there, 0.0, DROPPED)
        if row < 2:
            return total
        pair, pairs = lax.axis_index("lat") // 2, lax.axis_size("lat") // 2
        if row == 2:
            inside, wanted = pair > 0, self.upper
        else:
            inside, wanted = pair < pairs - 1, 1 - self.upper
        lane_row = (lax.broadcasted_iota(jnp.int32, (1, lanes), 1) // CELLS) % 2
        seen = (lane_row == wanted) & inside
        return total + jnp.where(seen, 0.0, DROPPED)


def head_scales(scale_ref, lanes):
    return [scale_ref[h : h + 1, lanes] for h in range(HALF)]


def key_bias(keys):
    return jnp.where(keys[:, 0:1].astype(F32) < 0.5 * DEAD_KEY, 0.0, DROPPED)


def score(keys, bias, weights_ref, lanes, scale_ref, sums):
    to_exp2 = [s * math.log2(math.e) for s in head_scales(scale_ref, lanes)]
    count = keys.shape[0]
    exps, probs = [], []
    for h in range(HALF):
        scores = dot(keys[:, lane_tile(h)], weights_ref[h, :, lanes])
        grad_prob = dot(keys[:, lane_tile(HALF + h)], weights_ref[HALF + h, :, lanes])
        masked = jnp.exp2(scores * to_exp2[h] + bias)
        if sums is not None:
            shape = (count // 8, 8, masked.shape[1])
            sums[h] = sums[h] + jnp.sum(masked.reshape(shape), 0)
            inner = (masked * grad_prob).reshape(shape)
            sums[HALF + h] = sums[HALF + h] + jnp.sum(inner, 0)
        exps.append(masked)
        probs.append(grad_prob)
    return exps, probs


ALL = slice(0, 4 * CELLS)
FIRST = slice(0, 2 * CELLS)
LAST = slice(2 * CELLS, 4 * CELLS)


def score_groups(place, groups, kv_refs, weights_ref, scale_ref, sums, e_mid, p_mid, e_left, p_left):
    side = [jnp.zeros((8, 2 * CELLS), F32) for _ in range(2 * HALF)]
    for index, (group, ref) in enumerate(zip(groups, kv_refs)):
        keys = ref[1:3].reshape(2 * CELLS, PAIR_WIDTH)
        bias = key_bias(keys) + place.bias(*group, 4 * CELLS)
        exps, probs = score(keys, bias, weights_ref, ALL, scale_ref, sums)
        for h in range(HALF):
            e_mid[h, index * 2 * CELLS : (index + 1) * 2 * CELLS] = exps[h]
            p_mid[h, index * 2 * CELLS : (index + 1) * 2 * CELLS] = probs[h]
    for index in range(0, len(kv_refs), 2):
        pair = [kv_refs[index][0], kv_refs[index + 1][0]]
        bias = side_bias(place, groups[index : index + 2], pair)
        keys = jnp.concatenate(pair, 0)
        exps, probs = score(keys, bias, weights_ref, FIRST, scale_ref, side)
        for h in range(HALF):
            e_left[h, index * CELLS : (index + 2) * CELLS] = exps[h]
            p_left[h, index * CELLS : (index + 2) * CELLS] = probs[h]
    return [jnp.concatenate([a[:, FIRST] + b, a[:, LAST]], 1) for a, b in zip(sums, side)]


def side_bias(place, groups, keys):
    return jnp.concatenate(
        [
            jnp.broadcast_to(
                key_bias(keys[i]) + place.bias(*groups[i], 2 * CELLS), (CELLS, 2 * CELLS)
            )
            for i in range(2)
        ],
        0,
    )


def away_groups(rows):
    return [(1, 0), (2, 0)], [(frame, row) for frame in (1, 2) for row in range(1, rows)]


def query_tables(qg_ref, weights, backward):
    rows = jnp.concatenate([qg_ref[0], qg_ref[2], qg_ref[1], qg_ref[3]], 0).astype(F32)
    cols = rows.T
    count = rows.shape[0]
    lane_half = lax.broadcasted_iota(jnp.int32, (count, TILE), 1) // HEAD_DIM
    row_half = lax.broadcasted_iota(jnp.int32, (TILE, count), 0) // HEAD_DIM
    for j in range(2 * HALF):
        backward[j] = jnp.where(lane_half == j % 2, rows[:, lane_tile(j)], 0.0).astype(BF16)
        weights[j] = jnp.where(row_half == j % 2, cols[lane_tile(j)], 0.0).astype(BF16)


def own_score_kernel(rows, scale_ref, qkv_ref, qg_ref, *refs):
    kv_refs, refs = refs[:rows], refs[rows:]
    turned_ref, weights, backward, sums_ref, e_mid, p_mid, e_left, p_left = refs
    for c in range(3):
        turned_ref[c] = qkv_ref[c].T
    queries = 4 * CELLS
    query_tables(qg_ref, weights, backward)
    sums = [jnp.zeros((8, queries), F32) for _ in range(2 * HALF)]
    sums = score_groups(
        Place(rows), [(0, row) for row in range(rows)], kv_refs, weights, scale_ref, sums,
        e_mid, p_mid, e_left, p_left,
    )
    for j in range(2 * HALF):
        sums_ref[j] = sums[j]


def away_score_kernel(rows, part, scale_ref, weights, sums_in, *refs):
    groups = away_groups(rows)[part]
    kv_refs, refs = refs[: len(groups)], refs[len(groups) :]
    sums_ref, e_mid, p_mid, e_left, p_left = refs
    sums = [sums_in[j] for j in range(2 * HALF)]
    sums = score_groups(
        Place(rows), groups, kv_refs, weights, scale_ref, sums, e_mid, p_mid, e_left, p_left
    )
    for j in range(2 * HALF):
        sums_ref[j] = sums[j]


def grad_parts(exps, probs, inverse, delta, scales):
    grads, halves_of = [], []
    for h in range(HALF):
        prob = exps[h] * inverse[h]
        halves_of.append(prob.astype(BF16))
        grads.append((prob * (probs[h] - delta[h]) * scales[h]).astype(BF16))
    return grads + halves_of


def key_grads(pieces, backward, lanes):
    outs = []
    for tile in range(TILES):
        both = jnp.concatenate([pieces[2 * tile], pieces[2 * tile + 1]], 1)
        rows = jnp.concatenate(
            [backward[2 * tile, lanes], backward[2 * tile + 1, lanes]], 0
        )
        outs.append(dot(both, rows))
    return jnp.concatenate(outs, 1)


def query_grads(keys, grads, h):
    own = slice((h % 2) * HEAD_DIM, (h % 2 + 1) * HEAD_DIM)
    return dot_first(keys[:, lane_tile(h)], grads)[own]


def sibling_score_kernel(rows, scale_ref, weights, early_ref, sums_ref, e_out, p_out):
    side = [jnp.zeros((8, 2 * CELLS), F32) for _ in range(2 * HALF)]
    groups = [(0, row) for row in range(rows)] + away_groups(rows)[0]
    for i in range(0, rows + 2, 2):
        pair = early_ref[i : i + 2]
        bias = side_bias(Place(rows), groups[i : i + 2], pair)
        keys = pair.reshape(2 * CELLS, PAIR_WIDTH)
        exps, probs = score(keys, bias, weights, LAST, scale_ref, side)
        for h in range(HALF):
            e_out[h, i * CELLS : (i + 2) * CELLS] = exps[h]
            p_out[h, i * CELLS : (i + 2) * CELLS] = probs[h]
    for j in range(2 * HALF):
        sums_ref[j] = side[j]


def sibling_kernel(
    rows, scale_ref, weights, backward, sums_in, side_in, e_early, p_early, early_ref, late_ref,
    part_ref, stats_ref, dq_ref,
):
    place = Place(rows)
    side = [side_in[j] for j in range(2 * HALF)]
    second = away_groups(rows)[1]
    pairs = [early_ref[i : i + 2] for i in range(0, rows + 2, 2)]
    pairs += [late_ref[i : i + 2] for i in range(0, len(second), 2)]
    made = []
    for i in range(0, rows + 2, 2):
        at = slice(i * CELLS, (i + 2) * CELLS)
        made.append(
            ([e_early[h, at] for h in range(HALF)], [p_early[h, at] for h in range(HALF)])
        )
    for i in range(0, len(second), 2):
        pair = late_ref[i : i + 2]
        bias = side_bias(place, second[i : i + 2], pair)
        keys = pair.reshape(2 * CELLS, PAIR_WIDTH)
        made.append(score(keys, bias, weights, LAST, scale_ref, side))
    inverse, delta = [], []
    for h in range(HALF):
        total, inner = (
            jnp.concatenate([sums_in[j, :, FIRST], sums_in[j, :, LAST] + side[j]], 1)
            for j in (h, HALF + h)
        )
        inverse.append(1.0 / jnp.sum(total, 0, keepdims=True))
        delta.append(jnp.sum(inner, 0, keepdims=True) * inverse[h])
        stats_ref[h : h + 1] = inverse[h]
        stats_ref[HALF + h : HALF + h + 1] = delta[h]
    inverse = [a[:, LAST] for a in inverse]
    delta = [a[:, LAST] for a in delta]
    scales = head_scales(scale_ref, LAST)
    grads = []
    for index in range(0, 3 * rows, 2):
        pieces = grad_parts(*made[index // 2], inverse, delta, scales)
        grads.append(pieces[:HALF])
        if index < rows:
            part = key_grads(pieces, backward, LAST)
            part_ref[index : index + 2] = part.reshape(2, CELLS, PAIR_WIDTH)
    keys = jnp.concatenate(pairs, 0).reshape(3 * rows * CELLS, PAIR_WIDTH)
    for h in range(HALF):
        dq_ref[h * HEAD_DIM : (h + 1) * HEAD_DIM] = query_grads(
            keys, jnp.concatenate([g[h] for g in grads], 0), h
        )


def cross_score_kernel(rows, scale_ref, *refs):
    qg_refs, refs = refs[:2], refs[2:]
    kv_refs, sibling_ref, refs = refs[:rows], refs[rows], refs[rows + 1 :]
    backward, e_mid, p_mid, e_side, p_side, weights = refs
    place = Place(rows)
    for side in range(2):
        query_tables(qg_refs[side], weights.at[side], backward.at[side])
    for row in range(rows):
        keys = kv_refs[row][1:3].reshape(2 * CELLS, PAIR_WIDTH)
        bias = key_bias(keys) + place.bias(0, row, 4 * CELLS)
        at = slice(row * 2 * CELLS, (row + 1) * 2 * CELLS)
        for side in range(2):
            exps, probs = score(keys, bias, weights.at[side], ALL, scale_ref, None)
            for h in range(HALF):
                e_mid[side, h, at] = exps[h]
                p_mid[side, h, at] = probs[h]
    for row in range(0, rows, 2):
        at = slice(row * CELLS, (row + 2) * CELLS)
        for edge, lanes in ((0, FIRST), (1, LAST)):
            if edge == 0:
                pair = [kv_refs[row][0], kv_refs[row + 1][0]]
            else:
                pair = [sibling_ref[row], sibling_ref[row + 1]]
            bias = side_bias(place, [(0, row), (0, row + 1)], pair)
            keys = jnp.concatenate(pair, 0)
            for side in range(2):
                exps, probs = score(keys, bias, weights.at[side], lanes, scale_ref, None)
                for h in range(HALF):
                    e_side[side, edge, h, at] = exps[h]
                    p_side[side, edge, h, at] = probs[h]


def cross_stats(rows, stats_refs, lanes):
    place = Place(rows)
    both = []
    for side, ref in enumerate(stats_refs):
        there = jnp.where(place.there[1 + side], 1.0, 0.0)
        inverse = [ref[h : h + 1, lanes] * there for h in range(HALF)]
        both.append((inverse, [ref[HALF + h : HALF + h + 1, lanes] for h in range(HALF)]))
    return both


def cross_sibling_kernel(
    rows, scale_ref, near_stats, far_stats, backward, e_side, p_side, part_in, part_ref
):
    scales = head_scales(scale_ref, LAST)
    stats = cross_stats(rows, (near_stats, far_stats), LAST)
    for row in range(0, rows, 2):
        at = slice(row * CELLS, (row + 2) * CELLS)
        total = part_in[row : row + 2].reshape(2 * CELLS, PAIR_WIDTH)
        for side in range(2):
            pieces = grad_parts(
                [e_side[side, 1, h, at] for h in range(HALF)],
                [p_side[side, 1, h, at] for h in range(HALF)],
                *stats[side], scales,
            )
            total = total + key_grads(pieces, backward.at[side], LAST)
        part_ref[row : row + 2] = total.reshape(2, CELLS, PAIR_WIDTH).astype(BF16)


def cross_back_kernel(
    rows, scale_ref, near_stats, far_stats, backward, e_mid, p_mid, e_side, p_side,
    own_ref, total_ref,
):
    scales = head_scales(scale_ref, ALL)
    stats = cross_stats(rows, (near_stats, far_stats), ALL)
    for row in range(rows):
        at = slice(row * 2 * CELLS, (row + 1) * 2 * CELLS)
        total = own_ref[row, 1:3].reshape(2 * CELLS, PAIR_WIDTH)
        for side in range(2):
            pieces = grad_parts(
                [e_mid[side, h, at] for h in range(HALF)],
                [p_mid[side, h, at] for h in range(HALF)],
                *stats[side], scales,
            )
            total = total + key_grads(pieces, backward.at[side], ALL)
        total_ref[row, 1:3] = total.reshape(2, CELLS, PAIR_WIDTH)
    scales = head_scales(scale_ref, FIRST)
    stats = cross_stats(rows, (near_stats, far_stats), FIRST)
    for row in range(0, rows, 2):
        at = slice(row * CELLS, (row + 2) * CELLS)
        total = own_ref[row : row + 2, 0].reshape(2 * CELLS, PAIR_WIDTH)
        for side in range(2):
            pieces = grad_parts(
                [e_side[side, 0, h, at] for h in range(HALF)],
                [p_side[side, 0, h, at] for h in range(HALF)],
                *stats[side], scales,
            )
            total = total + key_grads(pieces, backward.at[side], FIRST)
        total_ref[row : row + 2, 0] = total.reshape(2, CELLS, PAIR_WIDTH)


def own_back_kernel(
    rows, scale_ref, stats_ref, backward, e_mid, p_mid, e_left, p_left,
    first_e_mid, first_p_mid, first_e_left, first_p_left,
    second_e_mid, second_p_mid, second_e_left, second_p_left, dq_sibling, *refs,
):
    kv_refs, refs = refs[: 3 * rows], refs[3 * rows :]
    own_ref, dq_own_ref, dq_other_ref, d_mid, d_left = refs
    scales = head_scales(scale_ref, ALL)
    inverse = [stats_ref[h : h + 1] for h in range(HALF)]
    delta = [stats_ref[HALF + h : HALF + h + 1] for h in range(HALF)]
    for index in range(3 * rows):
        at = slice(index * 2 * CELLS, (index + 1) * 2 * CELLS)
        if index < rows:
            exps, probs, start = e_mid, p_mid, index * 2 * CELLS
        elif index < rows + 2:
            exps, probs, start = first_e_mid, first_p_mid, (index - rows) * 2 * CELLS
        else:
            exps, probs, start = second_e_mid, second_p_mid, (index - rows - 2) * 2 * CELLS
        cut = slice(start, start + 2 * CELLS)
        pieces = grad_parts(
            [exps[h, cut] for h in range(HALF)], [probs[h, cut] for h in range(HALF)],
            inverse, delta, scales,
        )
        for h in range(HALF):
            d_mid[h, at] = pieces[h]
        if index < rows:
            part = key_grads(pieces, backward, ALL)
            own_ref[index, 1:3] = part.reshape(2, CELLS, PAIR_WIDTH)
    scales = head_scales(scale_ref, FIRST)
    inverse = [a[:, FIRST] for a in inverse]
    delta = [a[:, FIRST] for a in delta]
    for index in range(0, 3 * rows, 2):
        at = slice(index * CELLS, (index + 2) * CELLS)
        if index < rows:
            exps, probs, start = e_left, p_left, index * CELLS
        elif index < rows + 2:
            exps, probs, start = first_e_left, first_p_left, (index - rows) * CELLS
        else:
            exps, probs, start = second_e_left, second_p_left, (index - rows - 2) * CELLS
        cut = slice(start, start + 2 * CELLS)
        pieces = grad_parts(
            [exps[h, cut] for h in range(HALF)], [probs[h, cut] for h in range(HALF)],
            inverse, delta, scales,
        )
        for h in range(HALF):
            d_left[h, at] = pieces[h]
        if index < rows:
            part = key_grads(pieces, backward, FIRST)
            own_ref[index : index + 2, 0] = part.reshape(2, CELLS, PAIR_WIDTH)
    mid = jnp.concatenate([ref[1:3].reshape(2 * CELLS, PAIR_WIDTH) for ref in kv_refs], 0)
    left = jnp.concatenate([ref[0] for ref in kv_refs], 0)
    columns = []
    for h in range(HALF):
        made = query_grads(mid, d_mid[h], h)
        first = query_grads(left, d_left[h], h)
        last = dq_sibling[h * HEAD_DIM : (h + 1) * HEAD_DIM]
        columns.append(made + jnp.concatenate([first, last], 1))
    dq = jnp.concatenate(columns, 0).T
    dq_own_ref[...] = jnp.concatenate([dq[:CELLS], dq[2 * CELLS : 3 * CELLS]], 1)
    dq_other_ref[...] = jnp.concatenate([dq[CELLS : 2 * CELLS], dq[3 * CELLS :]], 1).astype(BF16)


def column_out_kernel(total_ref, sibling_ref, dq_other_ref, inner_ref, to_lat_ref, edge_ref, corner_ref):
    inner_ref[0] = total_ref[0, 1]
    inner_ref[1] = total_ref[0, 2] + sibling_ref[0].astype(F32)
    to_lat_ref[0] = total_ref[1, 1].astype(BF16)
    to_lat_ref[2] = dq_other_ref[...]
    to_lat_ref[1] = (total_ref[1, 2] + sibling_ref[1].astype(F32)).astype(BF16)
    edge_ref[...] = total_ref[0, 0].astype(BF16)
    corner_ref[...] = total_ref[1, 0].astype(BF16)


def heads_back(query, inner, edge, raws, inverses, weights):
    pair = jnp.concatenate([inner[0] + edge, inner[1]], 0)
    query = jnp.concatenate([query[:, :HALF_WIDTH], query[:, HALF_WIDTH:]], 0)
    grads = (query, pair[:, :HALF_WIDTH], pair[:, HALF_WIDTH:])
    total = dot(grads[2].astype(BF16), weights[2])
    for c in range(2):
        mean = head_means(raws[c] * grads[c])
        cubed = inverses[c] * inverses[c] * inverses[c]
        grad_raw = inverses[c] * grads[c] - cubed * raws[c] * mean
        total = total + dot(grad_raw.astype(BF16), weights[c])
    return total


def own_finish_kernel(
    inner_ref, dq_ref, edge_ref, query_raw, query_inverse, key_raw, key_inverse, turned_ref,
    total_ref, raws_ref, inverses_ref, weights_ref,
):
    upper = lax.rem(lax.axis_index("lat"), 2) == 1

    def split(array):
        low, high = array[:, :HALF_WIDTH], array[:, HALF_WIDTH:]
        return jnp.where(upper, high, low), jnp.where(upper, low, high)

    raws, other_raws = zip(split(query_raw[...]), split(key_raw[...]))
    inverses, other_inverses = zip(split(query_inverse[...]), split(key_inverse[...]))
    weights = []
    for c in range(3):
        low, high = turned_ref[c, :HALF_WIDTH], turned_ref[c, HALF_WIDTH:]
        weights.append(jnp.where(upper, high, low))
        weights_ref[c] = jnp.where(upper, low, high)
    for c in range(2):
        raws_ref[c] = other_raws[c]
        inverses_ref[c] = other_inverses[c]
    total_ref[...] = heads_back(
        dq_ref[...], inner_ref[...], edge_ref[...].astype(F32), raws, inverses, weights
    )


def finish_kernel(
    total_ref, other_ref, corner_ref, raws_ref, inverses_ref, weights_ref,
    x_ref, order_ref, gain_ref, out_ref,
):
    grad_normed = total_ref[...] + heads_back(
        other_ref[2].astype(F32), other_ref[:2].astype(F32), corner_ref[...].astype(F32),
        (raws_ref[0], raws_ref[1]), (inverses_ref[0], inverses_ref[1]), weights_ref,
    )
    order = order_ref[...]
    x = x_ref[...].astype(F32)
    inverse = lax.rsqrt(jnp.mean(x * x, -1, keepdims=True) + EPS)
    grad = gain_ref[...].reshape(1, x.shape[1]) * grad_normed
    mean = jnp.mean(x * grad, -1, keepdims=True)
    grad = (inverse * grad - inverse * inverse * inverse * x * mean).astype(BF16)
    out_ref[...] = dot_first(order, grad).reshape(out_ref.shape).astype(BF16)


VMEM = pl.BlockSpec(memory_space=pltpu.VMEM)


def kernel_call(
    body, name, outs, args, scratch=(), limit_mib=16, micros=1.0
):
    return pl.pallas_call(
        body,
        name=name,
        out_shape=[jax.ShapeDtypeStruct(shape, dtype) for shape, dtype in outs],
        in_specs=[VMEM] * len(args),
        out_specs=[VMEM] * len(outs),
        scratch_shapes=list(scratch),
        compiler_params=pltpu.CompilerParams(vmem_limit_bytes=limit_mib * 1024 * 1024),
        cost_estimate=pl.CostEstimate(
            flops=int(micros * FLOPS_PER_US), bytes_accessed=0, transcendentals=0
        ),
    )(*args)


def per_device(tokens, key_count, norm_gain, qkv_weight, out_weight, logit_scale, grad_out):
    frames, lat_rows, lon_cols, width = tokens.shape
    assert frames == BLOCK and lat_rows == BLOCK and lon_cols == 2 * BLOCK
    assert lax.axis_size("lat") % 2 == 0 and lax.axis_size("lon") % 2 == 0
    cells = frames * lat_rows * lon_cols
    blocks = lon_cols // BLOCK
    head_width = HEADS * HEAD_DIM
    qg_shape = ((blocks, CELLS, PAIR_WIDTH), BF16)
    edge_shape = ((CELLS, PAIR_WIDTH), BF16)

    order, x = kernel_call(
        order_kernel, "order", [((cells, cells), BF16), ((cells, width), BF16)], [tokens],
        micros=10.0,
    )
    projected = ((cells, head_width), F32)
    kv_own, kv_other, edge, normed, key_raw, key_inverse = kernel_call(
        key_value_kernel, "key_value",
        [qg_shape, qg_shape, edge_shape, ((cells, width), BF16), projected, projected],
        [key_count, x, norm_gain, qkv_weight], micros=2.0,
    )
    edge = pair_swap(edge, "lon", 1)
    kv_made, kv_other = kv_other, pair_swap(kv_other, "lat", 0)
    qg_own, qg_other, corner, query_raw, query_inverse, scales = kernel_call(
        query_grad_kernel, "query_grad",
        [qg_shape, qg_shape, edge_shape, projected, projected, ((HALF, 4 * CELLS), F32)],
        [logit_scale, order, normed, grad_out, qkv_weight, out_weight, kv_made], micros=5.0,
    )
    corner = corner_swap(corner)
    (kv_other,) = kernel_call(join_kernel, "join", [qg_shape], [kv_other], micros=3.0)
    qg_other, kv_other = lax.optimization_barrier((qg_other, kv_other))
    qg_other = pair_swap(qg_other, "lat", 0)
    kv_rows = [
        jnp.concatenate([edge[None], kv_own], 0),
        jnp.concatenate([corner[None], kv_other], 0),
    ]
    upper = lax.rem(lax.axis_index("lat"), 2) == 1
    wide = lax.axis_size("lat") > 2
    if wide:
        even = jnp.where(upper, kv_rows[1], kv_rows[0])
        odd = jnp.where(upper, kv_rows[0], kv_rows[1])
        kv_rows += [shift_by(odd, "lat", 2), shift_by(even, "lat", -2)]
    rows = len(kv_rows)
    kv_away = [frame_swap(kv, phase) for phase in range(2) for kv in kv_rows]
    qg_both = jnp.concatenate([qg_own, qg_other], 0)
    qg_away = [frame_swap(qg_both, phase) for phase in range(2)]

    queries = 4 * CELLS
    tables = [((2 * HALF, TILE, queries), BF16), ((2 * HALF, queries, TILE), BF16)]
    sums_shape = ((2 * HALF, 8, queries), F32)

    def kept(groups):
        mid = ((HALF, groups * 2 * CELLS, queries), F32)
        left = ((HALF, groups * CELLS, 2 * CELLS), F32)
        return [mid, mid, left, left]

    turned, weights, backward, sums, *own_kept = kernel_call(
        functools.partial(own_score_kernel, rows), "own_score",
        [((3, head_width, width), BF16)] + tables + [sums_shape] + kept(rows),
        [scales, qkv_weight, qg_both, *kv_rows], micros=1.5,
    )
    kv_parts = [[kv_away[(frame - 1) * rows + row] for frame, row in part]
                for part in away_groups(rows)]
    early = pair_swap(jnp.stack([kv[2] for kv in kv_rows + kv_parts[0]], 0), "lon", 0)
    late = pair_swap(jnp.stack([kv[2] for kv in kv_parts[1]], 0), "lon", 0)
    away_kept = []
    for which, kvs in enumerate(kv_parts):
        sums, *made = kernel_call(
            functools.partial(away_score_kernel, rows, which), "away_score",
            [sums_shape] + kept(len(kvs)), [scales, weights, sums, *kvs],
            micros=(1.5, 20.0)[which],
        )
        away_kept += made
    half_part = (rows, CELLS, PAIR_WIDTH)
    side_sums, *early_kept = kernel_call(
        functools.partial(sibling_score_kernel, rows), "sibling_score",
        [((2 * HALF, 8, 2 * CELLS), F32)] + [((HALF, (rows + 2) * CELLS, 2 * CELLS), F32)] * 2,
        [scales, weights, early], micros=0.5,
    )
    sibling_part, stats, dq_sibling = kernel_call(
        functools.partial(sibling_kernel, rows), "sibling",
        [(half_part, F32), ((2 * HALF, queries), F32), ((HALF_WIDTH, 2 * CELLS), F32)],
        [scales, weights, backward, sums, side_sums, *early_kept, early, late], micros=1.5,
    )
    near_stats, far_stats = frame_swap(stats, 0), frame_swap(stats, 1)
    cross_mid = ((2, HALF, rows * 2 * CELLS, queries), F32)
    cross_side = ((2, 2, HALF, rows * CELLS, 2 * CELLS), F32)
    cross_backward, e_mid, p_mid, e_side, p_side = kernel_call(
        functools.partial(cross_score_kernel, rows), "cross_score",
        [((2,) + tables[1][0], BF16), cross_mid, cross_mid, cross_side, cross_side],
        [scales, *qg_away, *kv_rows, early], micros=2.0,
        scratch=[pltpu.VMEM((2,) + tables[0][0], BF16)],
    )
    part = (rows, blocks + 1, CELLS, PAIR_WIDTH)
    packed = (CELLS, 2 * HALF_WIDTH)
    own_part, dq_own, dq_other = kernel_call(
        functools.partial(own_back_kernel, rows), "own_back",
        [(part, F32), (packed, F32), (packed, BF16)],
        [scales, stats, backward, *own_kept, *away_kept, dq_sibling, *kv_rows,
         *kv_parts[0], *kv_parts[1]],
        micros=2.0,
        scratch=[
            pltpu.VMEM((HALF, 3 * rows * 2 * CELLS, queries), BF16),
            pltpu.VMEM((HALF, 3 * rows * CELLS, 2 * CELLS), BF16),
        ],
    )
    (sibling_part,) = kernel_call(
        functools.partial(cross_sibling_kernel, rows), "cross_sibling", [(half_part, BF16)],
        [scales, near_stats, far_stats, cross_backward, e_side, p_side, sibling_part],
        micros=0.5,
    )
    sibling_part = pair_swap(sibling_part, "lon", 0)
    (total,) = kernel_call(
        functools.partial(cross_back_kernel, rows), "cross_back", [(part, F32)],
        [scales, near_stats, far_stats, cross_backward, e_mid, p_mid, e_side, p_side,
         own_part],
        micros=1.5,
    )
    if wide:
        total = total.at[:, blocks].add(sibling_part.astype(F32))
        sibling_part = jnp.zeros_like(sibling_part)
        to_odd = shift_by(total[2].astype(BF16), "lat", -2).astype(F32)
        to_even = shift_by(total[3].astype(BF16), "lat", 2).astype(F32)
        total = total[:2] + jnp.stack(
            [jnp.where(upper, to_odd, to_even), jnp.where(upper, to_even, to_odd)], 0
        )
    inner, to_lat, edge, corner = kernel_call(
        column_out_kernel, "column_out",
        [((blocks, CELLS, PAIR_WIDTH), F32), ((blocks + 1, CELLS, PAIR_WIDTH), BF16),
         edge_shape, edge_shape],
        [total, sibling_part, dq_other],
    )
    edge = pair_swap(edge, "lon", 1)
    corner = corner_swap(corner)
    other = pair_swap(to_lat, "lat", 0)
    halved = ((2, cells, HALF_WIDTH), F32)
    summed, raws, inverses, weights = kernel_call(
        own_finish_kernel, "own_finish",
        [((cells, width), F32), halved, halved, ((3, HALF_WIDTH, width), BF16)],
        [inner, dq_own, edge, query_raw, query_inverse, key_raw, key_inverse, turned],
        micros=1.0,
    )
    (grad_tokens,) = kernel_call(
        finish_kernel, "finish", [(tokens.shape, BF16)],
        [summed, other, corner, raws, inverses, weights, x, order, norm_gain], micros=2.0,
    )
    return grad_tokens


def solution(mesh):
    in_specs = (
        P("tm", "lat", "lon", None),
        P("tm", "lat", "lon"),
        P(),
        P(),
        P(),
        P(),
        P("tm", "lat", "lon", None),
    )
    out_specs = P("tm", "lat", "lon", None)
    return jax.shard_map(
        per_device, mesh=mesh, in_specs=in_specs, out_specs=out_specs, check_vma=False
    )
```

```python
import functools
import math

import jax
import jax.numpy as jnp
from jax import lax
from jax.experimental import pallas as pl
from jax.experimental.pallas import tpu as pltpu
from jax.sharding import PartitionSpec as P

HEADS = 6
HEAD_DIM = 64
BLOCK = 4
CELLS = BLOCK * BLOCK * BLOCK
HALF = HEADS // 2
HALF_WIDTH = HALF * HEAD_DIM
PAIR_WIDTH = 2 * HALF_WIDTH
TILE = 2 * HEAD_DIM
TILES = PAIR_WIDTH // TILE
DEAD_KEY = 64.0
DROPPED = -1e30
FLOPS_PER_US = 1e9

EPS = 1e-06
F32 = jnp.float32
BF16 = jnp.bfloat16


def partner_of(device, count, phase):
    return device + 1 if device % 2 == phase else device - 1


def pair_swap(array, axis, phase):
    count = lax.axis_size(axis)
    pairs = [(device, partner_of(device, count, phase) % count) for device in range(count)]
    return lax.ppermute(array, axis, pairs)


def frame_swap(array, phase):
    frames, lons = lax.axis_size("tm"), lax.axis_size("lon")
    pairs = []
    for frame in range(frames):
        for lon in range(lons):
            to = (partner_of(frame, frames, phase), lon)
            if not 0 <= to[0] < frames:
                to = (frame, partner_of(lon, lons, 0))
            pairs.append((frame * lons + lon, to[0] * lons + to[1]))
    return lax.ppermute(array, ("tm", "lon"), pairs)


def corner_swap(array):
    lats, lons = lax.axis_size("lat"), lax.axis_size("lon")
    pairs = []
    for lat in range(lats):
        for lon in range(lons):
            to = partner_of(lat, lats, 0) * lons + partner_of(lon, lons, 1) % lons
            pairs.append((lat * lons + lon, to))
    return lax.ppermute(array, ("lat", "lon"), pairs)


def shift_by(array, axis, step):
    count = lax.axis_size(axis)
    pairs = [(i, i + step) for i in range(count) if 0 <= i + step < count]
    return lax.ppermute(array, axis, pairs)


def dot(a, b):
    return lax.dot_general(a, b, (((1,), (0,)), ((), ())), preferred_element_type=F32)


def dot_last(a, b):
    return lax.dot_general(a, b, (((1,), (1,)), ((), ())), preferred_element_type=F32)


def dot_first(a, b):
    return lax.dot_general(a, b, (((0,), (0,)), ((), ())), preferred_element_type=F32)


def head_means(values):
    rows = lax.broadcasted_iota(jnp.int32, (TILE, TILE), 0) // HEAD_DIM
    cols = lax.broadcasted_iota(jnp.int32, (TILE, TILE), 1) // HEAD_DIM
    ones = (rows == cols).astype(F32).astype(BF16)
    high = values.astype(BF16)
    low = (values - high.astype(F32)).astype(BF16)
    pieces = []
    for start in range(0, values.shape[1], TILE):
        cut = slice(start, min(start + TILE, values.shape[1]))
        square = ones[: cut.stop - start, : cut.stop - start]
        pieces.append(dot(high[:, cut], square) + dot(low[:, cut], square))
    return jnp.concatenate(pieces, 1) * (1.0 / HEAD_DIM)


def block_order(lat_rows, lon_cols, count, parity):
    blocks = lon_cols // BLOCK
    row = lax.broadcasted_iota(jnp.int32, (count, count), 0)
    source = lax.broadcasted_iota(jnp.int32, (count, count), 1)
    slot = row // CELLS
    place = row % CELLS
    frame = place // (BLOCK * BLOCK)
    lat = (place // BLOCK) % BLOCK
    col = place % BLOCK
    block = jnp.where(parity == 1, blocks - 1 - slot, slot)
    wanted = (frame * lat_rows + lat) * lon_cols + block * BLOCK + col
    return (source == wanted).astype(F32).astype(BF16)


def halves(first, second):
    low = jnp.concatenate([first[:, :HALF_WIDTH], second[:, :HALF_WIDTH]], 1)
    high = jnp.concatenate([first[:, HALF_WIDTH:], second[:, HALF_WIDTH:]], 1)
    return low, high


def normalised(x, gain_ref):
    inverse = lax.rsqrt(jnp.mean(x * x, -1, keepdims=True) + EPS)
    return (x * inverse * gain_ref[...].reshape(1, x.shape[1])).astype(BF16)


def order_kernel(tokens_ref, order_ref, x_ref):
    frames, lat_rows, lon_cols, width = tokens_ref.shape
    cells = frames * lat_rows * lon_cols
    order = block_order(lat_rows, lon_cols, cells, lax.rem(lax.axis_index("lon"), 2))
    order_ref[...] = order
    x = dot(order, tokens_ref[...].astype(F32).reshape(cells, width).astype(BF16)).astype(BF16)
    x_ref[...] = x


def key_value_kernel(
    count_ref, x_ref, gain_ref, qkv_ref,
    kv_own_ref, kv_other_ref, edge_ref, normed_ref, raw_ref, inverse_ref,
):
    cells = x_ref.shape[0]
    blocks = cells // CELLS
    parity = lax.rem(lax.axis_index("lon"), 2)
    upper = lax.rem(lax.axis_index("lat"), 2) == 1
    normed = normalised(x_ref[...].astype(F32), gain_ref)
    normed_ref[...] = normed
    key, value = dot(normed, qkv_ref[1]), dot(normed, qkv_ref[2])
    raw_ref[...] = key
    inverse = lax.rsqrt(head_means(key * key) + EPS)
    inverse_ref[...] = inverse
    place = lax.broadcasted_iota(jnp.int32, (CELLS, 1), 0)
    counts = count_ref[0]
    live = []
    for slot in range(blocks):
        flip = blocks - 1 - slot
        live.append(
            place
            < jnp.where(parity == 1, counts[:, flip : flip + 1], counts[:, slot : slot + 1])
        )
    key = jnp.where(jnp.concatenate(live, 0), key * inverse, DEAD_KEY)
    shape = (blocks, CELLS, PAIR_WIDTH)
    low, high = halves(key, value)
    kv_own_ref[...] = jnp.where(upper, high, low).astype(BF16).reshape(shape)
    kv_other_ref[...] = jnp.where(upper, low, high).astype(BF16).reshape(shape)
    edge_ref[...] = kv_own_ref[0]


def query_grad_kernel(
    scale_in, order_ref, normed_ref, grad_ref, qkv_ref, out_weight_ref, kv_other_ref,
    qg_own_ref, qg_other_ref, corner_ref, raw_ref, inverse_ref, scale_ref,
):
    corner_ref[...] = kv_other_ref[0]
    cells, width = normed_ref.shape
    upper = lax.rem(lax.axis_index("lat"), 2) == 1
    all_scales = scale_in[...].reshape(1, HEADS) * (1.0 / math.sqrt(HEAD_DIM))
    for h in range(HALF):
        mine = jnp.where(
            upper, all_scales[:, HALF + h : HALF + h + 1], all_scales[:, h : h + 1]
        )
        scale_ref[h : h + 1] = jnp.broadcast_to(mine, (1, 4 * CELLS))
    query = dot(normed_ref[...], qkv_ref[0])
    raw_ref[...] = query
    inverse = lax.rsqrt(head_means(query * query) + EPS)
    inverse_ref[...] = inverse
    grad = dot_last(
        grad_ref[...].astype(F32).reshape(cells, width).astype(BF16), out_weight_ref[...]
    ).astype(BF16)
    low, high = halves(query * inverse, dot(order_ref[...], grad))
    shape = (cells // CELLS, CELLS, PAIR_WIDTH)
    qg_own_ref[...] = jnp.where(upper, high, low).astype(BF16).reshape(shape)
    qg_other_ref[...] = jnp.where(upper, low, high).astype(BF16).reshape(shape)


def lane_tile(j):
    return slice((j // 2) * TILE, (j // 2 + 1) * TILE)


class Place:
    def __init__(self, rows):
        self.rows = rows
        tm, frames = lax.axis_index("tm"), lax.axis_size("tm")
        odd = lax.rem(tm, 2) == 1
        near, far = jnp.where(odd, tm - 1, tm + 1), jnp.where(odd, tm + 1, tm - 1)
        self.there = [None] + [((at >= 0) & (at < frames)) for at in (near, far)]
        self.upper = lax.rem(lax.axis_index("lat"), 2)

    def bias(self, frame, row, lanes):
        there = self.there[frame]
        total = 0.0 if there is None else jnp.where(there, 0.0, DROPPED)
        if row < 2:
            return total
        pair, pairs = lax.axis_index("lat") // 2, lax.axis_size("lat") // 2
        if row == 2:
            inside, wanted = pair > 0, self.upper
        else:
            inside, wanted = pair < pairs - 1, 1 - self.upper
        lane_row = (lax.broadcasted_iota(jnp.int32, (1, lanes), 1) // CELLS) % 2
        seen = (lane_row == wanted) & inside
        return total + jnp.where(seen, 0.0, DROPPED)


def head_scales(scale_ref, lanes):
    return [scale_ref[h : h + 1, lanes] for h in range(HALF)]


def key_bias(keys):
    return jnp.where(keys[:, 0:1].astype(F32) < 0.5 * DEAD_KEY, 0.0, DROPPED)


def score(keys, bias, weights_ref, lanes, scale_ref, sums):
    to_exp2 = [s * math.log2(math.e) for s in head_scales(scale_ref, lanes)]
    count = keys.shape[0]
    exps, probs = [], []
    for h in range(HALF):
        scores = dot(keys[:, lane_tile(h)], weights_ref[h, :, lanes])
        grad_prob = dot(keys[:, lane_tile(HALF + h)], weights_ref[HALF + h, :, lanes])
        masked = jnp.exp2(scores * to_exp2[h] + bias)
        if sums is not None:
            shape = (count // 8, 8, masked.shape[1])
            sums[h] = sums[h] + jnp.sum(masked.reshape(shape), 0)
            inner = (masked * grad_prob).reshape(shape)
            sums[HALF + h] = sums[HALF + h] + jnp.sum(inner, 0)
        exps.append(masked)
        probs.append(grad_prob)
    return exps, probs


ALL = slice(0, 4 * CELLS)
FIRST = slice(0, 2 * CELLS)
LAST = slice(2 * CELLS, 4 * CELLS)


def score_groups(place, groups, kv_refs, weights_ref, scale_ref, sums, e_mid, p_mid, e_left, p_left):
    side = [jnp.zeros((8, 2 * CELLS), F32) for _ in range(2 * HALF)]
    for index, (group, ref) in enumerate(zip(groups, kv_refs)):
        keys = ref[1:3].reshape(2 * CELLS, PAIR_WIDTH)
        bias = key_bias(keys) + place.bias(*group, 4 * CELLS)
        exps, probs = score(keys, bias, weights_ref, ALL, scale_ref, sums)
        for h in range(HALF):
            e_mid[h, index * 2 * CELLS : (index + 1) * 2 * CELLS] = exps[h]
            p_mid[h, index * 2 * CELLS : (index + 1) * 2 * CELLS] = probs[h]
    for index in range(0, len(kv_refs), 2):
        pair = [kv_refs[index][0], kv_refs[index + 1][0]]
        bias = side_bias(place, groups[index : index + 2], pair)
        keys = jnp.concatenate(pair, 0)
        exps, probs = score(keys, bias, weights_ref, FIRST, scale_ref, side)
        for h in range(HALF):
            e_left[h, index * CELLS : (index + 2) * CELLS] = exps[h]
            p_left[h, index * CELLS : (index + 2) * CELLS] = probs[h]
    return [jnp.concatenate([a[:, FIRST] + b, a[:, LAST]], 1) for a, b in zip(sums, side)]


def side_bias(place, groups, keys):
    return jnp.concatenate(
        [
            jnp.broadcast_to(
                key_bias(keys[i]) + place.bias(*groups[i], 2 * CELLS), (CELLS, 2 * CELLS)
            )
            for i in range(2)
        ],
        0,
    )


def away_groups(rows):
    return [(1, 0), (2, 0)], [(frame, row) for frame in (1, 2) for row in range(1, rows)]


def query_tables(qg_ref, weights, backward):
    rows = jnp.concatenate([qg_ref[0], qg_ref[2], qg_ref[1], qg_ref[3]], 0).astype(F32)
    cols = rows.T
    count = rows.shape[0]
    lane_half = lax.broadcasted_iota(jnp.int32, (count, TILE), 1) // HEAD_DIM
    row_half = lax.broadcasted_iota(jnp.int32, (TILE, count), 0) // HEAD_DIM
    for j in range(2 * HALF):
        backward[j] = jnp.where(lane_half == j % 2, rows[:, lane_tile(j)], 0.0).astype(BF16)
        weights[j] = jnp.where(row_half == j % 2, cols[lane_tile(j)], 0.0).astype(BF16)


def own_score_kernel(rows, scale_ref, qkv_ref, qg_ref, *refs):
    kv_refs, refs = refs[:rows], refs[rows:]
    turned_ref, weights, backward, sums_ref, e_mid, p_mid, e_left, p_left = refs
    for c in range(3):
        turned_ref[c] = qkv_ref[c].T
    queries = 4 * CELLS
    query_tables(qg_ref, weights, backward)
    sums = [jnp.zeros((8, queries), F32) for _ in range(2 * HALF)]
    sums = score_groups(
        Place(rows), [(0, row) for row in range(rows)], kv_refs, weights, scale_ref, sums,
        e_mid, p_mid, e_left, p_left,
    )
    for j in range(2 * HALF):
        sums_ref[j] = sums[j]


def away_score_kernel(rows, part, scale_ref, weights, sums_in, *refs):
    groups = away_groups(rows)[part]
    kv_refs, refs = refs[: len(groups)], refs[len(groups) :]
    sums_ref, e_mid, p_mid, e_left, p_left = refs
    sums = [sums_in[j] for j in range(2 * HALF)]
    sums = score_groups(
        Place(rows), groups, kv_refs, weights, scale_ref, sums, e_mid, p_mid, e_left, p_left
    )
    for j in range(2 * HALF):
        sums_ref[j] = sums[j]


def grad_parts(exps, probs, inverse, delta, scales):
    grads, halves_of = [], []
    for h in range(HALF):
        prob = exps[h] * inverse[h]
        halves_of.append(prob.astype(BF16))
        grads.append((prob * (probs[h] - delta[h]) * scales[h]).astype(BF16))
    return grads + halves_of


def key_grads(pieces, backward, lanes):
    outs = []
    for tile in range(TILES):
        both = jnp.concatenate([pieces[2 * tile], pieces[2 * tile + 1]], 1)
        rows = jnp.concatenate(
            [backward[2 * tile, lanes], backward[2 * tile + 1, lanes]], 0
        )
        outs.append(dot(both, rows))
    return jnp.concatenate(outs, 1)


def query_grads(keys, grads, h):
    own = slice((h % 2) * HEAD_DIM, (h % 2 + 1) * HEAD_DIM)
    return dot_first(keys[:, lane_tile(h)], grads)[own]


def sibling_kernel(
    rows, scale_ref, weights, backward, sums_in, early_ref, late_ref, part_ref, stats_ref, dq_ref
):
    place = Place(rows)
    side = [jnp.zeros((8, 2 * CELLS), F32) for _ in range(2 * HALF)]
    first, second = away_groups(rows)
    groups = [(0, row) for row in range(rows)] + first + second
    pairs = [early_ref[i : i + 2] for i in range(0, rows + 2, 2)]
    pairs += [late_ref[i : i + 2] for i in range(0, len(second), 2)]
    made = []
    for index, pair in enumerate(pairs):
        bias = side_bias(place, groups[2 * index : 2 * index + 2], pair)
        keys = pair.reshape(2 * CELLS, PAIR_WIDTH)
        made.append(score(keys, bias, weights, LAST, scale_ref, side))
    inverse, delta = [], []
    for h in range(HALF):
        total, inner = (
            jnp.concatenate([sums_in[j, :, FIRST], sums_in[j, :, LAST] + side[j]], 1)
            for j in (h, HALF + h)
        )
        inverse.append(1.0 / jnp.sum(total, 0, keepdims=True))
        delta.append(jnp.sum(inner, 0, keepdims=True) * inverse[h])
        stats_ref[h : h + 1] = inverse[h]
        stats_ref[HALF + h : HALF + h + 1] = delta[h]
    inverse = [a[:, LAST] for a in inverse]
    delta = [a[:, LAST] for a in delta]
    scales = head_scales(scale_ref, LAST)
    grads = []
    for index in range(0, 3 * rows, 2):
        pieces = grad_parts(*made[index // 2], inverse, delta, scales)
        grads.append(pieces[:HALF])
        if index < rows:
            part = key_grads(pieces, backward, LAST)
            part_ref[index : index + 2] = part.reshape(2, CELLS, PAIR_WIDTH)
    keys = jnp.concatenate(pairs, 0).reshape(3 * rows * CELLS, PAIR_WIDTH)
    for h in range(HALF):
        dq_ref[h * HEAD_DIM : (h + 1) * HEAD_DIM] = query_grads(
            keys, jnp.concatenate([g[h] for g in grads], 0), h
        )


def cross_score_kernel(rows, scale_ref, *refs):
    qg_refs, refs = refs[:2], refs[2:]
    kv_refs, sibling_ref, refs = refs[:rows], refs[rows], refs[rows + 1 :]
    backward, e_mid, p_mid, e_side, p_side, weights = refs
    place = Place(rows)
    for side in range(2):
        query_tables(qg_refs[side], weights.at[side], backward.at[side])
    for row in range(rows):
        keys = kv_refs[row][1:3].reshape(2 * CELLS, PAIR_WIDTH)
        bias = key_bias(keys) + place.bias(0, row, 4 * CELLS)
        at = slice(row * 2 * CELLS, (row + 1) * 2 * CELLS)
        for side in range(2):
            exps, probs = score(keys, bias, weights.at[side], ALL, scale_ref, None)
            for h in range(HALF):
                e_mid[side, h, at] = exps[h]
                p_mid[side, h, at] = probs[h]
    for row in range(0, rows, 2):
        at = slice(row * CELLS, (row + 2) * CELLS)
        for edge, lanes in ((0, FIRST), (1, LAST)):
            if edge == 0:
                pair = [kv_refs[row][0], kv_refs[row + 1][0]]
            else:
                pair = [sibling_ref[row], sibling_ref[row + 1]]
            bias = side_bias(place, [(0, row), (0, row + 1)], pair)
            keys = jnp.concatenate(pair, 0)
            for side in range(2):
                exps, probs = score(keys, bias, weights.at[side], lanes, scale_ref, None)
                for h in range(HALF):
                    e_side[side, edge, h, at] = exps[h]
                    p_side[side, edge, h, at] = probs[h]


def cross_stats(rows, stats_refs, lanes):
    place = Place(rows)
    both = []
    for side, ref in enumerate(stats_refs):
        there = jnp.where(place.there[1 + side], 1.0, 0.0)
        inverse = [ref[h : h + 1, lanes] * there for h in range(HALF)]
        both.append((inverse, [ref[HALF + h : HALF + h + 1, lanes] for h in range(HALF)]))
    return both


def cross_sibling_kernel(
    rows, scale_ref, near_stats, far_stats, backward, e_side, p_side, part_in, part_ref
):
    scales = head_scales(scale_ref, LAST)
    stats = cross_stats(rows, (near_stats, far_stats), LAST)
    for row in range(0, rows, 2):
        at = slice(row * CELLS, (row + 2) * CELLS)
        total = part_in[row : row + 2].reshape(2 * CELLS, PAIR_WIDTH)
        for side in range(2):
            pieces = grad_parts(
                [e_side[side, 1, h, at] for h in range(HALF)],
                [p_side[side, 1, h, at] for h in range(HALF)],
                *stats[side], scales,
            )
            total = total + key_grads(pieces, backward.at[side], LAST)
        part_ref[row : row + 2] = total.reshape(2, CELLS, PAIR_WIDTH).astype(BF16)


def cross_back_kernel(
    rows, scale_ref, near_stats, far_stats, backward, e_mid, p_mid, e_side, p_side,
    own_ref, total_ref,
):
    scales = head_scales(scale_ref, ALL)
    stats = cross_stats(rows, (near_stats, far_stats), ALL)
    for row in range(rows):
        at = slice(row * 2 * CELLS, (row + 1) * 2 * CELLS)
        total = own_ref[row, 1:3].reshape(2 * CELLS, PAIR_WIDTH)
        for side in range(2):
            pieces = grad_parts(
                [e_mid[side, h, at] for h in range(HALF)],
                [p_mid[side, h, at] for h in range(HALF)],
                *stats[side], scales,
            )
            total = total + key_grads(pieces, backward.at[side], ALL)
        total_ref[row, 1:3] = total.reshape(2, CELLS, PAIR_WIDTH)
    scales = head_scales(scale_ref, FIRST)
    stats = cross_stats(rows, (near_stats, far_stats), FIRST)
    for row in range(0, rows, 2):
        at = slice(row * CELLS, (row + 2) * CELLS)
        total = own_ref[row : row + 2, 0].reshape(2 * CELLS, PAIR_WIDTH)
        for side in range(2):
            pieces = grad_parts(
                [e_side[side, 0, h, at] for h in range(HALF)],
                [p_side[side, 0, h, at] for h in range(HALF)],
                *stats[side], scales,
            )
            total = total + key_grads(pieces, backward.at[side], FIRST)
        total_ref[row : row + 2, 0] = total.reshape(2, CELLS, PAIR_WIDTH)


def own_back_kernel(
    rows, scale_ref, stats_ref, backward, e_mid, p_mid, e_left, p_left,
    first_e_mid, first_p_mid, first_e_left, first_p_left,
    second_e_mid, second_p_mid, second_e_left, second_p_left, dq_sibling, *refs,
):
    kv_refs, refs = refs[: 3 * rows], refs[3 * rows :]
    own_ref, dq_own_ref, dq_other_ref, d_mid, d_left = refs
    scales = head_scales(scale_ref, ALL)
    inverse = [stats_ref[h : h + 1] for h in range(HALF)]
    delta = [stats_ref[HALF + h : HALF + h + 1] for h in range(HALF)]
    for index in range(3 * rows):
        at = slice(index * 2 * CELLS, (index + 1) * 2 * CELLS)
        if index < rows:
            exps, probs, start = e_mid, p_mid, index * 2 * CELLS
        elif index < rows + 2:
            exps, probs, start = first_e_mid, first_p_mid, (index - rows) * 2 * CELLS
        else:
            exps, probs, start = second_e_mid, second_p_mid, (index - rows - 2) * 2 * CELLS
        cut = slice(start, start + 2 * CELLS)
        pieces = grad_parts(
            [exps[h, cut] for h in range(HALF)], [probs[h, cut] for h in range(HALF)],
            inverse, delta, scales,
        )
        for h in range(HALF):
            d_mid[h, at] = pieces[h]
        if index < rows:
            part = key_grads(pieces, backward, ALL)
            own_ref[index, 1:3] = part.reshape(2, CELLS, PAIR_WIDTH)
    scales = head_scales(scale_ref, FIRST)
    inverse = [a[:, FIRST] for a in inverse]
    delta = [a[:, FIRST] for a in delta]
    for index in range(0, 3 * rows, 2):
        at = slice(index * CELLS, (index + 2) * CELLS)
        if index < rows:
            exps, probs, start = e_left, p_left, index * CELLS
        elif index < rows + 2:
            exps, probs, start = first_e_left, first_p_left, (index - rows) * CELLS
        else:
            exps, probs, start = second_e_left, second_p_left, (index - rows - 2) * CELLS
        cut = slice(start, start + 2 * CELLS)
        pieces = grad_parts(
            [exps[h, cut] for h in range(HALF)], [probs[h, cut] for h in range(HALF)],
            inverse, delta, scales,
        )
        for h in range(HALF):
            d_left[h, at] = pieces[h]
        if index < rows:
            part = key_grads(pieces, backward, FIRST)
            own_ref[index : index + 2, 0] = part.reshape(2, CELLS, PAIR_WIDTH)
    mid = jnp.concatenate([ref[1:3].reshape(2 * CELLS, PAIR_WIDTH) for ref in kv_refs], 0)
    left = jnp.concatenate([ref[0] for ref in kv_refs], 0)
    columns = []
    for h in range(HALF):
        made = query_grads(mid, d_mid[h], h)
        first = query_grads(left, d_left[h], h)
        last = dq_sibling[h * HEAD_DIM : (h + 1) * HEAD_DIM]
        columns.append(made + jnp.concatenate([first, last], 1))
    dq = jnp.concatenate(columns, 0).T
    dq_own_ref[...] = jnp.concatenate([dq[:CELLS], dq[2 * CELLS : 3 * CELLS]], 1)
    dq_other_ref[...] = jnp.concatenate([dq[CELLS : 2 * CELLS], dq[3 * CELLS :]], 1).astype(BF16)


def column_out_kernel(total_ref, sibling_ref, dq_other_ref, inner_ref, to_lat_ref, edge_ref, corner_ref):
    inner_ref[0] = total_ref[0, 1]
    inner_ref[1] = total_ref[0, 2] + sibling_ref[0].astype(F32)
    to_lat_ref[0] = total_ref[1, 1].astype(BF16)
    to_lat_ref[2] = dq_other_ref[...]
    to_lat_ref[1] = (total_ref[1, 2] + sibling_ref[1].astype(F32)).astype(BF16)
    edge_ref[...] = total_ref[0, 0].astype(BF16)
    corner_ref[...] = total_ref[1, 0].astype(BF16)


def heads_back(query, inner, edge, raws, inverses, weights):
    pair = jnp.concatenate([inner[0] + edge, inner[1]], 0)
    query = jnp.concatenate([query[:, :HALF_WIDTH], query[:, HALF_WIDTH:]], 0)
    grads = (query, pair[:, :HALF_WIDTH], pair[:, HALF_WIDTH:])
    total = dot(grads[2].astype(BF16), weights[2])
    for c in range(2):
        mean = head_means(raws[c] * grads[c])
        cubed = inverses[c] * inverses[c] * inverses[c]
        grad_raw = inverses[c] * grads[c] - cubed * raws[c] * mean
        total = total + dot(grad_raw.astype(BF16), weights[c])
    return total


def own_finish_kernel(
    inner_ref, dq_ref, edge_ref, query_raw, query_inverse, key_raw, key_inverse, turned_ref,
    total_ref, raws_ref, inverses_ref, weights_ref,
):
    upper = lax.rem(lax.axis_index("lat"), 2) == 1

    def split(array):
        low, high = array[:, :HALF_WIDTH], array[:, HALF_WIDTH:]
        return jnp.where(upper, high, low), jnp.where(upper, low, high)

    raws, other_raws = zip(split(query_raw[...]), split(key_raw[...]))
    inverses, other_inverses = zip(split(query_inverse[...]), split(key_inverse[...]))
    weights = []
    for c in range(3):
        low, high = turned_ref[c, :HALF_WIDTH], turned_ref[c, HALF_WIDTH:]
        weights.append(jnp.where(upper, high, low))
        weights_ref[c] = jnp.where(upper, low, high)
    for c in range(2):
        raws_ref[c] = other_raws[c]
        inverses_ref[c] = other_inverses[c]
    total_ref[...] = heads_back(
        dq_ref[...], inner_ref[...], edge_ref[...].astype(F32), raws, inverses, weights
    )


def finish_kernel(
    total_ref, other_ref, corner_ref, raws_ref, inverses_ref, weights_ref,
    x_ref, order_ref, gain_ref, out_ref,
):
    grad_normed = total_ref[...] + heads_back(
        other_ref[2].astype(F32), other_ref[:2].astype(F32), corner_ref[...].astype(F32),
        (raws_ref[0], raws_ref[1]), (inverses_ref[0], inverses_ref[1]), weights_ref,
    )
    order = order_ref[...]
    x = x_ref[...].astype(F32)
    inverse = lax.rsqrt(jnp.mean(x * x, -1, keepdims=True) + EPS)
    grad = gain_ref[...].reshape(1, x.shape[1]) * grad_normed
    mean = jnp.mean(x * grad, -1, keepdims=True)
    grad = (inverse * grad - inverse * inverse * inverse * x * mean).astype(BF16)
    out_ref[...] = dot_first(order, grad).reshape(out_ref.shape).astype(BF16)


VMEM = pl.BlockSpec(memory_space=pltpu.VMEM)


def kernel_call(
    body, name, outs, args, scratch=(), limit_mib=16, micros=1.0
):
    return pl.pallas_call(
        body,
        name=name,
        out_shape=[jax.ShapeDtypeStruct(shape, dtype) for shape, dtype in outs],
        in_specs=[VMEM] * len(args),
        out_specs=[VMEM] * len(outs),
        scratch_shapes=list(scratch),
        compiler_params=pltpu.CompilerParams(vmem_limit_bytes=limit_mib * 1024 * 1024),
        cost_estimate=pl.CostEstimate(
            flops=int(micros * FLOPS_PER_US), bytes_accessed=0, transcendentals=0
        ),
    )(*args)


def per_device(tokens, key_count, norm_gain, qkv_weight, out_weight, logit_scale, grad_out):
    frames, lat_rows, lon_cols, width = tokens.shape
    assert frames == BLOCK and lat_rows == BLOCK and lon_cols == 2 * BLOCK
    assert lax.axis_size("lat") % 2 == 0 and lax.axis_size("lon") % 2 == 0
    cells = frames * lat_rows * lon_cols
    blocks = lon_cols // BLOCK
    head_width = HEADS * HEAD_DIM
    qg_shape = ((blocks, CELLS, PAIR_WIDTH), BF16)
    edge_shape = ((CELLS, PAIR_WIDTH), BF16)

    order, x = kernel_call(
        order_kernel, "order", [((cells, cells), BF16), ((cells, width), BF16)], [tokens],
        micros=10.0,
    )
    projected = ((cells, head_width), F32)
    kv_own, kv_other, edge, normed, key_raw, key_inverse = kernel_call(
        key_value_kernel, "key_value",
        [qg_shape, qg_shape, edge_shape, ((cells, width), BF16), projected, projected],
        [key_count, x, norm_gain, qkv_weight], micros=2.0,
    )
    edge = pair_swap(edge, "lon", 1)
    kv_made, kv_other = kv_other, pair_swap(kv_other, "lat", 0)
    qg_own, qg_other, corner, query_raw, query_inverse, scales = kernel_call(
        query_grad_kernel, "query_grad",
        [qg_shape, qg_shape, edge_shape, projected, projected, ((HALF, 4 * CELLS), F32)],
        [logit_scale, order, normed, grad_out, qkv_weight, out_weight, kv_made], micros=5.0,
    )
    corner = corner_swap(corner)
    qg_other, kv_other = lax.optimization_barrier((qg_other, kv_other))
    qg_other = pair_swap(qg_other, "lat", 0)
    kv_rows = [
        jnp.concatenate([edge[None], kv_own], 0),
        jnp.concatenate([corner[None], kv_other], 0),
    ]
    upper = lax.rem(lax.axis_index("lat"), 2) == 1
    wide = lax.axis_size("lat") > 2
    if wide:
        even = jnp.where(upper, kv_rows[1], kv_rows[0])
        odd = jnp.where(upper, kv_rows[0], kv_rows[1])
        kv_rows += [shift_by(odd, "lat", 2), shift_by(even, "lat", -2)]
    rows = len(kv_rows)
    kv_away = [frame_swap(kv, phase) for phase in range(2) for kv in kv_rows]
    qg_both = jnp.concatenate([qg_own, qg_other], 0)
    qg_away = [frame_swap(qg_both, phase) for phase in range(2)]

    queries = 4 * CELLS
    tables = [((2 * HALF, TILE, queries), BF16), ((2 * HALF, queries, TILE), BF16)]
    sums_shape = ((2 * HALF, 8, queries), F32)

    def kept(groups):
        mid = ((HALF, groups * 2 * CELLS, queries), F32)
        left = ((HALF, groups * CELLS, 2 * CELLS), F32)
        return [mid, mid, left, left]

    turned, weights, backward, sums, *own_kept = kernel_call(
        functools.partial(own_score_kernel, rows), "own_score",
        [((3, head_width, width), BF16)] + tables + [sums_shape] + kept(rows),
        [scales, qkv_weight, qg_both, *kv_rows], micros=1.5,
    )
    kv_parts = [[kv_away[(frame - 1) * rows + row] for frame, row in part]
                for part in away_groups(rows)]
    early = pair_swap(jnp.stack([kv[2] for kv in kv_rows + kv_parts[0]], 0), "lon", 0)
    late = pair_swap(jnp.stack([kv[2] for kv in kv_parts[1]], 0), "lon", 0)
    away_kept = []
    for which, kvs in enumerate(kv_parts):
        sums, *made = kernel_call(
            functools.partial(away_score_kernel, rows, which), "away_score",
            [sums_shape] + kept(len(kvs)), [scales, weights, sums, *kvs],
            micros=(1.5, 20.0)[which],
        )
        away_kept += made
    half_part = (rows, CELLS, PAIR_WIDTH)
    sibling_part, stats, dq_sibling = kernel_call(
        functools.partial(sibling_kernel, rows), "sibling",
        [(half_part, F32), ((2 * HALF, queries), F32), ((HALF_WIDTH, 2 * CELLS), F32)],
        [scales, weights, backward, sums, early, late], micros=1.5,
    )
    near_stats, far_stats = frame_swap(stats, 0), frame_swap(stats, 1)
    cross_mid = ((2, HALF, rows * 2 * CELLS, queries), F32)
    cross_side = ((2, 2, HALF, rows * CELLS, 2 * CELLS), F32)
    cross_backward, e_mid, p_mid, e_side, p_side = kernel_call(
        functools.partial(cross_score_kernel, rows), "cross_score",
        [((2,) + tables[1][0], BF16), cross_mid, cross_mid, cross_side, cross_side],
        [scales, *qg_away, *kv_rows, early], micros=2.0,
        scratch=[pltpu.VMEM((2,) + tables[0][0], BF16)],
    )
    part = (rows, blocks + 1, CELLS, PAIR_WIDTH)
    packed = (CELLS, 2 * HALF_WIDTH)
    own_part, dq_own, dq_other = kernel_call(
        functools.partial(own_back_kernel, rows), "own_back",
        [(part, F32), (packed, F32), (packed, BF16)],
        [scales, stats, backward, *own_kept, *away_kept, dq_sibling, *kv_rows,
         *kv_parts[0], *kv_parts[1]],
        micros=2.0,
        scratch=[
            pltpu.VMEM((HALF, 3 * rows * 2 * CELLS, queries), BF16),
            pltpu.VMEM((HALF, 3 * rows * CELLS, 2 * CELLS), BF16),
        ],
    )
    (sibling_part,) = kernel_call(
        functools.partial(cross_sibling_kernel, rows), "cross_sibling", [(half_part, BF16)],
        [scales, near_stats, far_stats, cross_backward, e_side, p_side, sibling_part],
        micros=0.5,
    )
    sibling_part = pair_swap(sibling_part, "lon", 0)
    (total,) = kernel_call(
        functools.partial(cross_back_kernel, rows), "cross_back", [(part, F32)],
        [scales, near_stats, far_stats, cross_backward, e_mid, p_mid, e_side, p_side,
         own_part],
        micros=1.5,
    )
    if wide:
        total = total.at[:, blocks].add(sibling_part.astype(F32))
        sibling_part = jnp.zeros_like(sibling_part)
        to_odd = shift_by(total[2].astype(BF16), "lat", -2).astype(F32)
        to_even = shift_by(total[3].astype(BF16), "lat", 2).astype(F32)
        total = total[:2] + jnp.stack(
            [jnp.where(upper, to_odd, to_even), jnp.where(upper, to_even, to_odd)], 0
        )
    inner, to_lat, edge, corner = kernel_call(
        column_out_kernel, "column_out",
        [((blocks, CELLS, PAIR_WIDTH), F32), ((blocks + 1, CELLS, PAIR_WIDTH), BF16),
         edge_shape, edge_shape],
        [total, sibling_part, dq_other],
    )
    edge = pair_swap(edge, "lon", 1)
    corner = corner_swap(corner)
    other = pair_swap(to_lat, "lat", 0)
    halved = ((2, cells, HALF_WIDTH), F32)
    summed, raws, inverses, weights = kernel_call(
        own_finish_kernel, "own_finish",
        [((cells, width), F32), halved, halved, ((3, HALF_WIDTH, width), BF16)],
        [inner, dq_own, edge, query_raw, query_inverse, key_raw, key_inverse, turned],
        micros=1.0,
    )
    (grad_tokens,) = kernel_call(
        finish_kernel, "finish", [(tokens.shape, BF16)],
        [summed, other, corner, raws, inverses, weights, x, order, norm_gain], micros=2.0,
    )
    return grad_tokens


def solution(mesh):
    in_specs = (
        P("tm", "lat", "lon", None),
        P("tm", "lat", "lon"),
        P(),
        P(),
        P(),
        P(),
        P("tm", "lat", "lon", None),
    )
    out_specs = P("tm", "lat", "lon", None)
    return jax.shard_map(
        per_device, mesh=mesh, in_specs=in_specs, out_specs=out_specs, check_vma=False
    )
```
